32 devices in a mesh: groups: 2 (over y), hosts: 4 (over z), mp: 4 (over x, core).
Axes of the slice: x: 2, y: 2, z: 4, core: 2. Of those that a mesh axis runs over, the one named last changes fastest.
Arguments:
- hidden: bfloat16 [256, 4096], P(('groups', 'hosts'), 'mp'), parts along dimension 0, may hold values from -6 to 6
- base_query_projection: bfloat16 [256, 4096], P(('groups', 'hosts'), 'mp'), parts along dimension 0, may hold values from -160 to 160
- base_key_projection: bfloat16 [256, 4096], P(('groups', 'hosts'), 'mp'), parts along dimension 0, may hold values from -6 to 6
- base_value_projection: bfloat16 [256, 4096], P(('groups', 'hosts'), 'mp'), parts along dimension 0, may hold values from -6 to 6
- adapter_input_factors: bfloat16 [8, 4096, 128], P(('groups', 'hosts'), 'mp'), parts along dimension 0, may hold values from -0.09375 to 0.09375
- adapter_output_factors: bfloat16 [8, 2, 64, 4096], P(('groups', 'hosts'), None, None, 'mp'), parts along dimension 0, may hold values from -0.75 to 0.75
- statement_prefix_cache: bfloat16 [32, 2, 128, 4096], P(('groups', 'hosts'), None, None, 'mp'), parts along dimension 0, may hold values from -6 to 6
- generated_token_cache: bfloat16 [256, 2, 8, 4096], P(('groups', 'hosts'), None, None, 'mp'), parts along dimension 0, may hold values from -6 to 6
- attempt_theorem_index: int32 [256], P(('groups', 'hosts')), parts along dimension 0, may hold values from 0 to 3, as said below
- host_live_count: int32 [8], P(('groups', 'hosts')), parts along dimension 0, may hold values from 8 to 32, as said below
- adapter_pool_row: int32 [8], P('groups'), parts along dimension 0, may hold values from 0 to 3, as said below
- prefix_pool_row: int32 [8, 4], P('groups'), parts along dimension 0, may hold values from 0 to 15, as said below
- prefix_block_count: int32 [8], P('groups'), parts along dimension 0, may hold values from 1 to 4
Outputs:
- attended: bfloat16 [256, 4096], P(('groups', 'hosts'), 'mp'), parts along dimension 0
- key_rows: bfloat16 [256, 4096], P(('groups', 'hosts'), 'mp'), parts along dimension 0
- value_rows: bfloat16 [256, 4096], P(('groups', 'hosts'), 'mp'), parts along dimension 0
The draws below stay inside these ranges and needn't reach their ends.
There are 2 independent parts, one for each index of `groups`. The reference program is written for one: setup_inputs(seed, part) draws one part's arguments, and reference() takes and returns one part's arrays. A program takes and returns all parts, laid end to end along the dimension named above; each array names one. Nothing has to cross between parts.
Inputs may be any that keep to these rules, and one draw needn't show every extreme that they name: `attempt_theorem_index`: among the live attempts of one host, at most 8 name theorems whose adapter lies on any one host, and for each block index at most 8 name theorems whose block of that index lies on any one host. One host holds the adapters named by 8 live attempts of every host, and one host holds the first blocks named by 8 live attempts of every host. `host_live_count`: rows at or above a host's count are empty; some host has all 32 rows live. `adapter_pool_row`: all entries differ; pool row p lies on host p. `prefix_pool_row`: all entries differ; pool row p lies on host p // 4.
All inputs are finite; a program needn't handle non-finite values.
Results may differ from the reference program's by a relative error of at most 0.011.
Values may be sent and summed in bfloat16 or wider, within the bound.
A program may use at most 64 MiB of HBM per device.

```python
import jax
import jax.numpy as jnp
from jax import lax

MODEL_WIDTH = 4096
ATTENTION_HEADS = 32
HEAD_SIZE = 128
ADAPTER_RANK = 64
BLK = 128
PBLK = 4
ATT_DEV = 32
SUFFIX = 8
THM_DEV = 1
HOSTS = 4
ATTEMPTS = 128
THEOREM_VARIANTS = 4
BLK_DEV = 4
BLOCKS = 16


def layout_plan(key):
    streams = jax.random.split(jax.random.fold_in(key, 17), 9)
    adapter_perm = jax.random.permutation(streams[0], THEOREM_VARIANTS).astype(jnp.int32)
    adapter_inverse = jnp.argsort(adapter_perm).astype(jnp.int32)
    owner_of = adapter_perm // THM_DEV
    slot_of = adapter_perm % THM_DEV
    host_perms = jax.vmap(lambda subkey: jax.random.permutation(subkey, HOSTS))(jax.random.split(streams[1], PBLK)).astype(jnp.int32)
    block_table = host_perms[:, owner_of].T * BLK_DEV + jnp.arange(PBLK, dtype=jnp.int32)[None, :] * THM_DEV + slot_of[:, None]
    hottest = jax.random.randint(streams[2], (), 0, HOSTS).astype(jnp.int32)
    orders = jax.vmap(lambda subkey: jax.random.permutation(subkey, HOSTS))(jax.random.split(streams[3], HOSTS)).astype(jnp.int32)
    columns = jnp.arange(HOSTS, dtype=jnp.int32)
    hot_where = jnp.sum(jnp.where(orders == hottest, columns[None, :], 0), axis=1)
    capacity = max(1, ATT_DEV // HOSTS)
    ordinal = jnp.arange(ATT_DEV, dtype=jnp.int32)
    owner_rows = jnp.take_along_axis(orders, ((ordinal // capacity)[None, :] + hot_where[:, None]) % HOSTS, axis=1)
    choose = jax.random.randint(streams[5], (HOSTS, ATT_DEV), 0, THM_DEV).astype(jnp.int32)
    theorems = adapter_inverse[owner_rows * THM_DEV + choose].reshape(ATTEMPTS)
    counts = jax.random.randint(streams[6], (HOSTS,), capacity, ATT_DEV + 1).astype(jnp.int32)
    filled = jax.random.randint(streams[7], (), 0, HOSTS)
    counts = jnp.where(columns == filled, ATT_DEV, counts).astype(jnp.int32)
    lengths = jax.random.randint(streams[8], (THEOREM_VARIANTS,), 1, PBLK + 1).astype(jnp.int32)
    lengths = lengths.at[adapter_inverse[hottest * THM_DEV]].set(PBLK)
    return (theorems, counts, adapter_perm, block_table.astype(jnp.int32), lengths)


def draw_attempt_theorem_index(key, part):
    return layout_plan(key)[0]


def draw_host_live_count(key, part):
    return layout_plan(key)[1]


def draw_adapter_pool_row(key, part):
    return layout_plan(key)[2]


def draw_prefix_pool_row(key, part):
    return layout_plan(key)[3]


def draw_prefix_block_count(key, part):
    return layout_plan(key)[4]


def draw_base_query_projection(key, part):
    shape_rows = (ATTEMPTS, ATTENTION_HEADS * HEAD_SIZE)
    values = jnp.clip(1.8 * jax.random.normal(jax.random.fold_in(key, 3), shape_rows, jnp.float32), -10.0, 10.0)
    return values.astype(jnp.bfloat16)


def shard_levels(stream_key, shape, cuts, smallest, high):
    loudness, own = 1.0, jax.random.fold_in(stream_key, 6)
    for dim, shards_of in cuts:
        heights = jnp.exp(jax.random.uniform(jax.random.fold_in(own, dim), (shards_of,), jnp.float32, smallest / len(cuts), high / len(cuts)))
        loudness = loudness * jnp.repeat(heights, shape[dim] // shards_of).reshape([-1 if axis == dim else 1 for axis in range(len(shape))])
    return loudness


def scatter_about(stream_key, extent, deviation, bound, cuts=(), kind=jnp.bfloat16):
    entries = jax.random.normal(stream_key, extent, jnp.float32) * deviation
    if len(cuts) > 0:
        entries = shard_levels(stream_key, extent, cuts, -0.22, 0.18) * entries
    return jnp.clip(entries, min=-bound, max=bound).astype(kind)


def setup_inputs(seed: int = 0, part: int = 0) -> dict:
    key_list = jax.random.split(jax.random.key(seed), 14)
    part_keys = jax.random.split(jax.random.fold_in(key_list[13], part), 14)
    return {
        "hidden": scatter_about(part_keys[0], (ATTEMPTS, MODEL_WIDTH), 1.0, 6.0, ((0, 4), (1, 4))),
        "base_query_projection": draw_base_query_projection(jax.random.fold_in(jax.random.fold_in(key_list[13], part), 71), part),
        "base_key_projection": scatter_about(part_keys[2], (ATTEMPTS, ATTENTION_HEADS * HEAD_SIZE), 1.0, 6.0, ((0, 4), (1, 4))),
        "base_value_projection": scatter_about(part_keys[3], (ATTEMPTS, ATTENTION_HEADS * HEAD_SIZE), 1.0, 6.0, ((0, 4), (1, 4))),
        "adapter_input_factors": scatter_about(part_keys[4], (THEOREM_VARIANTS, MODEL_WIDTH, 2 * ADAPTER_RANK), MODEL_WIDTH ** -0.5, 0.09375, ((0, 4), (1, 4))),
        "adapter_output_factors": scatter_about(part_keys[5], (THEOREM_VARIANTS, 2, ADAPTER_RANK, ATTENTION_HEADS * HEAD_SIZE), ADAPTER_RANK ** -0.5, 0.75, ((0, 4), (3, 4))),
        "statement_prefix_cache": scatter_about(part_keys[6], (BLOCKS, 2, BLK, ATTENTION_HEADS * HEAD_SIZE), 1.0, 6.0, ((0, 4), (3, 4))),
        "generated_token_cache": scatter_about(part_keys[7], (ATTEMPTS, 2, SUFFIX, ATTENTION_HEADS * HEAD_SIZE), 1.0, 6.0, ((0, 4), (3, 4))),
        "attempt_theorem_index": draw_attempt_theorem_index(jax.random.fold_in(jax.random.fold_in(key_list[13], part), 71), part),
        "host_live_count": draw_host_live_count(jax.random.fold_in(jax.random.fold_in(key_list[13], part), 71), part),
        "adapter_pool_row": draw_adapter_pool_row(jax.random.fold_in(jax.random.fold_in(key_list[13], part), 71), part),
        "prefix_pool_row": draw_prefix_pool_row(jax.random.fold_in(jax.random.fold_in(key_list[13], part), 71), part),
        "prefix_block_count": draw_prefix_block_count(jax.random.fold_in(jax.random.fold_in(key_list[13], part), 71), part),
    }


ADAPTER_SCALE = 0.5
ROPE_BASE = 10000.0
NEG_FILL = -1.0e30


def rotate(values, position):
    shaped = values.reshape(values.shape[:-1] + (-1, HEAD_SIZE))
    halfway = HEAD_SIZE // 2
    frequency = ROPE_BASE ** (-(jnp.arange(halfway, dtype=jnp.float32) * (2.0 / HEAD_SIZE)))
    angles = position.astype(jnp.float32)[..., None] * frequency
    cosine = jnp.cos(angles)[..., None, :]
    sine_part = jnp.sin(angles)[..., None, :]
    first_half = shaped[..., :halfway]
    second = shaped[..., halfway:]
    turned = jnp.concatenate([first_half * cosine - second * sine_part, second * cosine + first_half * sine_part], axis=-1)
    return turned.reshape(values.shape)


def reference(hidden, base_query_projection, base_key_projection, base_value_projection, adapter_input_factors, adapter_output_factors, statement_prefix_cache, generated_token_cache, attempt_theorem_index, host_live_count, adapter_pool_row, prefix_pool_row, prefix_block_count):
    adapter_rows = adapter_pool_row[attempt_theorem_index]
    block_rows = prefix_pool_row[attempt_theorem_index]
    block_counts = prefix_block_count[attempt_theorem_index]
    row_width = ATTENTION_HEADS * HEAD_SIZE

    def one_attempt(packet):
        hidden_state_row, query_row, key_row, value_row, suffix_rows, adapter_position, block_list, block_count = packet
        adapter_rank_row = jnp.dot(hidden_state_row, adapter_input_factors[adapter_position], preferred_element_type=jnp.float32).astype(jnp.bfloat16)
        output_factor = adapter_output_factors[adapter_position]
        query_correction = (jnp.dot(adapter_rank_row[:ADAPTER_RANK], output_factor[0], preferred_element_type=jnp.float32) * ADAPTER_SCALE).astype(jnp.bfloat16)
        value_correction = (jnp.dot(adapter_rank_row[ADAPTER_RANK:], output_factor[1], preferred_element_type=jnp.float32) * ADAPTER_SCALE).astype(jnp.bfloat16)
        position = BLK * block_count + SUFFIX
        query_vector = rotate(query_row.astype(jnp.float32) + query_correction.astype(jnp.float32), position).astype(jnp.bfloat16)
        new_key = rotate(key_row.astype(jnp.float32), position).astype(jnp.bfloat16)
        new_value = (value_row.astype(jnp.float32) + value_correction.astype(jnp.float32)).astype(jnp.bfloat16)
        heads_query = query_vector.reshape(ATTENTION_HEADS, HEAD_SIZE).astype(jnp.float32)
        chosen = statement_prefix_cache[block_list]
        block_keys = chosen[:, 0].reshape(PBLK, BLK, ATTENTION_HEADS, HEAD_SIZE).astype(jnp.float32)
        block_values = chosen[:, 1].reshape(PBLK, BLK, ATTENTION_HEADS, HEAD_SIZE).astype(jnp.float32)
        scores = jnp.einsum("hd,bthd->bht", heads_query, block_keys) * (HEAD_SIZE ** -0.5)
        usable = jnp.arange(PBLK, dtype=jnp.int32) < block_count
        peak_score = jnp.where(usable[:, None], jnp.max(scores, axis=2), NEG_FILL)
        weights = jnp.where(usable[:, None, None], jnp.exp(scores - peak_score[..., None]), 0.0)
        totals = jnp.sum(weights, axis=2)
        rounded = lax.optimization_barrier(weights.astype(jnp.bfloat16)).astype(jnp.float32)
        mixed_rows = jnp.einsum("bht,bthd->bhd", rounded, block_values)
        own_keys = jnp.concatenate([suffix_rows[0], new_key[None, :]], axis=0).reshape(SUFFIX + 1, ATTENTION_HEADS, HEAD_SIZE).astype(jnp.float32)
        own_values = jnp.concatenate([suffix_rows[1], new_value[None, :]], axis=0).reshape(SUFFIX + 1, ATTENTION_HEADS, HEAD_SIZE).astype(jnp.float32)
        own_scores = jnp.einsum("hd,thd->ht", heads_query, own_keys) * (HEAD_SIZE ** -0.5)
        own_peak = jnp.max(own_scores, axis=1)
        own_weights = jnp.exp(own_scores - own_peak[:, None])
        own_totals = jnp.sum(own_weights, axis=1)
        own_rounded = lax.optimization_barrier(own_weights.astype(jnp.bfloat16)).astype(jnp.float32)
        own_mixed = jnp.einsum("ht,thd->hd", own_rounded, own_values)
        overall = jnp.maximum(jnp.max(peak_score, axis=0), own_peak)
        prefix_factor = jnp.exp(peak_score - overall[None, :])
        own_factor = jnp.exp(own_peak - overall)
        numerator = jnp.sum(mixed_rows * prefix_factor[..., None], axis=0) + own_mixed * own_factor[:, None]
        denominator = jnp.sum(totals * prefix_factor, axis=0) + own_totals * own_factor
        result = (numerator / denominator[:, None]).reshape(row_width).astype(jnp.bfloat16)
        return result, new_key, new_value

    attended, key_rows, value_rows = lax.map(one_attempt, (hidden, base_query_projection, base_key_projection, base_value_projection, generated_token_cache, adapter_rows, block_rows, block_counts))
    ordinal = jnp.arange(ATTEMPTS, dtype=jnp.int32)
    living = (ordinal % ATT_DEV) < host_live_count[ordinal // ATT_DEV]
    live_rows = living[:, None]
    return (jnp.where(live_rows, attended, 0.0).astype(jnp.bfloat16), jnp.where(live_rows, key_rows, 0.0).astype(jnp.bfloat16), jnp.where(live_rows, value_rows, 0.0).astype(jnp.bfloat16))
```

```python
import functools
import math

import jax
import jax.numpy as jnp
from jax import lax
from jax.experimental import pallas as pl
from jax.experimental.pallas import tpu as pltpu
from jax.sharding import PartitionSpec as P

HEAD_SIZE = 128
ADAPTER_RANK = 64
BLK = 128
PBLK = 4


ADAPTER_SCALE = 0.5
ROPE_BASE = 10000.0
NEG_FILL = -1e30
MESH = pl.DeviceIdType.MESH


def rotate(values, position):
    shaped = values.reshape(values.shape[:-1] + (-1, HEAD_SIZE))
    halfway = HEAD_SIZE // 2
    frequency = ROPE_BASE ** (-(jnp.arange(halfway, dtype=jnp.float32) * (2.0 / HEAD_SIZE)))
    angles = position.astype(jnp.float32)[..., None] * frequency
    cosine = jnp.cos(angles)[..., None, :]
    sine_part = jnp.sin(angles)[..., None, :]
    first_half = shaped[..., :halfway]
    second = shaped[..., halfway:]
    turned = jnp.concatenate(
        [first_half * cosine - second * sine_part, second * cosine + first_half * sine_part],
        axis=-1,
    )
    return turned.reshape(values.shape)


def lookup_table(source_table, wanted):
    matches = wanted[:, None] == jnp.arange(source_table.shape[0], dtype=jnp.int32)[None, :]
    if source_table.ndim == 1:
        return jnp.sum(jnp.where(matches, source_table[None, :], 0), axis=1)
    return jnp.sum(jnp.where(matches[:, :, None], source_table[None, :, :], 0), axis=1)


def route_matrix(destination, validity, capacity, host_total):
    ordinal = jnp.arange(destination.shape[0], dtype=jnp.int32)
    earlier = (
        (destination[:, None] == destination[None, :])
        & validity[None, :]
        & (ordinal[None, :] < ordinal[:, None])
    )
    ranking = jnp.sum(earlier.astype(jnp.int32), axis=1)
    target = destination * capacity + ranking
    places = jnp.arange(host_total * capacity, dtype=jnp.int32)
    return ((places[:, None] == target[None, :]) & validity[None, :]).astype(jnp.bfloat16)


def pack_rows(router, payload):
    return jnp.dot(router, payload, preferred_element_type=jnp.float32).astype(jnp.bfloat16)


def attend_local(queries, chosen, statement_prefix_cache):
    head_count = queries.shape[-1] // HEAD_SIZE
    blocks = statement_prefix_cache.shape[0]
    block_keys = statement_prefix_cache[:, 0].reshape(
        blocks, statement_prefix_cache.shape[2], head_count, HEAD_SIZE
    )
    block_values = statement_prefix_cache[:, 1].reshape(
        blocks, statement_prefix_cache.shape[2], head_count, HEAD_SIZE
    )
    shaped = queries.reshape(queries.shape[:-1] + (head_count, HEAD_SIZE))
    scores = jnp.einsum(
        "nchd,bthd->ncbht", shaped, block_keys, preferred_element_type=jnp.float32
    ) * HEAD_SIZE ** (-0.5)
    chosen_mask = (chosen > 0)[:, :, :, None, None]
    masked = jnp.where(chosen_mask, scores, NEG_FILL)
    top_score = jnp.max(masked, axis=(2, 4))
    weights = jnp.where(chosen_mask, jnp.exp(masked - top_score[:, :, None, :, None]), 0.0)
    totals = jnp.sum(weights, axis=(2, 4))
    mixed_rows = jnp.einsum(
        "ncbht,bthd->nchd",
        weights.astype(jnp.bfloat16),
        block_values,
        preferred_element_type=jnp.float32,
    )
    return (mixed_rows.reshape(queries.shape), top_score, totals)


def body(
    hidden,
    base_query_projection,
    base_key_projection,
    base_value_projection,
    adapter_input_factors,
    adapter_output_factors,
    statement_prefix_cache,
    generated_token_cache,
    attempt_theorem_index,
    host_live_count,
    adapter_pool_row,
    prefix_pool_row,
    prefix_block_count,
):
    host_total = lax.axis_size("hosts")
    attempts = hidden.shape[0]
    capacity = max(1, attempts // host_total)
    owner_held_rows = adapter_input_factors.shape[0]
    local_blocks = statement_prefix_cache.shape[0]
    row_width = base_query_projection.shape[1]
    head_count = row_width // HEAD_SIZE
    ordinal = jnp.arange(attempts, dtype=jnp.int32)
    living = ordinal < host_live_count[0]
    adapter_rows = lookup_table(adapter_pool_row, attempt_theorem_index)
    block_rows = lookup_table(prefix_pool_row, attempt_theorem_index)
    block_counts = lookup_table(prefix_block_count, attempt_theorem_index)
    position = BLK * block_counts + generated_token_cache.shape[2]
    adapter_router = route_matrix(adapter_rows // owner_held_rows, living, capacity, host_total)
    adapter_pick = (
        adapter_rows[:, None] % owner_held_rows
        == jnp.arange(owner_held_rows, dtype=jnp.int32)[None, :]
    ).astype(jnp.bfloat16)
    sent_hidden = pack_rows(adapter_router, hidden).reshape(host_total, capacity, hidden.shape[1])
    sent_pick = pack_rows(adapter_router, adapter_pick).reshape(
        host_total, capacity, owner_held_rows
    )
    incoming_rows = lax.all_to_all(sent_hidden, "hosts", split_axis=0, concat_axis=0, tiled=True)
    pick_in = lax.all_to_all(sent_pick, "hosts", split_axis=0, concat_axis=0, tiled=True)
    projected_rows = jnp.einsum(
        "xjp,epk->xjek", incoming_rows, adapter_input_factors, preferred_element_type=jnp.float32
    )
    partial_rank = jnp.sum(projected_rows * pick_in.astype(jnp.float32)[..., None], axis=2)
    rank_rows = lax.psum(partial_rank, "mp").astype(jnp.bfloat16)
    spread_rows = rank_rows[:, :, None, :] * pick_in[..., None]
    query_correction = jnp.einsum(
        "exqw,qwf->exf",
        spread_rows[..., :ADAPTER_RANK],
        adapter_output_factors[:, 0],
        preferred_element_type=jnp.float32,
    )
    value_correction = jnp.einsum(
        "exqw,qwf->exf",
        spread_rows[..., ADAPTER_RANK:],
        adapter_output_factors[:, 1],
        preferred_element_type=jnp.float32,
    )
    adapter_corrections = (
        jnp.concatenate([query_correction, value_correction], axis=-1) * ADAPTER_SCALE
    ).astype(jnp.bfloat16)
    returned = lax.all_to_all(adapter_corrections, "hosts", split_axis=0, concat_axis=0, tiled=True)
    adapter_corrections = jnp.dot(
        adapter_router.T,
        returned.reshape(host_total * capacity, 2 * row_width),
        preferred_element_type=jnp.float32,
    )
    query_rows = rotate(
        base_query_projection.astype(jnp.float32) + adapter_corrections[:, :row_width], position
    ).astype(jnp.bfloat16)
    value_rows = (
        base_value_projection.astype(jnp.float32) + adapter_corrections[:, row_width:]
    ).astype(jnp.bfloat16)
    key_rows = rotate(base_key_projection.astype(jnp.float32), position).astype(jnp.bfloat16)
    requests = []
    for block_index in range(PBLK):
        wanted = living & (block_index < block_counts)
        holder = block_rows[:, block_index]
        router = route_matrix(holder // local_blocks, wanted, capacity, host_total)
        block_pick = (
            holder[:, None] % local_blocks == jnp.arange(local_blocks, dtype=jnp.int32)[None, :]
        ).astype(jnp.bfloat16)
        sent_queries = pack_rows(router, query_rows).reshape(host_total, capacity, row_width)
        sent_blocks = pack_rows(router, block_pick).reshape(host_total, capacity, local_blocks)
        requests.append((router, wanted, sent_queries, sent_blocks))
    partials = []
    for request in requests:
        answer_mixed_rows, answer_top_score, answer_totals = attend_local(
            lax.all_to_all(request[2], "hosts", split_axis=0, concat_axis=0, tiled=True),
            lax.all_to_all(request[3], "hosts", split_axis=0, concat_axis=0, tiled=True),
            statement_prefix_cache,
        )
        partials.append(
            (
                lax.all_to_all(answer_mixed_rows, "hosts", split_axis=0, concat_axis=0, tiled=True),
                lax.all_to_all(answer_top_score, "hosts", split_axis=0, concat_axis=0, tiled=True),
                lax.all_to_all(answer_totals, "hosts", split_axis=0, concat_axis=0, tiled=True),
            )
        )
    entries = []
    for block_index in range(PBLK):
        router, wanted = (requests[block_index][0], requests[block_index][1])
        mixed_rows, top_score, totals = partials[block_index]
        back_router = router.T.astype(jnp.float32)
        flat_mixed = jnp.dot(
            back_router,
            mixed_rows.reshape(host_total * capacity, row_width),
            precision=lax.Precision.HIGHEST,
        )
        flat_top = jnp.dot(
            back_router,
            top_score.reshape(host_total * capacity, head_count),
            precision=lax.Precision.HIGHEST,
        )
        flat_totals = jnp.dot(
            back_router,
            totals.reshape(host_total * capacity, head_count),
            precision=lax.Precision.HIGHEST,
        )
        flat_top = jnp.where(wanted[:, None], flat_top, NEG_FILL)
        entries.append((flat_mixed, flat_top, flat_totals))
    shaped_query = query_rows.reshape(attempts, head_count, HEAD_SIZE)
    own_keys = jnp.concatenate([generated_token_cache[:, 0], key_rows[:, None, :]], axis=1).reshape(
        attempts, -1, head_count, HEAD_SIZE
    )
    own_values = jnp.concatenate(
        [generated_token_cache[:, 1], value_rows[:, None, :]], axis=1
    ).reshape(attempts, -1, head_count, HEAD_SIZE)
    own_scores = jnp.einsum(
        "ahd,athd->aht", shaped_query, own_keys, preferred_element_type=jnp.float32
    ) * HEAD_SIZE ** (-0.5)
    own_top = jnp.max(own_scores, axis=2)
    own_weights = jnp.exp(own_scores - own_top[..., None])
    own_totals = jnp.sum(own_weights, axis=2)
    own_mixed = jnp.einsum(
        "aht,athd->ahd",
        own_weights.astype(jnp.bfloat16),
        own_values,
        preferred_element_type=jnp.float32,
    )
    overall = own_top
    for flat_mixed, flat_top, flat_totals in entries:
        overall = jnp.maximum(overall, flat_top)
    own_factor = jnp.exp(own_top - overall)
    numerator = own_mixed * own_factor[..., None]
    denominator = own_totals * own_factor
    for flat_mixed, flat_top, flat_totals in entries:
        factor = jnp.exp(flat_top - overall)
        numerator = (
            numerator + flat_mixed.reshape(attempts, head_count, HEAD_SIZE) * factor[..., None]
        )
        denominator = denominator + flat_totals * factor
    attended = (numerator / denominator[..., None]).reshape(attempts, row_width)
    live_rows = living[:, None]
    return (
        jnp.where(live_rows, attended, 0.0).astype(jnp.bfloat16),
        jnp.where(live_rows, key_rows, 0.0),
        jnp.where(live_rows, value_rows, 0.0),
    )


def _iota(shape, dim):
    return lax.broadcasted_iota(jnp.int32, shape, dim)


def _dot(a, b):
    return jnp.dot(a, b, preferred_element_type=jnp.float32)


def _dot_t(a, b):
    return lax.dot_general(a, b, (((1,), (1,)), ((), ())), preferred_element_type=jnp.float32)


def fused_kernel(
    sizes,
    thm, live, apr, ppr, cnt,
    hidden, base_q, base_k, base_v, a_hbm, b_hbm, kv_hbm, gen_hbm,
    out, key_out, val_out,
    a_v, b_v, kv_v, gen_v,
    snd_h, rcv_h, snd_q, rcv_q, part, snd_v, rcv_v, snd_m, rcv_m, snd_l, rcv_l, own_mix,
    local_sem, h_s, h_r, bq_s, bq_r, p_s, p_r, q_s, q_r, v_s, v_r, m_s, m_r, l_s, l_r,
    *queries,
):
    H, MP, A, CAP, L, T, PB, HEADS, SUF, NCH = sizes
    f32, bf = jnp.float32, jnp.bfloat16
    D = HEAD_SIZE
    W = HEADS * D
    W2 = W // 2
    S = H * CAP
    CW = W // NCH
    shift = CAP.bit_length() - 1
    me = lax.axis_index("hosts")
    mme = lax.axis_index("mp")

    def other(axis, d):
        return lax.rem((me if axis == "hosts" else mme) + d, H if axis == "hosts" else MP)

    locals_ = [
        pltpu.make_async_copy(src, dst, local_sem.at[i])
        for i, (src, dst) in enumerate(
            [(a_hbm, a_v), (b_hbm, b_v), (kv_hbm, kv_v), (gen_hbm, gen_v)]
        )
    ]
    for copy in locals_:
        copy.start()

    barrier = pltpu.get_barrier_semaphore()
    for d in range(1, H):
        pl.semaphore_signal(barrier, inc=1, device_id={"hosts": other("hosts", d)}, device_id_type=MESH)
    for d in range(1, MP):
        pl.semaphore_signal(barrier, inc=1, device_id={"mp": other("mp", d)}, device_id_type=MESH)

    def send(src, dst, s, r, axis, d):
        copy = pltpu.make_async_remote_copy(
            src_ref=src, dst_ref=dst, send_sem=s, recv_sem=r,
            device_id={axis: other(axis, d)}, device_id_type=MESH,
        )
        copy.start()
        return copy

    lane8, sub8 = _iota((8, 128), 1), _iota((8, 128), 0)
    th = jnp.full((8, 128), -1, jnp.int32)
    for a in range(A):
        th = jnp.where(lane8 == a, thm[a], th)
    owner = jnp.full((8, 128), -1, jnp.int32)
    for t in range(T):
        owner = jnp.where(th == t, apr[t], owner)
    n_live = live[0]
    owner = jnp.where(lane8 < n_live, owner, -1)
    member = jnp.where(owner == sub8, 1.0, 0.0).astype(f32)
    before = jnp.where(_iota((128, 128), 0) < _iota((128, 128), 1), 1.0, 0.0).astype(bf)
    rank_f = jnp.sum(member * _dot(member.astype(bf), before), axis=0, keepdims=True)
    rank_row = rank_f.astype(jnp.int32)
    target = jnp.where(owner[0:1] >= 0, owner[0:1] * CAP + rank_row, -1)
    router = jnp.where(_iota((S, A), 0) == target[:, :A], 1.0, 0.0).astype(bf)

    def folded(rows, e):
        piece = rows[e * CAP : (e + 1) * CAP]
        return jnp.concatenate([piece[:, :W2], piece[:, W2:]], axis=0)

    packed = _dot(router, hidden[...])
    for e in range(H):
        snd_h[e] = folded(packed, e).astype(bf)
    pl.semaphore_wait(barrier, H - 1 + MP - 1)
    hs = [
        send(snd_h.at[other("hosts", d)], rcv_h.at[me], h_s.at[d], h_r.at[d], "hosts", d)
        for d in range(1, H)
    ]
    packed = _dot(router, base_q[...])
    for e in range(H):
        snd_q[e] = folded(packed, e).astype(bf)
    bqs = [
        send(snd_q.at[other("hosts", d)], rcv_q.at[me], bq_s.at[d], bq_r.at[d], "hosts", d)
        for d in range(1, H)
    ]
    rcv_h[me] = snd_h[me]
    rcv_q[me] = snd_q[me]

    lane = _iota((8, 128), 1)
    half = jnp.where(lane < D // 2, lane, lane - D // 2).astype(f32)
    freq = jnp.exp(half * (-2.0 / D * math.log(ROPE_BASE)))
    counts = jnp.zeros((8, 128), jnp.int32)
    my_count = jnp.int32(0)
    for t in range(T):
        counts = jnp.where(sub8 == t, cnt[t], counts)
        my_count = jnp.where(apr[t] == me, cnt[t], my_count)
    counts = jnp.where(sub8 == T, my_count, counts)
    angle = (BLK * counts + SUF).astype(f32) * freq
    cos_t = jnp.cos(angle)
    sin_t = jnp.sin(angle)
    sin_t = jnp.where(lane < D // 2, -sin_t, sin_t)

    def turn(x, c, s):
        return x * c + pltpu.roll(x, D // 2, 1) * s

    locals_[0].wait()
    for copy in hs:
        copy.wait_recv()
    rows = rcv_h[...].reshape(H * 2 * CAP, W2)
    left = _dot(rows, a_v[0, :W2, :])
    right = _dot(rows, a_v[0, W2:, :])
    part[mme] = jnp.concatenate(
        [
            left[2 * CAP * e : 2 * CAP * e + CAP] + right[2 * CAP * e + CAP : 2 * CAP * (e + 1)]
            for e in range(H)
        ],
        axis=0,
    )
    ps = [
        send(part.at[mme], part.at[mme], p_s.at[d], p_r.at[d], "mp", d) for d in range(1, MP)
    ]
    for copy in bqs:
        copy.wait_recv()
    bq = rcv_q[...].astype(f32)
    bq_half = [
        jnp.concatenate([bq[e, k * CAP : (k + 1) * CAP] for e in range(H)], axis=0)
        for k in range(2)
    ]
    locals_[1].wait()
    for copy in ps:
        copy.wait_recv()
    ranks = part[0]
    for m in range(1, MP):
        ranks = ranks + part[m]
    ranks = ranks.astype(bf).astype(f32)
    rank_q = ranks[:, :ADAPTER_RANK].astype(bf)
    rank_v = pltpu.roll(ranks, ADAPTER_RANK, 1)[:, :ADAPTER_RANK].astype(bf)
    qs = []
    for c in range(NCH):
        cols = slice(c * CW, (c + 1) * CW)
        delta = (_dot(rank_q, b_v[0, 0, :, cols]) * ADAPTER_SCALE).astype(bf).astype(f32)
        k, off = (c * CW) // W2, (c * CW) % W2
        raw = bq_half[k][:, off : off + CW] + delta
        for h in range(CW // D):
            queries[c][me, :, h * D : (h + 1) * D] = turn(
                raw[:, h * D : (h + 1) * D], cos_t[T : T + 1], sin_t[T : T + 1]
            ).astype(bf)
        view = queries[c].at[me]
        qs.append(
            [send(view, view, q_s.at[c, d], q_r.at[c, d], "hosts", d) for d in range(1, H)]
        )
    delta = _dot(rank_v, b_v[0, 1]) * ADAPTER_SCALE
    for e in range(H):
        snd_v[e] = folded(delta, e).astype(bf)
    vs = [
        send(snd_v.at[other("hosts", d)], rcv_v.at[me], v_s.at[d], v_r.at[d], "hosts", d)
        for d in range(1, H)
    ]
    rcv_v[me] = snd_v[me]

    sub128 = _iota((128, 128), 0)
    both = jnp.where(sub128 == 0, th[0:1].astype(f32), jnp.where(sub128 == 1, rank_f, 0.0))
    turned = both.T[:A].astype(jnp.int32)
    th_c, rank_c = turned[:, 0:1], turned[:, 1:2]
    lane_a = _iota((A, 128), 1)
    live_c = _iota((A, 1), 0) < n_live
    owner_c = jnp.full((A, 1), -1, jnp.int32)
    cos_a = jnp.zeros((A, 128), f32)
    sin_a = jnp.zeros((A, 128), f32)
    blocks_c = [jnp.full((A, 1), -1, jnp.int32) for _ in range(PB)]
    for t in range(T):
        here = th_c == t
        owner_c = jnp.where(here, apr[t], owner_c)
        cos_a = jnp.where(here, cos_t[t : t + 1], cos_a)
        sin_a = jnp.where(here, sin_t[t : t + 1], sin_a)
        for j in range(PB):
            blocks_c[j] = jnp.where(here, jnp.where(j < cnt[t], ppr[t, j], -1), blocks_c[j])
    owner_c = jnp.where(live_c, owner_c, -1)
    slot_ok = jnp.where(rank_c == (lane_a & (CAP - 1)), 1, 0)
    group = lane_a >> shift
    used = jnp.zeros((A, 128), jnp.int32)
    for j in range(PB):
        used = used + jnp.where(blocks_c[j] == group, 1, 0)
    used = jnp.where(live_c, used * slot_ok, 0) > 0
    fetch = jnp.where(owner_c * H + me == group, slot_ok, 0).astype(f32).astype(bf)
    unpack = jnp.where(
        owner_c * CAP + rank_c == _iota((A, S), 1), jnp.where(owner_c >= 0, 1.0, 0.0), 0.0
    ).astype(bf)
    keys = []
    for h in range(HEADS):
        cols = slice(h * D, (h + 1) * D)
        key = turn(base_k[:, cols].astype(f32), cos_a, sin_a).astype(bf).astype(f32)
        keys.append(key)
        key_out[:, cols] = jnp.where(live_c, key, 0.0).astype(bf)

    whose = []
    for b in range(L):
        index = jnp.int32(0)
        for t in range(T):
            for j in range(PB):
                index = jnp.where(ppr[t, j] == me * L + b, apr[t], index)
        whose.append(index)
    scale = D ** (-0.5)
    locals_[2].wait()
    lane128 = _iota((128, 128), 1)
    lse_all = jnp.zeros((128, 128), f32)
    ms = []
    for c in range(NCH):
        for copy in qs[c]:
            copy.wait_recv()
        for h in range(c * CW // D, (c + 1) * CW // D):
            cols = slice(h * D, (h + 1) * D)
            within = slice(h * D - c * CW, (h + 1) * D - c * CW)
            scores = jnp.concatenate(
                [_dot_t(queries[c][whose[b], :, within], kv_v[b, 0, :, cols]) for b in range(L)], axis=0
            ) * scale
            top = jnp.max(scores, axis=1, keepdims=True)
            weights = jnp.exp(scores - top)
            total = jnp.sum(weights, axis=1, keepdims=True)
            weights = weights.astype(bf)
            mixed = jnp.concatenate(
                [_dot(weights[b * S : (b + 1) * S], kv_v[b, 1, :, cols]) for b in range(L)], axis=0
            ) * (1.0 / total)
            lse_all = jnp.where(lane128 == h, top + jnp.log(total), lse_all)
            for e in range(H):
                snd_m[e, :, cols] = jnp.concatenate(
                    [mixed[b * S + e * CAP : b * S + (e + 1) * CAP] for b in range(L)], axis=0
                ).astype(bf)
        if c == NCH - 1:
            ordered = jnp.concatenate(
                [
                    lse_all[b * S + e * CAP : b * S + (e + 1) * CAP]
                    for e in range(H)
                    for b in range(L)
                ],
                axis=0,
            )
            lse_t = ordered.T[:HEADS]
            rcv_l[me] = lse_t
            for d in range(1, H):
                snd_l[d] = pltpu.roll(lse_t, (128 - L * CAP * d) % 128, 1)
            ls = [
                send(snd_l.at[d], rcv_l.at[me], l_s.at[d], l_r.at[d], "hosts", d)
                for d in range(1, H)
            ]
        span = pl.ds(c * CW, CW)
        ms.append(
            [
                send(
                    snd_m.at[other("hosts", d), :, span], rcv_m.at[me, :, span],
                    m_s.at[c, d], m_r.at[c, d], "hosts", d,
                )
                for d in range(1, H)
            ]
        )
    rcv_m[me] = snd_m[me]

    locals_[3].wait()
    for copy in vs:
        copy.wait_recv()
    dv = rcv_v[...].astype(f32)
    dv_att = [
        _dot(
            unpack,
            jnp.concatenate([dv[p, k * CAP : (k + 1) * CAP] for p in range(H)], axis=0).astype(bf),
        )
        for k in range(2)
    ]
    N = gen_v.shape[0]
    lane_n, sub_n = _iota((A, N), 1), _iota((A, N), 0)
    mine = ((lane_n >> (SUF.bit_length())) == sub_n) & ((lane_n & (2 * SUF - 1)) < SUF)
    own_top, own_total = [], []
    for h in range(HEADS):
        cols = slice(h * D, (h + 1) * D)
        k, off = (h * D) // W2, (h * D) % W2
        value = (base_v[:, cols].astype(f32) + dv_att[k][:, off : off + D]).astype(bf).astype(f32)
        val_out[:, cols] = jnp.where(live_c, value, 0.0).astype(bf)
        c, start = (h * D) // CW, (h * D) % CW
        query = _dot(fetch, queries[c][:, :, start : start + D].reshape(H * S, D))
        scores = _dot_t(query.astype(bf), gen_v[:, cols]) * scale
        scores = jnp.where(mine, scores, NEG_FILL)
        self_score = jnp.sum(query * keys[h], axis=1, keepdims=True) * scale
        top = jnp.maximum(jnp.max(scores, axis=1, keepdims=True), self_score)
        weights = jnp.where(mine, jnp.exp(scores - top), 0.0)
        self_weight = jnp.exp(self_score - top)
        own_top.append(top)
        own_total.append(jnp.sum(weights, axis=1, keepdims=True) + self_weight)
        own_mix[:, cols] = (
            _dot(pltpu.roll(weights, SUF, 1).astype(bf), gen_v[:, cols])
            + self_weight.astype(bf).astype(f32) * value
        )

    for copy in ls:
        copy.wait_recv()
    lse = jnp.zeros((HEADS, 128), f32)
    lane_h = _iota((HEADS, 128), 1)
    for g in range(H):
        lse = jnp.where((lane_h >= g * L * CAP) & (lane_h < (g + 1) * L * CAP), rcv_l[g], lse)
    for c in range(NCH):
        for copy in ms[c]:
            copy.wait_recv()
        for h in range(c * CW // D, (c + 1) * CW // D):
            cols = slice(h * D, (h + 1) * D)
            logs = jnp.where(used, lse[h : h + 1], NEG_FILL)
            top = jnp.maximum(jnp.max(logs, axis=1, keepdims=True), own_top[h])
            factor = jnp.where(used, jnp.exp(logs - top), 0.0)
            own_factor = jnp.exp(own_top[h] - top)
            inverse = 1.0 / (jnp.sum(factor, axis=1, keepdims=True) + own_total[h] * own_factor)
            result = _dot(
                (factor * inverse).astype(bf), rcv_m[:, :, cols].reshape(H * L * CAP, D)
            ) + own_mix[:, cols] * (own_factor * inverse)
            out[:, cols] = jnp.where(live_c, result, 0.0).astype(bf)
    for copies in [hs, bqs, ps, vs, ls] + qs + ms:
        for copy in copies:
            copy.wait_send()


def fused_body(
    hidden, base_q, base_k, base_v, a_in, b_out, cache, generated, thm, live, apr, ppr, cnt
):
    H, MP = lax.axis_size("hosts"), lax.axis_size("mp")
    A, W = hidden.shape
    CAP = A // H
    L, SUF = cache.shape[0], generated.shape[2]
    HEADS = W // HEAD_SIZE
    S = H * CAP
    NCH = 2
    bf, f32 = jnp.bfloat16, jnp.float32
    N = generated.shape[0] * 2 * SUF
    sizes = (H, MP, A, CAP, L, apr.shape[0], ppr.shape[1], HEADS, SUF, NCH)
    smem = pl.BlockSpec(memory_space=pltpu.SMEM)
    vmem = pl.BlockSpec(memory_space=pltpu.VMEM)
    hbm = pl.BlockSpec(memory_space=pl.ANY)
    fold = (H, 2 * CAP, W // 2)
    sem = lambda *shape: pltpu.SemaphoreType.DMA(shape)
    return pl.pallas_call(
        functools.partial(fused_kernel, sizes),
        out_shape=[jax.ShapeDtypeStruct((A, W), bf)] * 3,
        in_specs=[smem] * 5 + [vmem] * 4 + [hbm] * 4,
        out_specs=[vmem] * 3,
        scratch_shapes=[
            pltpu.VMEM(a_in.shape, bf),
            pltpu.VMEM(b_out.shape, bf),
            pltpu.VMEM(cache.shape, bf),
            pltpu.VMEM((N, W), bf),
            pltpu.VMEM(fold, bf),
            pltpu.VMEM(fold, bf),
            pltpu.VMEM(fold, bf),
            pltpu.VMEM(fold, bf),
            pltpu.VMEM((MP, S, 128), f32),
            pltpu.VMEM(fold, bf),
            pltpu.VMEM(fold, bf),
            pltpu.VMEM((H, L * CAP, W), bf),
            pltpu.VMEM((H, L * CAP, W), bf),
            pltpu.VMEM((H, HEADS, 128), f32),
            pltpu.VMEM((H, HEADS, 128), f32),
            pltpu.VMEM((A, W), f32),
            sem(4), sem(H), sem(H), sem(H), sem(H), sem(MP), sem(MP),
            sem(NCH, H), sem(NCH, H), sem(H), sem(H), sem(NCH, H), sem(NCH, H), sem(H), sem(H),
        ]
        + [pltpu.VMEM((H, S, W // NCH), bf)] * NCH,
        compiler_params=pltpu.CompilerParams(
            collective_id=0, has_side_effects=True, vmem_limit_bytes=60 * 1024 * 1024
        ),
        cost_estimate=pl.CostEstimate(
            flops=2 * 10**8, bytes_accessed=4 * 10**6, transcendentals=10**6
        ),
    )(
        thm, live, apr, ppr, cnt, hidden, base_q, base_k, base_v, a_in, b_out, cache,
        generated.reshape(N, W),
    )


def step(hidden, base_q, base_k, base_v, a_in, b_out, cache, generated, thm, live, apr, ppr, cnt):
    H = lax.axis_size("hosts")
    A, W = hidden.shape
    capacity = A // H
    fits = (
        capacity == 8
        and H <= 8
        and A <= 128
        and a_in.shape[0] == 1
        and A * cache.shape[0] == 128
        and cache.shape[2] == 128
        and H * A == 128
        and W == 8 * HEAD_SIZE
        and generated.shape[2] == 8
        and apr.shape[0] < 8
    )
    run = fused_body if fits else body
    return run(hidden, base_q, base_k, base_v, a_in, b_out, cache, generated, thm, live, apr, ppr, cnt)


def solution(mesh):
    placed = (
        P(("groups", "hosts"), "mp"),
        P(("groups", "hosts"), "mp"),
        P(("groups", "hosts"), "mp"),
        P(("groups", "hosts"), "mp"),
        P(("groups", "hosts"), "mp", None),
        P(("groups", "hosts"), None, None, "mp"),
        P(("groups", "hosts"), None, None, "mp"),
        P(("groups", "hosts"), None, None, "mp"),
        P(("groups", "hosts")),
        P(("groups", "hosts")),
        P("groups"),
        P("groups", None),
        P("groups"),
    )
    return jax.shard_map(
        step,
        mesh=mesh,
        in_specs=placed,
        out_specs=(
            P(("groups", "hosts"), "mp"),
            P(("groups", "hosts"), "mp"),
            P(("groups", "hosts"), "mp"),
        ),
        check_vma=False,
    )
```

```python
import functools
import math

import jax
import jax.numpy as jnp
from jax import lax
from jax.experimental import pallas as pl
from jax.experimental.pallas import tpu as pltpu
from jax.sharding import PartitionSpec as P

HEAD_SIZE = 128
ADAPTER_RANK = 64
BLK = 128
PBLK = 4


ADAPTER_SCALE = 0.5
ROPE_BASE = 10000.0
NEG_FILL = -1e30
MESH = pl.DeviceIdType.MESH


def rotate(values, position):
    shaped = values.reshape(values.shape[:-1] + (-1, HEAD_SIZE))
    halfway = HEAD_SIZE // 2
    frequency = ROPE_BASE ** (-(jnp.arange(halfway, dtype=jnp.float32) * (2.0 / HEAD_SIZE)))
    angles = position.astype(jnp.float32)[..., None] * frequency
    cosine = jnp.cos(angles)[..., None, :]
    sine_part = jnp.sin(angles)[..., None, :]
    first_half = shaped[..., :halfway]
    second = shaped[..., halfway:]
    turned = jnp.concatenate(
        [first_half * cosine - second * sine_part, second * cosine + first_half * sine_part],
        axis=-1,
    )
    return turned.reshape(values.shape)


def lookup_table(source_table, wanted):
    matches = wanted[:, None] == jnp.arange(source_table.shape[0], dtype=jnp.int32)[None, :]
    if source_table.ndim == 1:
        return jnp.sum(jnp.where(matches, source_table[None, :], 0), axis=1)
    return jnp.sum(jnp.where(matches[:, :, None], source_table[None, :, :], 0), axis=1)


def route_matrix(destination, validity, capacity, host_total):
    ordinal = jnp.arange(destination.shape[0], dtype=jnp.int32)
    earlier = (
        (destination[:, None] == destination[None, :])
        & validity[None, :]
        & (ordinal[None, :] < ordinal[:, None])
    )
    ranking = jnp.sum(earlier.astype(jnp.int32), axis=1)
    target = destination * capacity + ranking
    places = jnp.arange(host_total * capacity, dtype=jnp.int32)
    return ((places[:, None] == target[None, :]) & validity[None, :]).astype(jnp.bfloat16)


def pack_rows(router, payload):
    return jnp.dot(router, payload, preferred_element_type=jnp.float32).astype(jnp.bfloat16)


def attend_local(queries, chosen, statement_prefix_cache):
    head_count = queries.shape[-1] // HEAD_SIZE
    blocks = statement_prefix_cache.shape[0]
    block_keys = statement_prefix_cache[:, 0].reshape(
        blocks, statement_prefix_cache.shape[2], head_count, HEAD_SIZE
    )
    block_values = statement_prefix_cache[:, 1].reshape(
        blocks, statement_prefix_cache.shape[2], head_count, HEAD_SIZE
    )
    shaped = queries.reshape(queries.shape[:-1] + (head_count, HEAD_SIZE))
    scores = jnp.einsum(
        "nchd,bthd->ncbht", shaped, block_keys, preferred_element_type=jnp.float32
    ) * HEAD_SIZE ** (-0.5)
    chosen_mask = (chosen > 0)[:, :, :, None, None]
    masked = jnp.where(chosen_mask, scores, NEG_FILL)
    top_score = jnp.max(masked, axis=(2, 4))
    weights = jnp.where(chosen_mask, jnp.exp(masked - top_score[:, :, None, :, None]), 0.0)
    totals = jnp.sum(weights, axis=(2, 4))
    mixed_rows = jnp.einsum(
        "ncbht,bthd->nchd",
        weights.astype(jnp.bfloat16),
        block_values,
        preferred_element_type=jnp.float32,
    )
    return (mixed_rows.reshape(queries.shape), top_score, totals)


def body(
    hidden,
    base_query_projection,
    base_key_projection,
    base_value_projection,
    adapter_input_factors,
    adapter_output_factors,
    statement_prefix_cache,
    generated_token_cache,
    attempt_theorem_index,
    host_live_count,
    adapter_pool_row,
    prefix_pool_row,
    prefix_block_count,
):
    host_total = lax.axis_size("hosts")
    attempts = hidden.shape[0]
    capacity = max(1, attempts // host_total)
    owner_held_rows = adapter_input_factors.shape[0]
    local_blocks = statement_prefix_cache.shape[0]
    row_width = base_query_projection.shape[1]
    head_count = row_width // HEAD_SIZE
    ordinal = jnp.arange(attempts, dtype=jnp.int32)
    living = ordinal < host_live_count[0]
    adapter_rows = lookup_table(adapter_pool_row, attempt_theorem_index)
    block_rows = lookup_table(prefix_pool_row, attempt_theorem_index)
    block_counts = lookup_table(prefix_block_count, attempt_theorem_index)
    position = BLK * block_counts + generated_token_cache.shape[2]
    adapter_router = route_matrix(adapter_rows // owner_held_rows, living, capacity, host_total)
    adapter_pick = (
        adapter_rows[:, None] % owner_held_rows
        == jnp.arange(owner_held_rows, dtype=jnp.int32)[None, :]
    ).astype(jnp.bfloat16)
    sent_hidden = pack_rows(adapter_router, hidden).reshape(host_total, capacity, hidden.shape[1])
    sent_pick = pack_rows(adapter_router, adapter_pick).reshape(
        host_total, capacity, owner_held_rows
    )
    incoming_rows = lax.all_to_all(sent_hidden, "hosts", split_axis=0, concat_axis=0, tiled=True)
    pick_in = lax.all_to_all(sent_pick, "hosts", split_axis=0, concat_axis=0, tiled=True)
    projected_rows = jnp.einsum(
        "xjp,epk->xjek", incoming_rows, adapter_input_factors, preferred_element_type=jnp.float32
    )
    partial_rank = jnp.sum(projected_rows * pick_in.astype(jnp.float32)[..., None], axis=2)
    rank_rows = lax.psum(partial_rank, "mp").astype(jnp.bfloat16)
    spread_rows = rank_rows[:, :, None, :] * pick_in[..., None]
    query_correction = jnp.einsum(
        "exqw,qwf->exf",
        spread_rows[..., :ADAPTER_RANK],
        adapter_output_factors[:, 0],
        preferred_element_type=jnp.float32,
    )
    value_correction = jnp.einsum(
        "exqw,qwf->exf",
        spread_rows[..., ADAPTER_RANK:],
        adapter_output_factors[:, 1],
        preferred_element_type=jnp.float32,
    )
    adapter_corrections = (
        jnp.concatenate([query_correction, value_correction], axis=-1) * ADAPTER_SCALE
    ).astype(jnp.bfloat16)
    returned = lax.all_to_all(adapter_corrections, "hosts", split_axis=0, concat_axis=0, tiled=True)
    adapter_corrections = jnp.dot(
        adapter_router.T,
        returned.reshape(host_total * capacity, 2 * row_width),
        preferred_element_type=jnp.float32,
    )
    query_rows = rotate(
        base_query_projection.astype(jnp.float32) + adapter_corrections[:, :row_width], position
    ).astype(jnp.bfloat16)
    value_rows = (
        base_value_projection.astype(jnp.float32) + adapter_corrections[:, row_width:]
    ).astype(jnp.bfloat16)
    key_rows = rotate(base_key_projection.astype(jnp.float32), position).astype(jnp.bfloat16)
    requests = []
    for block_index in range(PBLK):
        wanted = living & (block_index < block_counts)
        holder = block_rows[:, block_index]
        router = route_matrix(holder // local_blocks, wanted, capacity, host_total)
        block_pick = (
            holder[:, None] % local_blocks == jnp.arange(local_blocks, dtype=jnp.int32)[None, :]
        ).astype(jnp.bfloat16)
        sent_queries = pack_rows(router, query_rows).reshape(host_total, capacity, row_width)
        sent_blocks = pack_rows(router, block_pick).reshape(host_total, capacity, local_blocks)
        requests.append((router, wanted, sent_queries, sent_blocks))
    partials = []
    for request in requests:
        answer_mixed_rows, answer_top_score, answer_totals = attend_local(
            lax.all_to_all(request[2], "hosts", split_axis=0, concat_axis=0, tiled=True),
            lax.all_to_all(request[3], "hosts", split_axis=0, concat_axis=0, tiled=True),
            statement_prefix_cache,
        )
        partials.append(
            (
                lax.all_to_all(answer_mixed_rows, "hosts", split_axis=0, concat_axis=0, tiled=True),
                lax.all_to_all(answer_top_score, "hosts", split_axis=0, concat_axis=0, tiled=True),
                lax.all_to_all(answer_totals, "hosts", split_axis=0, concat_axis=0, tiled=True),
            )
        )
    entries = []
    for block_index in range(PBLK):
        router, wanted = (requests[block_index][0], requests[block_index][1])
        mixed_rows, top_score, totals = partials[block_index]
        back_router = router.T.astype(jnp.float32)
        flat_mixed = jnp.dot(
            back_router,
            mixed_rows.reshape(host_total * capacity, row_width),
            precision=lax.Precision.HIGHEST,
        )
        flat_top = jnp.dot(
            back_router,
            top_score.reshape(host_total * capacity, head_count),
            precision=lax.Precision.HIGHEST,
        )
        flat_totals = jnp.dot(
            back_router,
            totals.reshape(host_total * capacity, head_count),
            precision=lax.Precision.HIGHEST,
        )
        flat_top = jnp.where(wanted[:, None], flat_top, NEG_FILL)
        entries.append((flat_mixed, flat_top, flat_totals))
    shaped_query = query_rows.reshape(attempts, head_count, HEAD_SIZE)
    own_keys = jnp.concatenate([generated_token_cache[:, 0], key_rows[:, None, :]], axis=1).reshape(
        attempts, -1, head_count, HEAD_SIZE
    )
    own_values = jnp.concatenate(
        [generated_token_cache[:, 1], value_rows[:, None, :]], axis=1
    ).reshape(attempts, -1, head_count, HEAD_SIZE)
    own_scores = jnp.einsum(
        "ahd,athd->aht", shaped_query, own_keys, preferred_element_type=jnp.float32
    ) * HEAD_SIZE ** (-0.5)
    own_top = jnp.max(own_scores, axis=2)
    own_weights = jnp.exp(own_scores - own_top[..., None])
    own_totals = jnp.sum(own_weights, axis=2)
    own_mixed = jnp.einsum(
        "aht,athd->ahd",
        own_weights.astype(jnp.bfloat16),
        own_values,
        preferred_element_type=jnp.float32,
    )
    overall = own_top
    for flat_mixed, flat_top, flat_totals in entries:
        overall = jnp.maximum(overall, flat_top)
    own_factor = jnp.exp(own_top - overall)
    numerator = own_mixed * own_factor[..., None]
    denominator = own_totals * own_factor
    for flat_mixed, flat_top, flat_totals in entries:
        factor = jnp.exp(flat_top - overall)
        numerator = (
            numerator + flat_mixed.reshape(attempts, head_count, HEAD_SIZE) * factor[..., None]
        )
        denominator = denominator + flat_totals * factor
    attended = (numerator / denominator[..., None]).reshape(attempts, row_width)
    live_rows = living[:, None]
    return (
        jnp.where(live_rows, attended, 0.0).astype(jnp.bfloat16),
        jnp.where(live_rows, key_rows, 0.0),
        jnp.where(live_rows, value_rows, 0.0),
    )


def _iota(shape, dim):
    return lax.broadcasted_iota(jnp.int32, shape, dim)


def _dot(a, b):
    return jnp.dot(a, b, preferred_element_type=jnp.float32)


def _dot_t(a, b):
    return lax.dot_general(a, b, (((1,), (1,)), ((), ())), preferred_element_type=jnp.float32)


def fused_kernel(
    sizes,
    thm, apr, ppr, cnt,
    hidden, base_q, live_hbm, k_hbm, val_hbm, a_hbm, b_hbm, kv_hbm, gen_hbm,
    out, key_out, val_out,
    live, base_k, base_v, a_v, b_v, kv_v, gen_v,
    snd_h, rcv_h, snd_q, rcv_q, part, snd_v, rcv_v, snd_m, rcv_m, snd_l, rcv_l, own_mix,
    local_sem, h_s, h_r, bq_s, bq_r, p_s, p_r, q_s, q_r, v_s, v_r, m_s, m_r, l_s, l_r,
    *queries,
):
    H, MP, A, CAP, L, T, PB, HEADS, SUF, NCH = sizes
    f32, bf = jnp.float32, jnp.bfloat16
    D = HEAD_SIZE
    W = HEADS * D
    W2 = W // 2
    S = H * CAP
    CW = W // NCH
    shift = CAP.bit_length() - 1
    me = lax.axis_index("hosts")
    mme = lax.axis_index("mp")

    def other(axis, d):
        return lax.rem((me if axis == "hosts" else mme) + d, H if axis == "hosts" else MP)

    locals_ = [
        pltpu.make_async_copy(src, dst, local_sem.at[i])
        for i, (src, dst) in enumerate(
            [
                (a_hbm, a_v), (b_hbm, b_v), (kv_hbm, kv_v), (gen_hbm, gen_v),
                (live_hbm, live), (k_hbm, base_k), (val_hbm, base_v),
            ]
        )
    ]
    for i in (4, 0, 1, 2, 5, 6, 3):
        locals_[i].start()

    barrier = pltpu.get_barrier_semaphore()
    for d in range(1, H):
        pl.semaphore_signal(barrier, inc=1, device_id={"hosts": other("hosts", d)}, device_id_type=MESH)
    for d in range(1, MP):
        pl.semaphore_signal(barrier, inc=1, device_id={"mp": other("mp", d)}, device_id_type=MESH)

    def send(src, dst, s, r, axis, d):
        copy = pltpu.make_async_remote_copy(
            src_ref=src, dst_ref=dst, send_sem=s, recv_sem=r,
            device_id={axis: other(axis, d)}, device_id_type=MESH,
        )
        copy.start()
        return copy

    lane8, sub8 = _iota((8, 128), 1), _iota((8, 128), 0)
    th = jnp.full((8, 128), -1, jnp.int32)
    for a in range(A):
        th = jnp.where(lane8 == a, thm[a], th)
    owner = jnp.full((8, 128), -1, jnp.int32)
    for t in range(T):
        owner = jnp.where(th == t, apr[t], owner)
    locals_[4].wait()
    n_live = live[0]
    owner = jnp.where(lane8 < n_live, owner, -1)
    member = jnp.where(owner == sub8, 1.0, 0.0).astype(f32)
    before = jnp.where(_iota((128, 128), 0) < _iota((128, 128), 1), 1.0, 0.0).astype(bf)
    rank_f = jnp.sum(member * _dot(member.astype(bf), before), axis=0, keepdims=True)
    rank_row = rank_f.astype(jnp.int32)
    target = jnp.where(owner[0:1] >= 0, owner[0:1] * CAP + rank_row, -1)
    router = jnp.where(_iota((S, A), 0) == target[:, :A], 1.0, 0.0).astype(bf)

    def folded(rows, e):
        piece = rows[e * CAP : (e + 1) * CAP]
        return jnp.concatenate([piece[:, :W2], piece[:, W2:]], axis=0)

    packed = _dot(router, hidden[...])
    for e in range(H):
        snd_h[e] = folded(packed, e).astype(bf)
    pl.semaphore_wait(barrier, H - 1 + MP - 1)
    hs = [
        send(snd_h.at[other("hosts", d)], rcv_h.at[me], h_s.at[d], h_r.at[d], "hosts", d)
        for d in range(1, H)
    ]
    packed = _dot(router, base_q[...])
    for e in range(H):
        snd_q[e] = folded(packed, e).astype(bf)
    bqs = [
        send(snd_q.at[other("hosts", d)], rcv_q.at[me], bq_s.at[d], bq_r.at[d], "hosts", d)
        for d in range(1, H)
    ]
    rcv_h[me] = snd_h[me]
    rcv_q[me] = snd_q[me]

    lane = _iota((8, 128), 1)
    half = jnp.where(lane < D // 2, lane, lane - D // 2).astype(f32)
    freq = jnp.exp(half * (-2.0 / D * math.log(ROPE_BASE)))
    counts = jnp.zeros((8, 128), jnp.int32)
    my_count = jnp.int32(0)
    for t in range(T):
        counts = jnp.where(sub8 == t, cnt[t], counts)
        my_count = jnp.where(apr[t] == me, cnt[t], my_count)
    counts = jnp.where(sub8 == T, my_count, counts)
    angle = (BLK * counts + SUF).astype(f32) * freq
    cos_t = jnp.cos(angle)
    sin_t = jnp.sin(angle)
    sin_t = jnp.where(lane < D // 2, -sin_t, sin_t)

    def turn(x, c, s):
        return x * c + pltpu.roll(x, D // 2, 1) * s

    locals_[0].wait()
    for copy in hs:
        copy.wait_recv()
    rows = rcv_h[...].reshape(H * 2 * CAP, W2)
    left = _dot(rows, a_v[0, :W2, :])
    right = _dot(rows, a_v[0, W2:, :])
    part[mme] = jnp.concatenate(
        [
            left[2 * CAP * e : 2 * CAP * e + CAP] + right[2 * CAP * e + CAP : 2 * CAP * (e + 1)]
            for e in range(H)
        ],
        axis=0,
    )
    ps = [
        send(part.at[mme], part.at[mme], p_s.at[d], p_r.at[d], "mp", d) for d in range(1, MP)
    ]
    for copy in bqs:
        copy.wait_recv()
    bq = rcv_q[...].astype(f32)
    bq_half = [
        jnp.concatenate([bq[e, k * CAP : (k + 1) * CAP] for e in range(H)], axis=0)
        for k in range(2)
    ]
    locals_[1].wait()
    for copy in ps:
        copy.wait_recv()
    ranks = part[0]
    for m in range(1, MP):
        ranks = ranks + part[m]
    ranks = ranks.astype(bf).astype(f32)
    rank_q = ranks[:, :ADAPTER_RANK].astype(bf)
    rank_v = pltpu.roll(ranks, ADAPTER_RANK, 1)[:, :ADAPTER_RANK].astype(bf)
    qs = []
    for c in range(NCH):
        cols = slice(c * CW, (c + 1) * CW)
        delta = (_dot(rank_q, b_v[0, 0, :, cols]) * ADAPTER_SCALE).astype(bf).astype(f32)
        k, off = (c * CW) // W2, (c * CW) % W2
        raw = bq_half[k][:, off : off + CW] + delta
        for h in range(CW // D):
            queries[c][me, :, h * D : (h + 1) * D] = turn(
                raw[:, h * D : (h + 1) * D], cos_t[T : T + 1], sin_t[T : T + 1]
            ).astype(bf)
        view = queries[c].at[me]
        qs.append(
            [send(view, view, q_s.at[c, d], q_r.at[c, d], "hosts", d) for d in range(1, H)]
        )
    delta = _dot(rank_v, b_v[0, 1]) * ADAPTER_SCALE
    for e in range(H):
        snd_v[e] = folded(delta, e).astype(bf)
    vs = [
        send(snd_v.at[other("hosts", d)], rcv_v.at[me], v_s.at[d], v_r.at[d], "hosts", d)
        for d in range(1, H)
    ]
    rcv_v[me] = snd_v[me]

    sub128 = _iota((128, 128), 0)
    both = jnp.where(sub128 == 0, th[0:1].astype(f32), jnp.where(sub128 == 1, rank_f, 0.0))
    turned = both.T[:A].astype(jnp.int32)
    th_c, rank_c = turned[:, 0:1], turned[:, 1:2]
    lane_a = _iota((A, 128), 1)
    live_c = _iota((A, 1), 0) < n_live
    owner_c = jnp.full((A, 1), -1, jnp.int32)
    cos_a = jnp.zeros((A, 128), f32)
    sin_a = jnp.zeros((A, 128), f32)
    blocks_c = [jnp.full((A, 1), -1, jnp.int32) for _ in range(PB)]
    for t in range(T):
        here = th_c == t
        owner_c = jnp.where(here, apr[t], owner_c)
        cos_a = jnp.where(here, cos_t[t : t + 1], cos_a)
        sin_a = jnp.where(here, sin_t[t : t + 1], sin_a)
        for j in range(PB):
            blocks_c[j] = jnp.where(here, jnp.where(j < cnt[t], ppr[t, j], -1), blocks_c[j])
    owner_c = jnp.where(live_c, owner_c, -1)
    slot_ok = jnp.where(rank_c == (lane_a & (CAP - 1)), 1, 0)
    group = lane_a >> shift
    used = jnp.zeros((A, 128), jnp.int32)
    for j in range(PB):
        used = used + jnp.where(blocks_c[j] == group, 1, 0)
    used = jnp.where(live_c, used * slot_ok, 0) > 0
    fetch = jnp.where(owner_c * H + me == group, slot_ok, 0).astype(f32).astype(bf)
    unpack = jnp.where(
        owner_c * CAP + rank_c == _iota((A, S), 1), jnp.where(owner_c >= 0, 1.0, 0.0), 0.0
    ).astype(bf)
    keys = []
    locals_[5].wait()
    for h in range(HEADS):
        cols = slice(h * D, (h + 1) * D)
        key = turn(base_k[:, cols].astype(f32), cos_a, sin_a).astype(bf).astype(f32)
        keys.append(key)
        key_out[:, cols] = jnp.where(live_c, key, 0.0).astype(bf)

    whose = []
    for b in range(L):
        index = jnp.int32(0)
        for t in range(T):
            for j in range(PB):
                index = jnp.where(ppr[t, j] == me * L + b, apr[t], index)
        whose.append(index)
    scale = D ** (-0.5)
    locals_[2].wait()
    lane128 = _iota((128, 128), 1)
    lse_all = jnp.zeros((128, 128), f32)
    ms = []
    for c in range(NCH):
        for copy in qs[c]:
            copy.wait_recv()
        for h in range(c * CW // D, (c + 1) * CW // D):
            cols = slice(h * D, (h + 1) * D)
            within = slice(h * D - c * CW, (h + 1) * D - c * CW)
            scores = jnp.concatenate(
                [_dot_t(queries[c][whose[b], :, within], kv_v[b, 0, :, cols]) for b in range(L)], axis=0
            ) * scale
            top = jnp.max(scores, axis=1, keepdims=True)
            weights = jnp.exp(scores - top)
            total = jnp.sum(weights, axis=1, keepdims=True)
            weights = weights.astype(bf)
            mixed = jnp.concatenate(
                [_dot(weights[b * S : (b + 1) * S], kv_v[b, 1, :, cols]) for b in range(L)], axis=0
            ) * (1.0 / total)
            lse_all = jnp.where(lane128 == h, top + jnp.log(total), lse_all)
            for e in range(H):
                snd_m[e, :, cols] = jnp.concatenate(
                    [mixed[b * S + e * CAP : b * S + (e + 1) * CAP] for b in range(L)], axis=0
                ).astype(bf)
        if c == NCH - 1:
            ordered = jnp.concatenate(
                [
                    lse_all[b * S + e * CAP : b * S + (e + 1) * CAP]
                    for e in range(H)
                    for b in range(L)
                ],
                axis=0,
            )
            lse_t = ordered.T[:HEADS]
            rcv_l[me] = lse_t
            for d in range(1, H):
                snd_l[d] = pltpu.roll(lse_t, (128 - L * CAP * d) % 128, 1)
            ls = [
                send(snd_l.at[d], rcv_l.at[me], l_s.at[d], l_r.at[d], "hosts", d)
                for d in range(1, H)
            ]
        span = pl.ds(c * CW, CW)
        ms.append(
            [
                send(
                    snd_m.at[other("hosts", d), :, span], rcv_m.at[me, :, span],
                    m_s.at[c, d], m_r.at[c, d], "hosts", d,
                )
                for d in range(1, H)
            ]
        )
    rcv_m[me] = snd_m[me]

    locals_[3].wait()
    locals_[6].wait()
    for copy in vs:
        copy.wait_recv()
    dv = rcv_v[...].astype(f32)
    dv_att = [
        _dot(
            unpack,
            jnp.concatenate([dv[p, k * CAP : (k + 1) * CAP] for p in range(H)], axis=0).astype(bf),
        )
        for k in range(2)
    ]
    N = gen_v.shape[0]
    lane_n, sub_n = _iota((A, N), 1), _iota((A, N), 0)
    mine = ((lane_n >> (SUF.bit_length())) == sub_n) & ((lane_n & (2 * SUF - 1)) < SUF)
    own_top, own_total = [], []
    for h in range(HEADS):
        cols = slice(h * D, (h + 1) * D)
        k, off = (h * D) // W2, (h * D) % W2
        value = (base_v[:, cols].astype(f32) + dv_att[k][:, off : off + D]).astype(bf).astype(f32)
        val_out[:, cols] = jnp.where(live_c, value, 0.0).astype(bf)
        c, start = (h * D) // CW, (h * D) % CW
        query = _dot(fetch, queries[c][:, :, start : start + D].reshape(H * S, D))
        scores = _dot_t(query.astype(bf), gen_v[:, cols]) * scale
        scores = jnp.where(mine, scores, NEG_FILL)
        self_score = jnp.sum(query * keys[h], axis=1, keepdims=True) * scale
        top = jnp.maximum(jnp.max(scores, axis=1, keepdims=True), self_score)
        weights = jnp.where(mine, jnp.exp(scores - top), 0.0)
        self_weight = jnp.exp(self_score - top)
        own_top.append(top)
        own_total.append(jnp.sum(weights, axis=1, keepdims=True) + self_weight)
        own_mix[:, cols] = (
            _dot(pltpu.roll(weights, SUF, 1).astype(bf), gen_v[:, cols])
            + self_weight.astype(bf).astype(f32) * value
        )

    for copy in ls:
        copy.wait_recv()
    lse = jnp.zeros((HEADS, 128), f32)
    lane_h = _iota((HEADS, 128), 1)
    for g in range(H):
        lse = jnp.where((lane_h >= g * L * CAP) & (lane_h < (g + 1) * L * CAP), rcv_l[g], lse)
    for c in range(NCH):
        for copy in ms[c]:
            copy.wait_recv()
        for h in range(c * CW // D, (c + 1) * CW // D):
            cols = slice(h * D, (h + 1) * D)
            logs = jnp.where(used, lse[h : h + 1], NEG_FILL)
            top = jnp.maximum(jnp.max(logs, axis=1, keepdims=True), own_top[h])
            factor = jnp.where(used, jnp.exp(logs - top), 0.0)
            own_factor = jnp.exp(own_top[h] - top)
            inverse = 1.0 / (jnp.sum(factor, axis=1, keepdims=True) + own_total[h] * own_factor)
            result = _dot(
                (factor * inverse).astype(bf), rcv_m[:, :, cols].reshape(H * L * CAP, D)
            ) + own_mix[:, cols] * (own_factor * inverse)
            out[:, cols] = jnp.where(live_c, result, 0.0).astype(bf)
    for copies in [hs, bqs, ps, vs, ls] + qs + ms:
        for copy in copies:
            copy.wait_send()


def write_kernel(*refs):
    sems = refs[6]
    copies = [pltpu.make_async_copy(refs[i], refs[3 + i], sems.at[i]) for i in range(3)]
    for copy in copies:
        copy.start()
    for copy in copies:
        copy.wait()


def fused_body(
    hidden, base_q, base_k, base_v, a_in, b_out, cache, generated, thm, live, apr, ppr, cnt
):
    H, MP = lax.axis_size("hosts"), lax.axis_size("mp")
    A, W = hidden.shape
    CAP = A // H
    L, SUF = cache.shape[0], generated.shape[2]
    HEADS = W // HEAD_SIZE
    S = H * CAP
    NCH = 2
    bf, f32 = jnp.bfloat16, jnp.float32
    N = generated.shape[0] * 2 * SUF
    sizes = (H, MP, A, CAP, L, apr.shape[0], ppr.shape[1], HEADS, SUF, NCH)
    smem = pl.BlockSpec(memory_space=pltpu.SMEM)
    vmem = pl.BlockSpec(memory_space=pltpu.VMEM)
    hbm = pl.BlockSpec(memory_space=pl.ANY)
    fold = (H, 2 * CAP, W // 2)
    sem = lambda *shape: pltpu.SemaphoreType.DMA(shape)
    results = pl.pallas_call(
        functools.partial(fused_kernel, sizes),
        out_shape=[pltpu.VMEM((A, W), bf)] * 3,
        in_specs=[smem] * 4 + [vmem] * 2 + [hbm] * 7,
        out_specs=[vmem] * 3,
        scratch_shapes=[
            pltpu.SMEM(live.shape, jnp.int32),
            pltpu.VMEM((A, W), bf),
            pltpu.VMEM((A, W), bf),
            pltpu.VMEM(a_in.shape, bf),
            pltpu.VMEM(b_out.shape, bf),
            pltpu.VMEM(cache.shape, bf),
            pltpu.VMEM((N, W), bf),
            pltpu.VMEM(fold, bf),
            pltpu.VMEM(fold, bf),
            pltpu.VMEM(fold, bf),
            pltpu.VMEM(fold, bf),
            pltpu.VMEM((MP, S, 128), f32),
            pltpu.VMEM(fold, bf),
            pltpu.VMEM(fold, bf),
            pltpu.VMEM((H, L * CAP, W), bf),
            pltpu.VMEM((H, L * CAP, W), bf),
            pltpu.VMEM((H, HEADS, 128), f32),
            pltpu.VMEM((H, HEADS, 128), f32),
            pltpu.VMEM((A, W), f32),
            sem(7), sem(H), sem(H), sem(H), sem(H), sem(MP), sem(MP),
            sem(NCH, H), sem(NCH, H), sem(H), sem(H), sem(NCH, H), sem(NCH, H), sem(H), sem(H),
        ]
        + [pltpu.VMEM((H, S, W // NCH), bf)] * NCH,
        compiler_params=pltpu.CompilerParams(
            collective_id=0, has_side_effects=True, vmem_limit_bytes=60 * 1024 * 1024
        ),
        cost_estimate=pl.CostEstimate(
            flops=2 * 10**8, bytes_accessed=4 * 10**6, transcendentals=10**6
        ),
    )(
        thm, apr, ppr, cnt, hidden, base_q, live, base_k, base_v, a_in, b_out, cache,
        generated.reshape(N, W),
    )
    return pl.pallas_call(
        write_kernel,
        out_shape=[jax.ShapeDtypeStruct((A, W), bf)] * 3,
        in_specs=[vmem] * 3,
        out_specs=[hbm] * 3,
        scratch_shapes=[sem(3)],
    )(*results)


def step(hidden, base_q, base_k, base_v, a_in, b_out, cache, generated, thm, live, apr, ppr, cnt):
    H = lax.axis_size("hosts")
    A, W = hidden.shape
    capacity = A // H
    fits = (
        capacity == 8
        and H <= 8
        and A <= 128
        and a_in.shape[0] == 1
        and A * cache.shape[0] == 128
        and cache.shape[2] == 128
        and H * A == 128
        and W == 8 * HEAD_SIZE
        and generated.shape[2] == 8
        and apr.shape[0] < 8
    )
    run = fused_body if fits else body
    return run(hidden, base_q, base_k, base_v, a_in, b_out, cache, generated, thm, live, apr, ppr, cnt)


def solution(mesh):
    placed = (
        P(("groups", "hosts"), "mp"),
        P(("groups", "hosts"), "mp"),
        P(("groups", "hosts"), "mp"),
        P(("groups", "hosts"), "mp"),
        P(("groups", "hosts"), "mp", None),
        P(("groups", "hosts"), None, None, "mp"),
        P(("groups", "hosts"), None, None, "mp"),
        P(("groups", "hosts"), None, None, "mp"),
        P(("groups", "hosts")),
        P(("groups", "hosts")),
        P("groups"),
        P("groups", None),
        P("groups"),
    )
    return jax.shard_map(
        step,
        mesh=mesh,
        in_specs=placed,
        out_specs=(
            P(("groups", "hosts"), "mp"),
            P(("groups", "hosts"), "mp"),
            P(("groups", "hosts"), "mp"),
        ),
        check_vma=False,
    )
```

```python
import functools
import math

import jax
import jax.numpy as jnp
from jax import lax
from jax.experimental import pallas as pl
from jax.experimental.pallas import tpu as pltpu
from jax.sharding import PartitionSpec as P

HEAD_SIZE = 128
ADAPTER_RANK = 64
BLK = 128
PBLK = 4


ADAPTER_SCALE = 0.5
ROPE_BASE = 10000.0
NEG_FILL = -1e30
MESH = pl.DeviceIdType.MESH


def rotate(values, position):
    shaped = values.reshape(values.shape[:-1] + (-1, HEAD_SIZE))
    halfway = HEAD_SIZE // 2
    frequency = ROPE_BASE ** (-(jnp.arange(halfway, dtype=jnp.float32) * (2.0 / HEAD_SIZE)))
    angles = position.astype(jnp.float32)[..., None] * frequency
    cosine = jnp.cos(angles)[..., None, :]
    sine_part = jnp.sin(angles)[..., None, :]
    first_half = shaped[..., :halfway]
    second = shaped[..., halfway:]
    turned = jnp.concatenate(
        [first_half * cosine - second * sine_part, second * cosine + first_half * sine_part],
        axis=-1,
    )
    return turned.reshape(values.shape)


def lookup_table(source_table, wanted):
    matches = wanted[:, None] == jnp.arange(source_table.shape[0], dtype=jnp.int32)[None, :]
    if source_table.ndim == 1:
        return jnp.sum(jnp.where(matches, source_table[None, :], 0), axis=1)
    return jnp.sum(jnp.where(matches[:, :, None], source_table[None, :, :], 0), axis=1)


def route_matrix(destination, validity, capacity, host_total):
    ordinal = jnp.arange(destination.shape[0], dtype=jnp.int32)
    earlier = (
        (destination[:, None] == destination[None, :])
        & validity[None, :]
        & (ordinal[None, :] < ordinal[:, None])
    )
    ranking = jnp.sum(earlier.astype(jnp.int32), axis=1)
    target = destination * capacity + ranking
    places = jnp.arange(host_total * capacity, dtype=jnp.int32)
    return ((places[:, None] == target[None, :]) & validity[None, :]).astype(jnp.bfloat16)


def pack_rows(router, payload):
    return jnp.dot(router, payload, preferred_element_type=jnp.float32).astype(jnp.bfloat16)


def attend_local(queries, chosen, statement_prefix_cache):
    head_count = queries.shape[-1] // HEAD_SIZE
    blocks = statement_prefix_cache.shape[0]
    block_keys = statement_prefix_cache[:, 0].reshape(
        blocks, statement_prefix_cache.shape[2], head_count, HEAD_SIZE
    )
    block_values = statement_prefix_cache[:, 1].reshape(
        blocks, statement_prefix_cache.shape[2], head_count, HEAD_SIZE
    )
    shaped = queries.reshape(queries.shape[:-1] + (head_count, HEAD_SIZE))
    scores = jnp.einsum(
        "nchd,bthd->ncbht", shaped, block_keys, preferred_element_type=jnp.float32
    ) * HEAD_SIZE ** (-0.5)
    chosen_mask = (chosen > 0)[:, :, :, None, None]
    masked = jnp.where(chosen_mask, scores, NEG_FILL)
    top_score = jnp.max(masked, axis=(2, 4))
    weights = jnp.where(chosen_mask, jnp.exp(masked - top_score[:, :, None, :, None]), 0.0)
    totals = jnp.sum(weights, axis=(2, 4))
    mixed_rows = jnp.einsum(
        "ncbht,bthd->nchd",
        weights.astype(jnp.bfloat16),
        block_values,
        preferred_element_type=jnp.float32,
    )
    return (mixed_rows.reshape(queries.shape), top_score, totals)


def body(
    hidden,
    base_query_projection,
    base_key_projection,
    base_value_projection,
    adapter_input_factors,
    adapter_output_factors,
    statement_prefix_cache,
    generated_token_cache,
    attempt_theorem_index,
    host_live_count,
    adapter_pool_row,
    prefix_pool_row,
    prefix_block_count,
):
    host_total = lax.axis_size("hosts")
    attempts = hidden.shape[0]
    capacity = max(1, attempts // host_total)
    owner_held_rows = adapter_input_factors.shape[0]
    local_blocks = statement_prefix_cache.shape[0]
    row_width = base_query_projection.shape[1]
    head_count = row_width // HEAD_SIZE
    ordinal = jnp.arange(attempts, dtype=jnp.int32)
    living = ordinal < host_live_count[0]
    adapter_rows = lookup_table(adapter_pool_row, attempt_theorem_index)
    block_rows = lookup_table(prefix_pool_row, attempt_theorem_index)
    block_counts = lookup_table(prefix_block_count, attempt_theorem_index)
    position = BLK * block_counts + generated_token_cache.shape[2]
    adapter_router = route_matrix(adapter_rows // owner_held_rows, living, capacity, host_total)
    adapter_pick = (
        adapter_rows[:, None] % owner_held_rows
        == jnp.arange(owner_held_rows, dtype=jnp.int32)[None, :]
    ).astype(jnp.bfloat16)
    sent_hidden = pack_rows(adapter_router, hidden).reshape(host_total, capacity, hidden.shape[1])
    sent_pick = pack_rows(adapter_router, adapter_pick).reshape(
        host_total, capacity, owner_held_rows
    )
    incoming_rows = lax.all_to_all(sent_hidden, "hosts", split_axis=0, concat_axis=0, tiled=True)
    pick_in = lax.all_to_all(sent_pick, "hosts", split_axis=0, concat_axis=0, tiled=True)
    projected_rows = jnp.einsum(
        "xjp,epk->xjek", incoming_rows, adapter_input_factors, preferred_element_type=jnp.float32
    )
    partial_rank = jnp.sum(projected_rows * pick_in.astype(jnp.float32)[..., None], axis=2)
    rank_rows = lax.psum(partial_rank, "mp").astype(jnp.bfloat16)
    spread_rows = rank_rows[:, :, None, :] * pick_in[..., None]
    query_correction = jnp.einsum(
        "exqw,qwf->exf",
        spread_rows[..., :ADAPTER_RANK],
        adapter_output_factors[:, 0],
        preferred_element_type=jnp.float32,
    )
    value_correction = jnp.einsum(
        "exqw,qwf->exf",
        spread_rows[..., ADAPTER_RANK:],
        adapter_output_factors[:, 1],
        preferred_element_type=jnp.float32,
    )
    adapter_corrections = (
        jnp.concatenate([query_correction, value_correction], axis=-1) * ADAPTER_SCALE
    ).astype(jnp.bfloat16)
    returned = lax.all_to_all(adapter_corrections, "hosts", split_axis=0, concat_axis=0, tiled=True)
    adapter_corrections = jnp.dot(
        adapter_router.T,
        returned.reshape(host_total * capacity, 2 * row_width),
        preferred_element_type=jnp.float32,
    )
    query_rows = rotate(
        base_query_projection.astype(jnp.float32) + adapter_corrections[:, :row_width], position
    ).astype(jnp.bfloat16)
    value_rows = (
        base_value_projection.astype(jnp.float32) + adapter_corrections[:, row_width:]
    ).astype(jnp.bfloat16)
    key_rows = rotate(base_key_projection.astype(jnp.float32), position).astype(jnp.bfloat16)
    requests = []
    for block_index in range(PBLK):
        wanted = living & (block_index < block_counts)
        holder = block_rows[:, block_index]
        router = route_matrix(holder // local_blocks, wanted, capacity, host_total)
        block_pick = (
            holder[:, None] % local_blocks == jnp.arange(local_blocks, dtype=jnp.int32)[None, :]
        ).astype(jnp.bfloat16)
        sent_queries = pack_rows(router, query_rows).reshape(host_total, capacity, row_width)
        sent_blocks = pack_rows(router, block_pick).reshape(host_total, capacity, local_blocks)
        requests.append((router, wanted, sent_queries, sent_blocks))
    partials = []
    for request in requests:
        answer_mixed_rows, answer_top_score, answer_totals = attend_local(
            lax.all_to_all(request[2], "hosts", split_axis=0, concat_axis=0, tiled=True),
            lax.all_to_all(request[3], "hosts", split_axis=0, concat_axis=0, tiled=True),
            statement_prefix_cache,
        )
        partials.append(
            (
                lax.all_to_all(answer_mixed_rows, "hosts", split_axis=0, concat_axis=0, tiled=True),
                lax.all_to_all(answer_top_score, "hosts", split_axis=0, concat_axis=0, tiled=True),
                lax.all_to_all(answer_totals, "hosts", split_axis=0, concat_axis=0, tiled=True),
            )
        )
    entries = []
    for block_index in range(PBLK):
        router, wanted = (requests[block_index][0], requests[block_index][1])
        mixed_rows, top_score, totals = partials[block_index]
        back_router = router.T.astype(jnp.float32)
        flat_mixed = jnp.dot(
            back_router,
            mixed_rows.reshape(host_total * capacity, row_width),
            precision=lax.Precision.HIGHEST,
        )
        flat_top = jnp.dot(
            back_router,
            top_score.reshape(host_total * capacity, head_count),
            precision=lax.Precision.HIGHEST,
        )
        flat_totals = jnp.dot(
            back_router,
            totals.reshape(host_total * capacity, head_count),
            precision=lax.Precision.HIGHEST,
        )
        flat_top = jnp.where(wanted[:, None], flat_top, NEG_FILL)
        entries.append((flat_mixed, flat_top, flat_totals))
    shaped_query = query_rows.reshape(attempts, head_count, HEAD_SIZE)
    own_keys = jnp.concatenate([generated_token_cache[:, 0], key_rows[:, None, :]], axis=1).reshape(
        attempts, -1, head_count, HEAD_SIZE
    )
    own_values = jnp.concatenate(
        [generated_token_cache[:, 1], value_rows[:, None, :]], axis=1
    ).reshape(attempts, -1, head_count, HEAD_SIZE)
    own_scores = jnp.einsum(
        "ahd,athd->aht", shaped_query, own_keys, preferred_element_type=jnp.float32
    ) * HEAD_SIZE ** (-0.5)
    own_top = jnp.max(own_scores, axis=2)
    own_weights = jnp.exp(own_scores - own_top[..., None])
    own_totals = jnp.sum(own_weights, axis=2)
    own_mixed = jnp.einsum(
        "aht,athd->ahd",
        own_weights.astype(jnp.bfloat16),
        own_values,
        preferred_element_type=jnp.float32,
    )
    overall = own_top
    for flat_mixed, flat_top, flat_totals in entries:
        overall = jnp.maximum(overall, flat_top)
    own_factor = jnp.exp(own_top - overall)
    numerator = own_mixed * own_factor[..., None]
    denominator = own_totals * own_factor
    for flat_mixed, flat_top, flat_totals in entries:
        factor = jnp.exp(flat_top - overall)
        numerator = (
            numerator + flat_mixed.reshape(attempts, head_count, HEAD_SIZE) * factor[..., None]
        )
        denominator = denominator + flat_totals * factor
    attended = (numerator / denominator[..., None]).reshape(attempts, row_width)
    live_rows = living[:, None]
    return (
        jnp.where(live_rows, attended, 0.0).astype(jnp.bfloat16),
        jnp.where(live_rows, key_rows, 0.0),
        jnp.where(live_rows, value_rows, 0.0),
    )


def _iota(shape, dim):
    return lax.broadcasted_iota(jnp.int32, shape, dim)


def _dot(a, b):
    return jnp.dot(a, b, preferred_element_type=jnp.float32)


def _dot_t(a, b):
    return lax.dot_general(a, b, (((1,), (1,)), ((), ())), preferred_element_type=jnp.float32)


def fused_kernel(
    sizes,
    thm, apr, ppr, cnt,
    hidden, base_q, live_hbm, k_hbm, val_hbm, a_hbm, b_hbm, kv_hbm, gen_hbm,
    out, key_out, val_out,
    live, base_k, base_v, a_v, b_v, kv_v, gen_v,
    snd_h, rcv_h, snd_q, rcv_q, part, snd_v, rcv_v, snd_m, rcv_m, snd_l, rcv_l, own_mix,
    local_sem, h_s, h_r, bq_s, bq_r, p_s, p_r, q_s, q_r, v_s, v_r, m_s, m_r, l_s, l_r,
    *queries,
):
    H, MP, A, CAP, L, T, PB, HEADS, SUF, NCH = sizes
    f32, bf = jnp.float32, jnp.bfloat16
    D = HEAD_SIZE
    W = HEADS * D
    W2 = W // 2
    S = H * CAP
    CW = W // NCH
    shift = CAP.bit_length() - 1
    me = lax.axis_index("hosts")
    mme = lax.axis_index("mp")

    def other(axis, d):
        return lax.rem((me if axis == "hosts" else mme) + d, H if axis == "hosts" else MP)

    locals_ = [
        pltpu.make_async_copy(src, dst, local_sem.at[i])
        for i, (src, dst) in enumerate(
            [
                (a_hbm, a_v), (b_hbm, b_v), (kv_hbm, kv_v), (gen_hbm, gen_v),
                (live_hbm, live), (k_hbm, base_k), (val_hbm, base_v),
            ]
        )
    ]
    for i in (4, 0, 1, 2, 5, 6, 3):
        locals_[i].start()

    barrier = pltpu.get_barrier_semaphore()
    for d in range(1, H):
        pl.semaphore_signal(barrier, inc=1, device_id={"hosts": other("hosts", d)}, device_id_type=MESH)
    for d in range(1, MP):
        pl.semaphore_signal(barrier, inc=1, device_id={"mp": other("mp", d)}, device_id_type=MESH)

    def send(src, dst, s, r, axis, d):
        copy = pltpu.make_async_remote_copy(
            src_ref=src, dst_ref=dst, send_sem=s, recv_sem=r,
            device_id={axis: other(axis, d)}, device_id_type=MESH,
        )
        copy.start()
        return copy

    lane8, sub8 = _iota((8, 128), 1), _iota((8, 128), 0)
    th = jnp.full((8, 128), -1, jnp.int32)
    for a in range(A):
        th = jnp.where(lane8 == a, thm[a], th)
    owner = jnp.full((8, 128), -1, jnp.int32)
    for t in range(T):
        owner = jnp.where(th == t, apr[t], owner)
    locals_[4].wait()
    n_live = live[0]
    owner = jnp.where(lane8 < n_live, owner, -1)
    member = jnp.where(owner == sub8, 1.0, 0.0).astype(f32)
    before = jnp.where(_iota((128, 128), 0) < _iota((128, 128), 1), 1.0, 0.0).astype(bf)
    rank_f = jnp.sum(member * _dot(member.astype(bf), before), axis=0, keepdims=True)
    rank_row = rank_f.astype(jnp.int32)
    target = jnp.where(owner[0:1] >= 0, owner[0:1] * CAP + rank_row, -1)
    router = jnp.where(_iota((S, A), 0) == target[:, :A], 1.0, 0.0).astype(bf)

    def folded(rows, e):
        piece = rows[e * CAP : (e + 1) * CAP]
        return jnp.concatenate([piece[:, :W2], piece[:, W2:]], axis=0)

    packed = _dot(router, hidden[...])
    for e in range(H):
        snd_h[e] = folded(packed, e).astype(bf)
    pl.semaphore_wait(barrier, H - 1 + MP - 1)
    hs = [
        send(snd_h.at[other("hosts", d)], rcv_h.at[me], h_s.at[d], h_r.at[d], "hosts", d)
        for d in range(1, H)
    ]
    packed = _dot(router, base_q[...])
    for e in range(H):
        snd_q[e] = folded(packed, e).astype(bf)
    rcv_h[me] = snd_h[me]
    rcv_q[me] = snd_q[me]

    lane = _iota((8, 128), 1)
    half = jnp.where(lane < D // 2, lane, lane - D // 2).astype(f32)
    freq = jnp.exp(half * (-2.0 / D * math.log(ROPE_BASE)))
    counts = jnp.zeros((8, 128), jnp.int32)
    my_count = jnp.int32(0)
    for t in range(T):
        counts = jnp.where(sub8 == t, cnt[t], counts)
        my_count = jnp.where(apr[t] == me, cnt[t], my_count)
    counts = jnp.where(sub8 == T, my_count, counts)
    angle = (BLK * counts + SUF).astype(f32) * freq
    cos_t = jnp.cos(angle)
    sin_t = jnp.sin(angle)
    sin_t = jnp.where(lane < D // 2, -sin_t, sin_t)

    def turn(x, c, s):
        return x * c + pltpu.roll(x, D // 2, 1) * s

    locals_[0].wait()
    for copy in hs:
        copy.wait_recv()
    rows = rcv_h[...].reshape(H * 2 * CAP, W2)
    left = _dot(rows, a_v[0, :W2, :])
    right = _dot(rows, a_v[0, W2:, :])
    part[mme] = jnp.concatenate(
        [
            left[2 * CAP * e : 2 * CAP * e + CAP] + right[2 * CAP * e + CAP : 2 * CAP * (e + 1)]
            for e in range(H)
        ],
        axis=0,
    )
    ps = [
        send(part.at[mme], part.at[mme], p_s.at[d], p_r.at[d], "mp", d) for d in range(1, MP)
    ]
    bqs = [
        send(snd_q.at[other("hosts", d)], rcv_q.at[me], bq_s.at[d], bq_r.at[d], "hosts", d)
        for d in range(1, H)
    ]
    for copy in bqs:
        copy.wait_recv()
    bq = rcv_q[...].astype(f32)
    bq_half = [
        jnp.concatenate([bq[e, k * CAP : (k + 1) * CAP] for e in range(H)], axis=0)
        for k in range(2)
    ]
    locals_[1].wait()
    for copy in ps:
        copy.wait_recv()
    ranks = part[0]
    for m in range(1, MP):
        ranks = ranks + part[m]
    ranks = ranks.astype(bf).astype(f32)
    rank_q = ranks[:, :ADAPTER_RANK].astype(bf)
    rank_v = pltpu.roll(ranks, ADAPTER_RANK, 1)[:, :ADAPTER_RANK].astype(bf)
    qs = []
    for c in range(NCH):
        cols = slice(c * CW, (c + 1) * CW)
        delta = (_dot(rank_q, b_v[0, 0, :, cols]) * ADAPTER_SCALE).astype(bf).astype(f32)
        k, off = (c * CW) // W2, (c * CW) % W2
        raw = bq_half[k][:, off : off + CW] + delta
        for h in range(CW // D):
            queries[c][me, :, h * D : (h + 1) * D] = turn(
                raw[:, h * D : (h + 1) * D], cos_t[T : T + 1], sin_t[T : T + 1]
            ).astype(bf)
        view = queries[c].at[me]
        qs.append(
            [send(view, view, q_s.at[c, d], q_r.at[c, d], "hosts", d) for d in range(1, H)]
        )
    delta = _dot(rank_v, b_v[0, 1]) * ADAPTER_SCALE
    for e in range(H):
        snd_v[e] = folded(delta, e).astype(bf)
    rcv_v[me] = snd_v[me]

    sub128 = _iota((128, 128), 0)
    both = jnp.where(sub128 == 0, th[0:1].astype(f32), jnp.where(sub128 == 1, rank_f, 0.0))
    turned = both.T[:A].astype(jnp.int32)
    th_c, rank_c = turned[:, 0:1], turned[:, 1:2]
    lane_a = _iota((A, 128), 1)
    live_c = _iota((A, 1), 0) < n_live
    owner_c = jnp.full((A, 1), -1, jnp.int32)
    cos_a = jnp.zeros((A, 128), f32)
    sin_a = jnp.zeros((A, 128), f32)
    blocks_c = [jnp.full((A, 1), -1, jnp.int32) for _ in range(PB)]
    for t in range(T):
        here = th_c == t
        owner_c = jnp.where(here, apr[t], owner_c)
        cos_a = jnp.where(here, cos_t[t : t + 1], cos_a)
        sin_a = jnp.where(here, sin_t[t : t + 1], sin_a)
        for j in range(PB):
            blocks_c[j] = jnp.where(here, jnp.where(j < cnt[t], ppr[t, j], -1), blocks_c[j])
    owner_c = jnp.where(live_c, owner_c, -1)
    slot_ok = jnp.where(rank_c == (lane_a & (CAP - 1)), 1, 0)
    group = lane_a >> shift
    used = jnp.zeros((A, 128), jnp.int32)
    for j in range(PB):
        used = used + jnp.where(blocks_c[j] == group, 1, 0)
    used = jnp.where(live_c, used * slot_ok, 0) > 0
    fetch = jnp.where(owner_c * H + me == group, slot_ok, 0).astype(f32).astype(bf)
    unpack = jnp.where(
        owner_c * CAP + rank_c == _iota((A, S), 1), jnp.where(owner_c >= 0, 1.0, 0.0), 0.0
    ).astype(bf)
    keys = []
    locals_[5].wait()
    for h in range(HEADS):
        cols = slice(h * D, (h + 1) * D)
        key = turn(base_k[:, cols].astype(f32), cos_a, sin_a).astype(bf).astype(f32)
        keys.append(key)
        key_out[:, cols] = jnp.where(live_c, key, 0.0).astype(bf)

    whose = []
    for b in range(L):
        index = jnp.int32(0)
        for t in range(T):
            for j in range(PB):
                index = jnp.where(ppr[t, j] == me * L + b, apr[t], index)
        whose.append(index)
    scale = D ** (-0.5)
    locals_[2].wait()
    lane128 = _iota((128, 128), 1)
    lse_all = jnp.zeros((128, 128), f32)
    ms = []
    for c in range(NCH):
        for copy in qs[c]:
            copy.wait_recv()
        for h in range(c * CW // D, (c + 1) * CW // D):
            cols = slice(h * D, (h + 1) * D)
            within = slice(h * D - c * CW, (h + 1) * D - c * CW)
            scores = jnp.concatenate(
                [_dot_t(queries[c][whose[b], :, within], kv_v[b, 0, :, cols]) for b in range(L)], axis=0
            ) * scale
            top = jnp.max(scores, axis=1, keepdims=True)
            weights = jnp.exp(scores - top)
            total = jnp.sum(weights, axis=1, keepdims=True)
            weights = weights.astype(bf)
            mixed = jnp.concatenate(
                [_dot(weights[b * S : (b + 1) * S], kv_v[b, 1, :, cols]) for b in range(L)], axis=0
            ) * (1.0 / total)
            lse_all = jnp.where(lane128 == h, top + jnp.log(total), lse_all)
            for e in range(H):
                snd_m[e, :, cols] = jnp.concatenate(
                    [mixed[b * S + e * CAP : b * S + (e + 1) * CAP] for b in range(L)], axis=0
                ).astype(bf)
        if c == NCH - 1:
            ordered = jnp.concatenate(
                [
                    lse_all[b * S + e * CAP : b * S + (e + 1) * CAP]
                    for e in range(H)
                    for b in range(L)
                ],
                axis=0,
            )
            lse_t = ordered.T[:HEADS]
            rcv_l[me] = lse_t
            for d in range(1, H):
                snd_l[d] = pltpu.roll(lse_t, (128 - L * CAP * d) % 128, 1)
            ls = [
                send(snd_l.at[d], rcv_l.at[me], l_s.at[d], l_r.at[d], "hosts", d)
                for d in range(1, H)
            ]
        span = pl.ds(c * CW, CW)
        ms.append(
            [
                send(
                    snd_m.at[other("hosts", d), :, span], rcv_m.at[me, :, span],
                    m_s.at[c, d], m_r.at[c, d], "hosts", d,
                )
                for d in range(1, H)
            ]
        )
        if c == 0:
            vs = [
                send(snd_v.at[other("hosts", d)], rcv_v.at[me], v_s.at[d], v_r.at[d], "hosts", d)
                for d in range(1, H)
            ]
    rcv_m[me] = snd_m[me]

    locals_[3].wait()
    locals_[6].wait()
    for copy in vs:
        copy.wait_recv()
    dv = rcv_v[...].astype(f32)
    dv_att = [
        _dot(
            unpack,
            jnp.concatenate([dv[p, k * CAP : (k + 1) * CAP] for p in range(H)], axis=0).astype(bf),
        )
        for k in range(2)
    ]
    N = gen_v.shape[0]
    lane_n, sub_n = _iota((A, N), 1), _iota((A, N), 0)
    mine = ((lane_n >> (SUF.bit_length())) == sub_n) & ((lane_n & (2 * SUF - 1)) < SUF)
    own_top, own_total = [], []
    for h in range(HEADS):
        cols = slice(h * D, (h + 1) * D)
        k, off = (h * D) // W2, (h * D) % W2
        value = (base_v[:, cols].astype(f32) + dv_att[k][:, off : off + D]).astype(bf).astype(f32)
        val_out[:, cols] = jnp.where(live_c, value, 0.0).astype(bf)
        c, start = (h * D) // CW, (h * D) % CW
        query = _dot(fetch, queries[c][:, :, start : start + D].reshape(H * S, D))
        scores = _dot_t(query.astype(bf), gen_v[:, cols]) * scale
        scores = jnp.where(mine, scores, NEG_FILL)
        self_score = jnp.sum(query * keys[h], axis=1, keepdims=True) * scale
        top = jnp.maximum(jnp.max(scores, axis=1, keepdims=True), self_score)
        weights = jnp.where(mine, jnp.exp(scores - top), 0.0)
        self_weight = jnp.exp(self_score - top)
        own_top.append(top)
        own_total.append(jnp.sum(weights, axis=1, keepdims=True) + self_weight)
        own_mix[:, cols] = (
            _dot(pltpu.roll(weights, SUF, 1).astype(bf), gen_v[:, cols])
            + self_weight.astype(bf).astype(f32) * value
        )

    for copy in ls:
        copy.wait_recv()
    lse = jnp.zeros((HEADS, 128), f32)
    lane_h = _iota((HEADS, 128), 1)
    for g in range(H):
        lse = jnp.where((lane_h >= g * L * CAP) & (lane_h < (g + 1) * L * CAP), rcv_l[g], lse)
    for c in range(NCH):
        for copy in ms[c]:
            copy.wait_recv()
        for h in range(c * CW // D, (c + 1) * CW // D):
            cols = slice(h * D, (h + 1) * D)
            logs = jnp.where(used, lse[h : h + 1], NEG_FILL)
            top = jnp.maximum(jnp.max(logs, axis=1, keepdims=True), own_top[h])
            factor = jnp.where(used, jnp.exp(logs - top), 0.0)
            own_factor = jnp.exp(own_top[h] - top)
            inverse = 1.0 / (jnp.sum(factor, axis=1, keepdims=True) + own_total[h] * own_factor)
            result = _dot(
                (factor * inverse).astype(bf), rcv_m[:, :, cols].reshape(H * L * CAP, D)
            ) + own_mix[:, cols] * (own_factor * inverse)
            out[:, cols] = jnp.where(live_c, result, 0.0).astype(bf)
    for copies in [hs, bqs, ps, vs, ls] + qs + ms:
        for copy in copies:
            copy.wait_send()


def write_kernel(*refs):
    sems = refs[6]
    copies = [pltpu.make_async_copy(refs[i], refs[3 + i], sems.at[i]) for i in range(3)]
    for copy in copies:
        copy.start()
    for copy in copies:
        copy.wait()


def fused_body(
    hidden, base_q, base_k, base_v, a_in, b_out, cache, generated, thm, live, apr, ppr, cnt
):
    H, MP = lax.axis_size("hosts"), lax.axis_size("mp")
    A, W = hidden.shape
    CAP = A // H
    L, SUF = cache.shape[0], generated.shape[2]
    HEADS = W // HEAD_SIZE
    S = H * CAP
    NCH = 2
    bf, f32 = jnp.bfloat16, jnp.float32
    N = generated.shape[0] * 2 * SUF
    sizes = (H, MP, A, CAP, L, apr.shape[0], ppr.shape[1], HEADS, SUF, NCH)
    smem = pl.BlockSpec(memory_space=pltpu.SMEM)
    vmem = pl.BlockSpec(memory_space=pltpu.VMEM)
    hbm = pl.BlockSpec(memory_space=pl.ANY)
    fold = (H, 2 * CAP, W // 2)
    sem = lambda *shape: pltpu.SemaphoreType.DMA(shape)
    results = pl.pallas_call(
        functools.partial(fused_kernel, sizes),
        out_shape=[pltpu.VMEM((A, W), bf)] * 3,
        in_specs=[smem] * 4 + [vmem] * 2 + [hbm] * 7,
        out_specs=[vmem] * 3,
        scratch_shapes=[
            pltpu.SMEM(live.shape, jnp.int32),
            pltpu.VMEM((A, W), bf),
            pltpu.VMEM((A, W), bf),
            pltpu.VMEM(a_in.shape, bf),
            pltpu.VMEM(b_out.shape, bf),
            pltpu.VMEM(cache.shape, bf),
            pltpu.VMEM((N, W), bf),
            pltpu.VMEM(fold, bf),
            pltpu.VMEM(fold, bf),
            pltpu.VMEM(fold, bf),
            pltpu.VMEM(fold, bf),
            pltpu.VMEM((MP, S, 128), f32),
            pltpu.VMEM(fold, bf),
            pltpu.VMEM(fold, bf),
            pltpu.VMEM((H, L * CAP, W), bf),
            pltpu.VMEM((H, L * CAP, W), bf),
            pltpu.VMEM((H, HEADS, 128), f32),
            pltpu.VMEM((H, HEADS, 128), f32),
            pltpu.VMEM((A, W), f32),
            sem(7), sem(H), sem(H), sem(H), sem(H), sem(MP), sem(MP),
            sem(NCH, H), sem(NCH, H), sem(H), sem(H), sem(NCH, H), sem(NCH, H), sem(H), sem(H),
        ]
        + [pltpu.VMEM((H, S, W // NCH), bf)] * NCH,
        compiler_params=pltpu.CompilerParams(
            collective_id=0, has_side_effects=True, vmem_limit_bytes=60 * 1024 * 1024
        ),
        cost_estimate=pl.CostEstimate(
            flops=2 * 10**8, bytes_accessed=4 * 10**6, transcendentals=10**6
        ),
    )(
        thm, apr, ppr, cnt, hidden, base_q, live, base_k, base_v, a_in, b_out, cache,
        generated.reshape(N, W),
    )
    return pl.pallas_call(
        write_kernel,
        out_shape=[jax.ShapeDtypeStruct((A, W), bf)] * 3,
        in_specs=[vmem] * 3,
        out_specs=[hbm] * 3,
        scratch_shapes=[sem(3)],
        compiler_params=pltpu.CompilerParams(vmem_limit_bytes=2**20),
    )(*results)


def step(hidden, base_q, base_k, base_v, a_in, b_out, cache, generated, thm, live, apr, ppr, cnt):
    H = lax.axis_size("hosts")
    A, W = hidden.shape
    capacity = A // H
    fits = (
        capacity == 8
        and H <= 8
        and A <= 128
        and a_in.shape[0] == 1
        and A * cache.shape[0] == 128
        and cache.shape[2] == 128
        and H * A == 128
        and W == 8 * HEAD_SIZE
        and generated.shape[2] == 8
        and apr.shape[0] < 8
    )
    run = fused_body if fits else body
    return run(hidden, base_q, base_k, base_v, a_in, b_out, cache, generated, thm, live, apr, ppr, cnt)


def solution(mesh):
    placed = (
        P(("groups", "hosts"), "mp"),
        P(("groups", "hosts"), "mp"),
        P(("groups", "hosts"), "mp"),
        P(("groups", "hosts"), "mp"),
        P(("groups", "hosts"), "mp", None),
        P(("groups", "hosts"), None, None, "mp"),
        P(("groups", "hosts"), None, None, "mp"),
        P(("groups", "hosts"), None, None, "mp"),
        P(("groups", "hosts")),
        P(("groups", "hosts")),
        P("groups"),
        P("groups", None),
        P("groups"),
    )
    return jax.shard_map(
        step,
        mesh=mesh,
        in_specs=placed,
        out_specs=(
            P(("groups", "hosts"), "mp"),
            P(("groups", "hosts"), "mp"),
            P(("groups", "hosts"), "mp"),
        ),
        check_vma=False,
    )
```

```python
import functools
import math

import jax
import jax.numpy as jnp
from jax import lax
from jax.experimental import pallas as pl
from jax.experimental.pallas import tpu as pltpu
from jax.sharding import PartitionSpec as P

HEAD_SIZE = 128
ADAPTER_RANK = 64
BLK = 128
PBLK = 4


ADAPTER_SCALE = 0.5
ROPE_BASE = 10000.0
NEG_FILL = -1e30
MESH = pl.DeviceIdType.MESH


def rotate(values, position):
    shaped = values.reshape(values.shape[:-1] + (-1, HEAD_SIZE))
    halfway = HEAD_SIZE // 2
    frequency = ROPE_BASE ** (-(jnp.arange(halfway, dtype=jnp.float32) * (2.0 / HEAD_SIZE)))
    angles = position.astype(jnp.float32)[..., None] * frequency
    cosine = jnp.cos(angles)[..., None, :]
    sine_part = jnp.sin(angles)[..., None, :]
    first_half = shaped[..., :halfway]
    second = shaped[..., halfway:]
    turned = jnp.concatenate(
        [first_half * cosine - second * sine_part, second * cosine + first_half * sine_part],
        axis=-1,
    )
    return turned.reshape(values.shape)


def lookup_table(source_table, wanted):
    matches = wanted[:, None] == jnp.arange(source_table.shape[0], dtype=jnp.int32)[None, :]
    if source_table.ndim == 1:
        return jnp.sum(jnp.where(matches, source_table[None, :], 0), axis=1)
    return jnp.sum(jnp.where(matches[:, :, None], source_table[None, :, :], 0), axis=1)


def route_matrix(destination, validity, capacity, host_total):
    ordinal = jnp.arange(destination.shape[0], dtype=jnp.int32)
    earlier = (
        (destination[:, None] == destination[None, :])
        & validity[None, :]
        & (ordinal[None, :] < ordinal[:, None])
    )
    ranking = jnp.sum(earlier.astype(jnp.int32), axis=1)
    target = destination * capacity + ranking
    places = jnp.arange(host_total * capacity, dtype=jnp.int32)
    return ((places[:, None] == target[None, :]) & validity[None, :]).astype(jnp.bfloat16)


def pack_rows(router, payload):
    return jnp.dot(router, payload, preferred_element_type=jnp.float32).astype(jnp.bfloat16)


def attend_local(queries, chosen, statement_prefix_cache):
    head_count = queries.shape[-1] // HEAD_SIZE
    blocks = statement_prefix_cache.shape[0]
    block_keys = statement_prefix_cache[:, 0].reshape(
        blocks, statement_prefix_cache.shape[2], head_count, HEAD_SIZE
    )
    block_values = statement_prefix_cache[:, 1].reshape(
        blocks, statement_prefix_cache.shape[2], head_count, HEAD_SIZE
    )
    shaped = queries.reshape(queries.shape[:-1] + (head_count, HEAD_SIZE))
    scores = jnp.einsum(
        "nchd,bthd->ncbht", shaped, block_keys, preferred_element_type=jnp.float32
    ) * HEAD_SIZE ** (-0.5)
    chosen_mask = (chosen > 0)[:, :, :, None, None]
    masked = jnp.where(chosen_mask, scores, NEG_FILL)
    top_score = jnp.max(masked, axis=(2, 4))
    weights = jnp.where(chosen_mask, jnp.exp(masked - top_score[:, :, None, :, None]), 0.0)
    totals = jnp.sum(weights, axis=(2, 4))
    mixed_rows = jnp.einsum(
        "ncbht,bthd->nchd",
        weights.astype(jnp.bfloat16),
        block_values,
        preferred_element_type=jnp.float32,
    )
    return (mixed_rows.reshape(queries.shape), top_score, totals)


def body(
    hidden,
    base_query_projection,
    base_key_projection,
    base_value_projection,
    adapter_input_factors,
    adapter_output_factors,
    statement_prefix_cache,
    generated_token_cache,
    attempt_theorem_index,
    host_live_count,
    adapter_pool_row,
    prefix_pool_row,
    prefix_block_count,
):
    host_total = lax.axis_size("hosts")
    attempts = hidden.shape[0]
    capacity = max(1, attempts // host_total)
    owner_held_rows = adapter_input_factors.shape[0]
    local_blocks = statement_prefix_cache.shape[0]
    row_width = base_query_projection.shape[1]
    head_count = row_width // HEAD_SIZE
    ordinal = jnp.arange(attempts, dtype=jnp.int32)
    living = ordinal < host_live_count[0]
    adapter_rows = lookup_table(adapter_pool_row, attempt_theorem_index)
    block_rows = lookup_table(prefix_pool_row, attempt_theorem_index)
    block_counts = lookup_table(prefix_block_count, attempt_theorem_index)
    position = BLK * block_counts + generated_token_cache.shape[2]
    adapter_router = route_matrix(adapter_rows // owner_held_rows, living, capacity, host_total)
    adapter_pick = (
        adapter_rows[:, None] % owner_held_rows
        == jnp.arange(owner_held_rows, dtype=jnp.int32)[None, :]
    ).astype(jnp.bfloat16)
    sent_hidden = pack_rows(adapter_router, hidden).reshape(host_total, capacity, hidden.shape[1])
    sent_pick = pack_rows(adapter_router, adapter_pick).reshape(
        host_total, capacity, owner_held_rows
    )
    incoming_rows = lax.all_to_all(sent_hidden, "hosts", split_axis=0, concat_axis=0, tiled=True)
    pick_in = lax.all_to_all(sent_pick, "hosts", split_axis=0, concat_axis=0, tiled=True)
    projected_rows = jnp.einsum(
        "xjp,epk->xjek", incoming_rows, adapter_input_factors, preferred_element_type=jnp.float32
    )
    partial_rank = jnp.sum(projected_rows * pick_in.astype(jnp.float32)[..., None], axis=2)
    rank_rows = lax.psum(partial_rank, "mp").astype(jnp.bfloat16)
    spread_rows = rank_rows[:, :, None, :] * pick_in[..., None]
    query_correction = jnp.einsum(
        "exqw,qwf->exf",
        spread_rows[..., :ADAPTER_RANK],
        adapter_output_factors[:, 0],
        preferred_element_type=jnp.float32,
    )
    value_correction = jnp.einsum(
        "exqw,qwf->exf",
        spread_rows[..., ADAPTER_RANK:],
        adapter_output_factors[:, 1],
        preferred_element_type=jnp.float32,
    )
    adapter_corrections = (
        jnp.concatenate([query_correction, value_correction], axis=-1) * ADAPTER_SCALE
    ).astype(jnp.bfloat16)
    returned = lax.all_to_all(adapter_corrections, "hosts", split_axis=0, concat_axis=0, tiled=True)
    adapter_corrections = jnp.dot(
        adapter_router.T,
        returned.reshape(host_total * capacity, 2 * row_width),
        preferred_element_type=jnp.float32,
    )
    query_rows = rotate(
        base_query_projection.astype(jnp.float32) + adapter_corrections[:, :row_width], position
    ).astype(jnp.bfloat16)
    value_rows = (
        base_value_projection.astype(jnp.float32) + adapter_corrections[:, row_width:]
    ).astype(jnp.bfloat16)
    key_rows = rotate(base_key_projection.astype(jnp.float32), position).astype(jnp.bfloat16)
    requests = []
    for block_index in range(PBLK):
        wanted = living & (block_index < block_counts)
        holder = block_rows[:, block_index]
        router = route_matrix(holder // local_blocks, wanted, capacity, host_total)
        block_pick = (
            holder[:, None] % local_blocks == jnp.arange(local_blocks, dtype=jnp.int32)[None, :]
        ).astype(jnp.bfloat16)
        sent_queries = pack_rows(router, query_rows).reshape(host_total, capacity, row_width)
        sent_blocks = pack_rows(router, block_pick).reshape(host_total, capacity, local_blocks)
        requests.append((router, wanted, sent_queries, sent_blocks))
    partials = []
    for request in requests:
        answer_mixed_rows, answer_top_score, answer_totals = attend_local(
            lax.all_to_all(request[2], "hosts", split_axis=0, concat_axis=0, tiled=True),
            lax.all_to_all(request[3], "hosts", split_axis=0, concat_axis=0, tiled=True),
            statement_prefix_cache,
        )
        partials.append(
            (
                lax.all_to_all(answer_mixed_rows, "hosts", split_axis=0, concat_axis=0, tiled=True),
                lax.all_to_all(answer_top_score, "hosts", split_axis=0, concat_axis=0, tiled=True),
                lax.all_to_all(answer_totals, "hosts", split_axis=0, concat_axis=0, tiled=True),
            )
        )
    entries = []
    for block_index in range(PBLK):
        router, wanted = (requests[block_index][0], requests[block_index][1])
        mixed_rows, top_score, totals = partials[block_index]
        back_router = router.T.astype(jnp.float32)
        flat_mixed = jnp.dot(
            back_router,
            mixed_rows.reshape(host_total * capacity, row_width),
            precision=lax.Precision.HIGHEST,
        )
        flat_top = jnp.dot(
            back_router,
            top_score.reshape(host_total * capacity, head_count),
            precision=lax.Precision.HIGHEST,
        )
        flat_totals = jnp.dot(
            back_router,
            totals.reshape(host_total * capacity, head_count),
            precision=lax.Precision.HIGHEST,
        )
        flat_top = jnp.where(wanted[:, None], flat_top, NEG_FILL)
        entries.append((flat_mixed, flat_top, flat_totals))
    shaped_query = query_rows.reshape(attempts, head_count, HEAD_SIZE)
    own_keys = jnp.concatenate([generated_token_cache[:, 0], key_rows[:, None, :]], axis=1).reshape(
        attempts, -1, head_count, HEAD_SIZE
    )
    own_values = jnp.concatenate(
        [generated_token_cache[:, 1], value_rows[:, None, :]], axis=1
    ).reshape(attempts, -1, head_count, HEAD_SIZE)
    own_scores = jnp.einsum(
        "ahd,athd->aht", shaped_query, own_keys, preferred_element_type=jnp.float32
    ) * HEAD_SIZE ** (-0.5)
    own_top = jnp.max(own_scores, axis=2)
    own_weights = jnp.exp(own_scores - own_top[..., None])
    own_totals = jnp.sum(own_weights, axis=2)
    own_mixed = jnp.einsum(
        "aht,athd->ahd",
        own_weights.astype(jnp.bfloat16),
        own_values,
        preferred_element_type=jnp.float32,
    )
    overall = own_top
    for flat_mixed, flat_top, flat_totals in entries:
        overall = jnp.maximum(overall, flat_top)
    own_factor = jnp.exp(own_top - overall)
    numerator = own_mixed * own_factor[..., None]
    denominator = own_totals * own_factor
    for flat_mixed, flat_top, flat_totals in entries:
        factor = jnp.exp(flat_top - overall)
        numerator = (
            numerator + flat_mixed.reshape(attempts, head_count, HEAD_SIZE) * factor[..., None]
        )
        denominator = denominator + flat_totals * factor
    attended = (numerator / denominator[..., None]).reshape(attempts, row_width)
    live_rows = living[:, None]
    return (
        jnp.where(live_rows, attended, 0.0).astype(jnp.bfloat16),
        jnp.where(live_rows, key_rows, 0.0),
        jnp.where(live_rows, value_rows, 0.0),
    )


def _iota(shape, dim):
    return lax.broadcasted_iota(jnp.int32, shape, dim)


def _dot(a, b):
    return jnp.dot(a, b, preferred_element_type=jnp.float32)


def _dot_t(a, b):
    return lax.dot_general(a, b, (((1,), (1,)), ((), ())), preferred_element_type=jnp.float32)


def fused_kernel(
    sizes,
    thm, apr, ppr, cnt,
    hidden, base_q, live_hbm, k_hbm, val_hbm, a_hbm, b_hbm, kv_hbm, gen_hbm,
    out, key_out, val_out,
    live, base_k, base_v, a_v, b_v, kv_v, gen_v,
    snd_h, rcv_h, snd_q, rcv_q, part, snd_v, rcv_v, snd_m, rcv_m, snd_l, rcv_l, own_mix,
    local_sem, h_s, h_r, bq_s, bq_r, p_s, p_r, q_s, q_r, v_s, v_r, m_s, m_r, l_s, l_r,
    *queries,
):
    H, MP, A, CAP, L, T, PB, HEADS, SUF, NCH = sizes
    f32, bf = jnp.float32, jnp.bfloat16
    D = HEAD_SIZE
    W = HEADS * D
    W2 = W // 2
    S = H * CAP
    CW = W // NCH
    shift = CAP.bit_length() - 1
    me = lax.axis_index("hosts")
    mme = lax.axis_index("mp")

    def other(axis, d):
        return lax.rem((me if axis == "hosts" else mme) + d, H if axis == "hosts" else MP)

    locals_ = [
        pltpu.make_async_copy(src, dst, local_sem.at[i])
        for i, (src, dst) in enumerate(
            [
                (a_hbm, a_v), (b_hbm, b_v), (kv_hbm, kv_v), (gen_hbm, gen_v),
                (live_hbm, live), (k_hbm, base_k), (val_hbm, base_v),
            ]
        )
    ]
    for i in (4, 0, 1, 2, 5, 6, 3):
        locals_[i].start()

    barrier = pltpu.get_barrier_semaphore()
    for d in range(1, H):
        pl.semaphore_signal(barrier, inc=1, device_id={"hosts": other("hosts", d)}, device_id_type=MESH)
    for d in range(1, MP):
        pl.semaphore_signal(barrier, inc=1, device_id={"mp": other("mp", d)}, device_id_type=MESH)

    def send(src, dst, s, r, axis, d):
        copy = pltpu.make_async_remote_copy(
            src_ref=src, dst_ref=dst, send_sem=s, recv_sem=r,
            device_id={axis: other(axis, d)}, device_id_type=MESH,
        )
        copy.start()
        return copy

    lane8, sub8 = _iota((8, 128), 1), _iota((8, 128), 0)
    th = jnp.full((8, 128), -1, jnp.int32)
    for a in range(A):
        th = jnp.where(lane8 == a, thm[a], th)
    owner = jnp.full((8, 128), -1, jnp.int32)
    for t in range(T):
        owner = jnp.where(th == t, apr[t], owner)
    locals_[4].wait()
    n_live = live[0]
    owner = jnp.where(lane8 < n_live, owner, -1)
    member = jnp.where(owner == sub8, 1.0, 0.0).astype(f32)
    before = jnp.where(_iota((128, 128), 0) < _iota((128, 128), 1), 1.0, 0.0).astype(bf)
    rank_f = jnp.sum(member * _dot(member.astype(bf), before), axis=0, keepdims=True)
    rank_row = rank_f.astype(jnp.int32)
    target = jnp.where(owner[0:1] >= 0, owner[0:1] * CAP + rank_row, -1)
    router = jnp.where(_iota((S, A), 0) == target[:, :A], 1.0, 0.0).astype(bf)

    def folded(rows, e):
        piece = rows[e * CAP : (e + 1) * CAP]
        return jnp.concatenate([piece[:, :W2], piece[:, W2:]], axis=0)

    packed = _dot(router, hidden[...])
    for e in range(H):
        snd_h[e] = folded(packed, e).astype(bf)
    pl.semaphore_wait(barrier, H - 1 + MP - 1)
    hs = [
        send(snd_h.at[other("hosts", d)], rcv_h.at[me], h_s.at[d], h_r.at[d], "hosts", d)
        for d in range(1, H)
    ]
    packed = _dot(router, base_q[...])
    for e in range(H):
        snd_q[e] = folded(packed, e).astype(bf)
    bqs = [
        send(snd_q.at[other("hosts", d)], rcv_q.at[me], bq_s.at[d], bq_r.at[d], "hosts", d)
        for d in range(1, H)
    ]
    rcv_h[me] = snd_h[me]
    rcv_q[me] = snd_q[me]

    lane = _iota((8, 128), 1)
    half = jnp.where(lane < D // 2, lane, lane - D // 2).astype(f32)
    freq = jnp.exp(half * (-2.0 / D * math.log(ROPE_BASE)))
    counts = jnp.zeros((8, 128), jnp.int32)
    my_count = jnp.int32(0)
    for t in range(T):
        counts = jnp.where(sub8 == t, cnt[t], counts)
        my_count = jnp.where(apr[t] == me, cnt[t], my_count)
    counts = jnp.where(sub8 == T, my_count, counts)
    angle = (BLK * counts + SUF).astype(f32) * freq
    cos_t = jnp.cos(angle)
    sin_t = jnp.sin(angle)
    sin_t = jnp.where(lane < D // 2, -sin_t, sin_t)

    def turn(x, c, s):
        return x * c + pltpu.roll(x, D // 2, 1) * s

    locals_[0].wait()
    for copy in hs:
        copy.wait_recv()
    rows = rcv_h[...].reshape(H * 2 * CAP, W2)
    left = _dot(rows, a_v[0, :W2, :])
    right = _dot(rows, a_v[0, W2:, :])
    part[mme] = jnp.concatenate(
        [
            left[2 * CAP * e : 2 * CAP * e + CAP] + right[2 * CAP * e + CAP : 2 * CAP * (e + 1)]
            for e in range(H)
        ],
        axis=0,
    )
    ps = [
        send(part.at[mme], part.at[mme], p_s.at[d], p_r.at[d], "mp", d) for d in range(1, MP)
    ]
    for copy in bqs:
        copy.wait_recv()
    bq = rcv_q[...].astype(f32)
    bq_half = [
        jnp.concatenate([bq[e, k * CAP : (k + 1) * CAP] for e in range(H)], axis=0)
        for k in range(2)
    ]
    locals_[1].wait()
    for copy in ps:
        copy.wait_recv()
    ranks = part[0]
    for m in range(1, MP):
        ranks = ranks + part[m]
    ranks = ranks.astype(bf).astype(f32)
    rank_q = ranks[:, :ADAPTER_RANK].astype(bf)
    rank_v = pltpu.roll(ranks, ADAPTER_RANK, 1)[:, :ADAPTER_RANK].astype(bf)
    qs = []
    for c in range(NCH):
        cols = slice(c * CW, (c + 1) * CW)
        delta = (_dot(rank_q, b_v[0, 0, :, cols]) * ADAPTER_SCALE).astype(bf).astype(f32)
        k, off = (c * CW) // W2, (c * CW) % W2
        raw = bq_half[k][:, off : off + CW] + delta
        for h in range(CW // D):
            queries[c][me, :, h * D : (h + 1) * D] = turn(
                raw[:, h * D : (h + 1) * D], cos_t[T : T + 1], sin_t[T : T + 1]
            ).astype(bf)
        view = queries[c].at[me]
        qs.append(
            [send(view, view, q_s.at[c, d], q_r.at[c, d], "hosts", d) for d in range(1, H)]
        )
    delta = _dot(rank_v, b_v[0, 1]) * ADAPTER_SCALE
    for e in range(H):
        snd_v[e] = folded(delta, e).astype(bf)
    vs = [
        send(snd_v.at[other("hosts", d)], rcv_v.at[me], v_s.at[d], v_r.at[d], "hosts", d)
        for d in range(1, H)
    ]
    rcv_v[me] = snd_v[me]

    sub128 = _iota((128, 128), 0)
    both = jnp.where(sub128 == 0, th[0:1].astype(f32), jnp.where(sub128 == 1, rank_f, 0.0))
    turned = both.T[:A].astype(jnp.int32)
    th_c, rank_c = turned[:, 0:1], turned[:, 1:2]
    lane_a = _iota((A, 128), 1)
    live_c = _iota((A, 1), 0) < n_live
    owner_c = jnp.full((A, 1), -1, jnp.int32)
    cos_a = jnp.zeros((A, 128), f32)
    sin_a = jnp.zeros((A, 128), f32)
    blocks_c = [jnp.full((A, 1), -1, jnp.int32) for _ in range(PB)]
    for t in range(T):
        here = th_c == t
        owner_c = jnp.where(here, apr[t], owner_c)
        cos_a = jnp.where(here, cos_t[t : t + 1], cos_a)
        sin_a = jnp.where(here, sin_t[t : t + 1], sin_a)
        for j in range(PB):
            blocks_c[j] = jnp.where(here, jnp.where(j < cnt[t], ppr[t, j], -1), blocks_c[j])
    owner_c = jnp.where(live_c, owner_c, -1)
    slot_ok = jnp.where(rank_c == (lane_a & (CAP - 1)), 1, 0)
    group = lane_a >> shift
    used = jnp.zeros((A, 128), jnp.int32)
    for j in range(PB):
        used = used + jnp.where(blocks_c[j] == group, 1, 0)
    used = jnp.where(live_c, used * slot_ok, 0) > 0
    fetch = jnp.where(owner_c * H + me == group, slot_ok, 0).astype(f32).astype(bf)
    unpack = jnp.where(
        owner_c * CAP + rank_c == _iota((A, S), 1), jnp.where(owner_c >= 0, 1.0, 0.0), 0.0
    ).astype(bf)
    keys = []
    locals_[5].wait()
    for h in range(HEADS):
        cols = slice(h * D, (h + 1) * D)
        key = turn(base_k[:, cols].astype(f32), cos_a, sin_a).astype(bf).astype(f32)
        keys.append(key)
        key_out[:, cols] = jnp.where(live_c, key, 0.0).astype(bf)

    whose = []
    for b in range(L):
        index = jnp.int32(0)
        for t in range(T):
            for j in range(PB):
                index = jnp.where(ppr[t, j] == me * L + b, apr[t], index)
        whose.append(index)
    scale = D ** (-0.5)
    locals_[2].wait()
    lane128 = _iota((128, 128), 1)
    lse_all = jnp.zeros((128, 128), f32)
    ms = []
    for c in range(NCH):
        for copy in qs[c]:
            copy.wait_recv()
        for h in range(c * CW // D, (c + 1) * CW // D):
            cols = slice(h * D, (h + 1) * D)
            within = slice(h * D - c * CW, (h + 1) * D - c * CW)
            scores = jnp.concatenate(
                [_dot_t(queries[c][whose[b], :, within], kv_v[b, 0, :, cols]) for b in range(L)], axis=0
            ) * scale
            top = jnp.max(scores, axis=1, keepdims=True)
            weights = jnp.exp(scores - top)
            total = jnp.sum(weights, axis=1, keepdims=True)
            weights = weights.astype(bf)
            mixed = jnp.concatenate(
                [_dot(weights[b * S : (b + 1) * S], kv_v[b, 1, :, cols]) for b in range(L)], axis=0
            ) * (1.0 / total)
            lse_all = jnp.where(lane128 == h, top + jnp.log(total), lse_all)
            for e in range(H):
                snd_m[e, :, cols] = jnp.concatenate(
                    [mixed[b * S + e * CAP : b * S + (e + 1) * CAP] for b in range(L)], axis=0
                ).astype(bf)
        if c == NCH - 1:
            ordered = jnp.concatenate(
                [
                    lse_all[b * S + e * CAP : b * S + (e + 1) * CAP]
                    for e in range(H)
                    for b in range(L)
                ],
                axis=0,
            )
            lse_t = ordered.T[:HEADS]
            rcv_l[me] = lse_t
            for d in range(1, H):
                snd_l[d] = pltpu.roll(lse_t, (128 - L * CAP * d) % 128, 1)
            ls = [
                send(snd_l.at[d], rcv_l.at[me], l_s.at[d], l_r.at[d], "hosts", d)
                for d in range(1, H)
            ]
        span = pl.ds(c * CW, CW)
        ms.append(
            [
                send(
                    snd_m.at[other("hosts", d), :, span], rcv_m.at[me, :, span],
                    m_s.at[c, d], m_r.at[c, d], "hosts", d,
                )
                for d in range(1, H)
            ]
        )
    rcv_m[me] = snd_m[me]

    locals_[3].wait()
    N = gen_v.shape[0]
    lane_n, sub_n = _iota((A, N), 1), _iota((A, N), 0)
    mine = ((lane_n >> (SUF.bit_length())) == sub_n) & ((lane_n & (2 * SUF - 1)) < SUF)
    own_top, own_total, own_self = [], [], []
    for h in range(HEADS):
        cols = slice(h * D, (h + 1) * D)
        c, start = (h * D) // CW, (h * D) % CW
        query = _dot(fetch, queries[c][:, :, start : start + D].reshape(H * S, D))
        scores = _dot_t(query.astype(bf), gen_v[:, cols]) * scale
        scores = jnp.where(mine, scores, NEG_FILL)
        self_score = jnp.sum(query * keys[h], axis=1, keepdims=True) * scale
        top = jnp.maximum(jnp.max(scores, axis=1, keepdims=True), self_score)
        weights = jnp.where(mine, jnp.exp(scores - top), 0.0)
        self_weight = jnp.exp(self_score - top)
        own_top.append(top)
        own_total.append(jnp.sum(weights, axis=1, keepdims=True) + self_weight)
        own_mix[:, cols] = (
            _dot(pltpu.roll(weights, SUF, 1).astype(bf), gen_v[:, cols])
        )
        own_self.append(self_weight.astype(bf).astype(f32))

    locals_[6].wait()
    for copy in vs:
        copy.wait_recv()
    dv = rcv_v[...].astype(f32)
    dv_att = [
        _dot(
            unpack,
            jnp.concatenate([dv[p, k * CAP : (k + 1) * CAP] for p in range(H)], axis=0).astype(bf),
        )
        for k in range(2)
    ]
    for h in range(HEADS):
        cols = slice(h * D, (h + 1) * D)
        k, off = (h * D) // W2, (h * D) % W2
        value = (base_v[:, cols].astype(f32) + dv_att[k][:, off : off + D]).astype(bf).astype(f32)
        val_out[:, cols] = jnp.where(live_c, value, 0.0).astype(bf)
        own_mix[:, cols] += own_self[h] * value

    for copy in ls:
        copy.wait_recv()
    lse = jnp.zeros((HEADS, 128), f32)
    lane_h = _iota((HEADS, 128), 1)
    for g in range(H):
        lse = jnp.where((lane_h >= g * L * CAP) & (lane_h < (g + 1) * L * CAP), rcv_l[g], lse)
    for c in range(NCH):
        for copy in ms[c]:
            copy.wait_recv()
        for h in range(c * CW // D, (c + 1) * CW // D):
            cols = slice(h * D, (h + 1) * D)
            logs = jnp.where(used, lse[h : h + 1], NEG_FILL)
            top = jnp.maximum(jnp.max(logs, axis=1, keepdims=True), own_top[h])
            factor = jnp.where(used, jnp.exp(logs - top), 0.0)
            own_factor = jnp.exp(own_top[h] - top)
            inverse = 1.0 / (jnp.sum(factor, axis=1, keepdims=True) + own_total[h] * own_factor)
            result = _dot(
                (factor * inverse).astype(bf), rcv_m[:, :, cols].reshape(H * L * CAP, D)
            ) + own_mix[:, cols] * (own_factor * inverse)
            out[:, cols] = jnp.where(live_c, result, 0.0).astype(bf)
    for copies in [hs, bqs, ps, vs, ls] + qs + ms:
        for copy in copies:
            copy.wait_send()


def write_kernel(*refs):
    sems = refs[6]
    copies = [pltpu.make_async_copy(refs[i], refs[3 + i], sems.at[i]) for i in range(3)]
    for copy in copies:
        copy.start()
    for copy in copies:
        copy.wait()


def fused_body(
    hidden, base_q, base_k, base_v, a_in, b_out, cache, generated, thm, live, apr, ppr, cnt
):
    H, MP = lax.axis_size("hosts"), lax.axis_size("mp")
    A, W = hidden.shape
    CAP = A // H
    L, SUF = cache.shape[0], generated.shape[2]
    HEADS = W // HEAD_SIZE
    S = H * CAP
    NCH = 2
    bf, f32 = jnp.bfloat16, jnp.float32
    N = generated.shape[0] * 2 * SUF
    sizes = (H, MP, A, CAP, L, apr.shape[0], ppr.shape[1], HEADS, SUF, NCH)
    smem = pl.BlockSpec(memory_space=pltpu.SMEM)
    vmem = pl.BlockSpec(memory_space=pltpu.VMEM)
    hbm = pl.BlockSpec(memory_space=pl.ANY)
    fold = (H, 2 * CAP, W // 2)
    sem = lambda *shape: pltpu.SemaphoreType.DMA(shape)
    results = pl.pallas_call(
        functools.partial(fused_kernel, sizes),
        out_shape=[pltpu.VMEM((A, W), bf)] * 3,
        in_specs=[smem] * 4 + [vmem] * 2 + [hbm] * 7,
        out_specs=[vmem] * 3,
        scratch_shapes=[
            pltpu.SMEM(live.shape, jnp.int32),
            pltpu.VMEM((A, W), bf),
            pltpu.VMEM((A, W), bf),
            pltpu.VMEM(a_in.shape, bf),
            pltpu.VMEM(b_out.shape, bf),
            pltpu.VMEM(cache.shape, bf),
            pltpu.VMEM((N, W), bf),
            pltpu.VMEM(fold, bf),
            pltpu.VMEM(fold, bf),
            pltpu.VMEM(fold, bf),
            pltpu.VMEM(fold, bf),
            pltpu.VMEM((MP, S, 128), f32),
            pltpu.VMEM(fold, bf),
            pltpu.VMEM(fold, bf),
            pltpu.VMEM((H, L * CAP, W), bf),
            pltpu.VMEM((H, L * CAP, W), bf),
            pltpu.VMEM((H, HEADS, 128), f32),
            pltpu.VMEM((H, HEADS, 128), f32),
            pltpu.VMEM((A, W), f32),
            sem(7), sem(H), sem(H), sem(H), sem(H), sem(MP), sem(MP),
            sem(NCH, H), sem(NCH, H), sem(H), sem(H), sem(NCH, H), sem(NCH, H), sem(H), sem(H),
        ]
        + [pltpu.VMEM((H, S, W // NCH), bf)] * NCH,
        compiler_params=pltpu.CompilerParams(
            collective_id=0, has_side_effects=True, vmem_limit_bytes=60 * 1024 * 1024
        ),
        cost_estimate=pl.CostEstimate(
            flops=2 * 10**8, bytes_accessed=4 * 10**6, transcendentals=10**6
        ),
    )(
        thm, apr, ppr, cnt, hidden, base_q, live, base_k, base_v, a_in, b_out, cache,
        generated.reshape(N, W),
    )
    return pl.pallas_call(
        write_kernel,
        out_shape=[jax.ShapeDtypeStruct((A, W), bf)] * 3,
        in_specs=[vmem] * 3,
        out_specs=[hbm] * 3,
        scratch_shapes=[sem(3)],
        compiler_params=pltpu.CompilerParams(vmem_limit_bytes=2**20),
    )(*results)


def step(hidden, base_q, base_k, base_v, a_in, b_out, cache, generated, thm, live, apr, ppr, cnt):
    H = lax.axis_size("hosts")
    A, W = hidden.shape
    capacity = A // H
    fits = (
        capacity == 8
        and H <= 8
        and A <= 128
        and a_in.shape[0] == 1
        and A * cache.shape[0] == 128
        and cache.shape[2] == 128
        and H * A == 128
        and W == 8 * HEAD_SIZE
        and generated.shape[2] == 8
        and apr.shape[0] < 8
    )
    run = fused_body if fits else body
    return run(hidden, base_q, base_k, base_v, a_in, b_out, cache, generated, thm, live, apr, ppr, cnt)


def solution(mesh):
    placed = (
        P(("groups", "hosts"), "mp"),
        P(("groups", "hosts"), "mp"),
        P(("groups", "hosts"), "mp"),
        P(("groups", "hosts"), "mp"),
        P(("groups", "hosts"), "mp", None),
        P(("groups", "hosts"), None, None, "mp"),
        P(("groups", "hosts"), None, None, "mp"),
        P(("groups", "hosts"), None, None, "mp"),
        P(("groups", "hosts")),
        P(("groups", "hosts")),
        P("groups"),
        P("groups", None),
        P("groups"),
    )
    return jax.shard_map(
        step,
        mesh=mesh,
        in_specs=placed,
        out_specs=(
            P(("groups", "hosts"), "mp"),
            P(("groups", "hosts"), "mp"),
            P(("groups", "hosts"), "mp"),
        ),
        check_vma=False,
    )
```

```python
import functools
import math

import jax
import jax.numpy as jnp
from jax import lax
from jax.experimental import pallas as pl
from jax.experimental.pallas import tpu as pltpu
from jax.sharding import PartitionSpec as P

HEAD_SIZE = 128
ADAPTER_RANK = 64
BLK = 128
PBLK = 4


ADAPTER_SCALE = 0.5
ROPE_BASE = 10000.0
NEG_FILL = -1e30
MESH = pl.DeviceIdType.MESH


def rotate(values, position):
    shaped = values.reshape(values.shape[:-1] + (-1, HEAD_SIZE))
    halfway = HEAD_SIZE // 2
    frequency = ROPE_BASE ** (-(jnp.arange(halfway, dtype=jnp.float32) * (2.0 / HEAD_SIZE)))
    angles = position.astype(jnp.float32)[..., None] * frequency
    cosine = jnp.cos(angles)[..., None, :]
    sine_part = jnp.sin(angles)[..., None, :]
    first_half = shaped[..., :halfway]
    second = shaped[..., halfway:]
    turned = jnp.concatenate(
        [first_half * cosine - second * sine_part, second * cosine + first_half * sine_part],
        axis=-1,
    )
    return turned.reshape(values.shape)


def lookup_table(source_table, wanted):
    matches = wanted[:, None] == jnp.arange(source_table.shape[0], dtype=jnp.int32)[None, :]
    if source_table.ndim == 1:
        return jnp.sum(jnp.where(matches, source_table[None, :], 0), axis=1)
    return jnp.sum(jnp.where(matches[:, :, None], source_table[None, :, :], 0), axis=1)


def route_matrix(destination, validity, capacity, host_total):
    ordinal = jnp.arange(destination.shape[0], dtype=jnp.int32)
    earlier = (
        (destination[:, None] == destination[None, :])
        & validity[None, :]
        & (ordinal[None, :] < ordinal[:, None])
    )
    ranking = jnp.sum(earlier.astype(jnp.int32), axis=1)
    target = destination * capacity + ranking
    places = jnp.arange(host_total * capacity, dtype=jnp.int32)
    return ((places[:, None] == target[None, :]) & validity[None, :]).astype(jnp.bfloat16)


def pack_rows(router, payload):
    return jnp.dot(router, payload, preferred_element_type=jnp.float32).astype(jnp.bfloat16)


def attend_local(queries, chosen, statement_prefix_cache):
    head_count = queries.shape[-1] // HEAD_SIZE
    blocks = statement_prefix_cache.shape[0]
    block_keys = statement_prefix_cache[:, 0].reshape(
        blocks, statement_prefix_cache.shape[2], head_count, HEAD_SIZE
    )
    block_values = statement_prefix_cache[:, 1].reshape(
        blocks, statement_prefix_cache.shape[2], head_count, HEAD_SIZE
    )
    shaped = queries.reshape(queries.shape[:-1] + (head_count, HEAD_SIZE))
    scores = jnp.einsum(
        "nchd,bthd->ncbht", shaped, block_keys, preferred_element_type=jnp.float32
    ) * HEAD_SIZE ** (-0.5)
    chosen_mask = (chosen > 0)[:, :, :, None, None]
    masked = jnp.where(chosen_mask, scores, NEG_FILL)
    top_score = jnp.max(masked, axis=(2, 4))
    weights = jnp.where(chosen_mask, jnp.exp(masked - top_score[:, :, None, :, None]), 0.0)
    totals = jnp.sum(weights, axis=(2, 4))
    mixed_rows = jnp.einsum(
        "ncbht,bthd->nchd",
        weights.astype(jnp.bfloat16),
        block_values,
        preferred_element_type=jnp.float32,
    )
    return (mixed_rows.reshape(queries.shape), top_score, totals)


def body(
    hidden,
    base_query_projection,
    base_key_projection,
    base_value_projection,
    adapter_input_factors,
    adapter_output_factors,
    statement_prefix_cache,
    generated_token_cache,
    attempt_theorem_index,
    host_live_count,
    adapter_pool_row,
    prefix_pool_row,
    prefix_block_count,
):
    host_total = lax.axis_size("hosts")
    attempts = hidden.shape[0]
    capacity = max(1, attempts // host_total)
    owner_held_rows = adapter_input_factors.shape[0]
    local_blocks = statement_prefix_cache.shape[0]
    row_width = base_query_projection.shape[1]
    head_count = row_width // HEAD_SIZE
    ordinal = jnp.arange(attempts, dtype=jnp.int32)
    living = ordinal < host_live_count[0]
    adapter_rows = lookup_table(adapter_pool_row, attempt_theorem_index)
    block_rows = lookup_table(prefix_pool_row, attempt_theorem_index)
    block_counts = lookup_table(prefix_block_count, attempt_theorem_index)
    position = BLK * block_counts + generated_token_cache.shape[2]
    adapter_router = route_matrix(adapter_rows // owner_held_rows, living, capacity, host_total)
    adapter_pick = (
        adapter_rows[:, None] % owner_held_rows
        == jnp.arange(owner_held_rows, dtype=jnp.int32)[None, :]
    ).astype(jnp.bfloat16)
    sent_hidden = pack_rows(adapter_router, hidden).reshape(host_total, capacity, hidden.shape[1])
    sent_pick = pack_rows(adapter_router, adapter_pick).reshape(
        host_total, capacity, owner_held_rows
    )
    incoming_rows = lax.all_to_all(sent_hidden, "hosts", split_axis=0, concat_axis=0, tiled=True)
    pick_in = lax.all_to_all(sent_pick, "hosts", split_axis=0, concat_axis=0, tiled=True)
    projected_rows = jnp.einsum(
        "xjp,epk->xjek", incoming_rows, adapter_input_factors, preferred_element_type=jnp.float32
    )
    partial_rank = jnp.sum(projected_rows * pick_in.astype(jnp.float32)[..., None], axis=2)
    rank_rows = lax.psum(partial_rank, "mp").astype(jnp.bfloat16)
    spread_rows = rank_rows[:, :, None, :] * pick_in[..., None]
    query_correction = jnp.einsum(
        "exqw,qwf->exf",
        spread_rows[..., :ADAPTER_RANK],
        adapter_output_factors[:, 0],
        preferred_element_type=jnp.float32,
    )
    value_correction = jnp.einsum(
        "exqw,qwf->exf",
        spread_rows[..., ADAPTER_RANK:],
        adapter_output_factors[:, 1],
        preferred_element_type=jnp.float32,
    )
    adapter_corrections = (
        jnp.concatenate([query_correction, value_correction], axis=-1) * ADAPTER_SCALE
    ).astype(jnp.bfloat16)
    returned = lax.all_to_all(adapter_corrections, "hosts", split_axis=0, concat_axis=0, tiled=True)
    adapter_corrections = jnp.dot(
        adapter_router.T,
        returned.reshape(host_total * capacity, 2 * row_width),
        preferred_element_type=jnp.float32,
    )
    query_rows = rotate(
        base_query_projection.astype(jnp.float32) + adapter_corrections[:, :row_width], position
    ).astype(jnp.bfloat16)
    value_rows = (
        base_value_projection.astype(jnp.float32) + adapter_corrections[:, row_width:]
    ).astype(jnp.bfloat16)
    key_rows = rotate(base_key_projection.astype(jnp.float32), position).astype(jnp.bfloat16)
    requests = []
    for block_index in range(PBLK):
        wanted = living & (block_index < block_counts)
        holder = block_rows[:, block_index]
        router = route_matrix(holder // local_blocks, wanted, capacity, host_total)
        block_pick = (
            holder[:, None] % local_blocks == jnp.arange(local_blocks, dtype=jnp.int32)[None, :]
        ).astype(jnp.bfloat16)
        sent_queries = pack_rows(router, query_rows).reshape(host_total, capacity, row_width)
        sent_blocks = pack_rows(router, block_pick).reshape(host_total, capacity, local_blocks)
        requests.append((router, wanted, sent_queries, sent_blocks))
    partials = []
    for request in requests:
        answer_mixed_rows, answer_top_score, answer_totals = attend_local(
            lax.all_to_all(request[2], "hosts", split_axis=0, concat_axis=0, tiled=True),
            lax.all_to_all(request[3], "hosts", split_axis=0, concat_axis=0, tiled=True),
            statement_prefix_cache,
        )
        partials.append(
            (
                lax.all_to_all(answer_mixed_rows, "hosts", split_axis=0, concat_axis=0, tiled=True),
                lax.all_to_all(answer_top_score, "hosts", split_axis=0, concat_axis=0, tiled=True),
                lax.all_to_all(answer_totals, "hosts", split_axis=0, concat_axis=0, tiled=True),
            )
        )
    entries = []
    for block_index in range(PBLK):
        router, wanted = (requests[block_index][0], requests[block_index][1])
        mixed_rows, top_score, totals = partials[block_index]
        back_router = router.T.astype(jnp.float32)
        flat_mixed = jnp.dot(
            back_router,
            mixed_rows.reshape(host_total * capacity, row_width),
            precision=lax.Precision.HIGHEST,
        )
        flat_top = jnp.dot(
            back_router,
            top_score.reshape(host_total * capacity, head_count),
            precision=lax.Precision.HIGHEST,
        )
        flat_totals = jnp.dot(
            back_router,
            totals.reshape(host_total * capacity, head_count),
            precision=lax.Precision.HIGHEST,
        )
        flat_top = jnp.where(wanted[:, None], flat_top, NEG_FILL)
        entries.append((flat_mixed, flat_top, flat_totals))
    shaped_query = query_rows.reshape(attempts, head_count, HEAD_SIZE)
    own_keys = jnp.concatenate([generated_token_cache[:, 0], key_rows[:, None, :]], axis=1).reshape(
        attempts, -1, head_count, HEAD_SIZE
    )
    own_values = jnp.concatenate(
        [generated_token_cache[:, 1], value_rows[:, None, :]], axis=1
    ).reshape(attempts, -1, head_count, HEAD_SIZE)
    own_scores = jnp.einsum(
        "ahd,athd->aht", shaped_query, own_keys, preferred_element_type=jnp.float32
    ) * HEAD_SIZE ** (-0.5)
    own_top = jnp.max(own_scores, axis=2)
    own_weights = jnp.exp(own_scores - own_top[..., None])
    own_totals = jnp.sum(own_weights, axis=2)
    own_mixed = jnp.einsum(
        "aht,athd->ahd",
        own_weights.astype(jnp.bfloat16),
        own_values,
        preferred_element_type=jnp.float32,
    )
    overall = own_top
    for flat_mixed, flat_top, flat_totals in entries:
        overall = jnp.maximum(overall, flat_top)
    own_factor = jnp.exp(own_top - overall)
    numerator = own_mixed * own_factor[..., None]
    denominator = own_totals * own_factor
    for flat_mixed, flat_top, flat_totals in entries:
        factor = jnp.exp(flat_top - overall)
        numerator = (
            numerator + flat_mixed.reshape(attempts, head_count, HEAD_SIZE) * factor[..., None]
        )
        denominator = denominator + flat_totals * factor
    attended = (numerator / denominator[..., None]).reshape(attempts, row_width)
    live_rows = living[:, None]
    return (
        jnp.where(live_rows, attended, 0.0).astype(jnp.bfloat16),
        jnp.where(live_rows, key_rows, 0.0),
        jnp.where(live_rows, value_rows, 0.0),
    )


def _iota(shape, dim):
    return lax.broadcasted_iota(jnp.int32, shape, dim)


def _dot(a, b):
    return jnp.dot(a, b, preferred_element_type=jnp.float32)


def _dot_t(a, b):
    return lax.dot_general(a, b, (((1,), (1,)), ((), ())), preferred_element_type=jnp.float32)


def fused_kernel(
    sizes,
    thm, apr, ppr, cnt,
    hidden, base_q, live_hbm, k_hbm, val_hbm, a_hbm, b_hbm, kv_hbm, gen_hbm,
    out, key_out, val_out,
    live, base_k, base_v, a_v, b_v, kv_v, gen_v,
    snd_h, rcv_h, snd_q, rcv_q, part, snd_v, rcv_v, snd_m, rcv_m, snd_l, rcv_l, own_mix,
    local_sem, h_s, h_r, bq_s, bq_r, p_s, p_r, q_s, q_r, v_s, v_r, m_s, m_r, l_s, l_r,
    *queries,
):
    H, MP, A, CAP, L, T, PB, HEADS, SUF, NCH = sizes
    f32, bf = jnp.float32, jnp.bfloat16
    D = HEAD_SIZE
    W = HEADS * D
    W2 = W // 2
    S = H * CAP
    CW = W // NCH
    shift = CAP.bit_length() - 1
    me = lax.axis_index("hosts")
    mme = lax.axis_index("mp")

    def other(axis, d):
        return lax.rem((me if axis == "hosts" else mme) + d, H if axis == "hosts" else MP)

    locals_ = [
        pltpu.make_async_copy(src, dst, local_sem.at[i])
        for i, (src, dst) in enumerate(
            [
                (a_hbm, a_v), (b_hbm, b_v), (kv_hbm, kv_v), (gen_hbm, gen_v),
                (live_hbm, live), (k_hbm, base_k), (val_hbm, base_v),
            ]
        )
    ]
    for i in (4, 0, 1, 2, 5, 6, 3):
        locals_[i].start()

    barrier = pltpu.get_barrier_semaphore()
    for d in range(1, H):
        pl.semaphore_signal(barrier, inc=1, device_id={"hosts": other("hosts", d)}, device_id_type=MESH)
    for d in range(1, MP):
        pl.semaphore_signal(barrier, inc=1, device_id={"mp": other("mp", d)}, device_id_type=MESH)

    def send(src, dst, s, r, axis, d):
        copy = pltpu.make_async_remote_copy(
            src_ref=src, dst_ref=dst, send_sem=s, recv_sem=r,
            device_id={axis: other(axis, d)}, device_id_type=MESH,
        )
        copy.start()
        return copy

    lane8, sub8 = _iota((8, 128), 1), _iota((8, 128), 0)
    th = jnp.full((8, 128), -1, jnp.int32)
    for a in range(A):
        th = jnp.where(lane8 == a, thm[a], th)
    owner = jnp.full((8, 128), -1, jnp.int32)
    for t in range(T):
        owner = jnp.where(th == t, apr[t], owner)
    locals_[4].wait()
    n_live = live[0]
    owner = jnp.where(lane8 < n_live, owner, -1)
    member = jnp.where(owner == sub8, 1.0, 0.0).astype(f32)
    before = jnp.where(_iota((128, 128), 0) < _iota((128, 128), 1), 1.0, 0.0).astype(bf)
    rank_f = jnp.sum(member * _dot(member.astype(bf), before), axis=0, keepdims=True)
    rank_row = rank_f.astype(jnp.int32)
    target = jnp.where(owner[0:1] >= 0, owner[0:1] * CAP + rank_row, -1)
    router = jnp.where(_iota((S, A), 0) == target[:, :A], 1.0, 0.0).astype(bf)

    def folded(rows, e):
        piece = rows[e * CAP : (e + 1) * CAP]
        return jnp.concatenate([piece[:, :W2], piece[:, W2:]], axis=0)

    packed = _dot(router, hidden[...])
    for e in range(H):
        snd_h[e] = folded(packed, e).astype(bf)
    pl.semaphore_wait(barrier, H - 1 + MP - 1)
    hs = [
        send(snd_h.at[other("hosts", d)], rcv_h.at[me], h_s.at[d], h_r.at[d], "hosts", d)
        for d in range(1, H)
    ]
    packed = _dot(router, base_q[...])
    for e in range(H):
        snd_q[e] = folded(packed, e).astype(bf)
    bqs = [
        send(snd_q.at[other("hosts", d)], rcv_q.at[me], bq_s.at[d], bq_r.at[d], "hosts", d)
        for d in range(1, H)
    ]
    rcv_h[me] = snd_h[me]
    rcv_q[me] = snd_q[me]

    lane = _iota((8, 128), 1)
    half = jnp.where(lane < D // 2, lane, lane - D // 2).astype(f32)
    freq = jnp.exp(half * (-2.0 / D * math.log(ROPE_BASE)))
    counts = jnp.zeros((8, 128), jnp.int32)
    my_count = jnp.int32(0)
    for t in range(T):
        counts = jnp.where(sub8 == t, cnt[t], counts)
        my_count = jnp.where(apr[t] == me, cnt[t], my_count)
    counts = jnp.where(sub8 == T, my_count, counts)
    angle = (BLK * counts + SUF).astype(f32) * freq
    cos_t = jnp.cos(angle)
    sin_t = jnp.sin(angle)
    sin_t = jnp.where(lane < D // 2, -sin_t, sin_t)

    def turn(x, c, s):
        return x * c + pltpu.roll(x, D // 2, 1) * s

    locals_[0].wait()
    for copy in hs:
        copy.wait_recv()
    rows = rcv_h[...].reshape(H * 2 * CAP, W2)
    left = _dot(rows, a_v[0, :W2, :])
    right = _dot(rows, a_v[0, W2:, :])
    part[mme] = jnp.concatenate(
        [
            left[2 * CAP * e : 2 * CAP * e + CAP] + right[2 * CAP * e + CAP : 2 * CAP * (e + 1)]
            for e in range(H)
        ],
        axis=0,
    )
    ps = [
        send(part.at[mme], part.at[mme], p_s.at[d], p_r.at[d], "mp", d) for d in range(1, MP)
    ]
    for copy in bqs:
        copy.wait_recv()
    bq = rcv_q[...].astype(f32)
    bq_half = [
        jnp.concatenate([bq[e, k * CAP : (k + 1) * CAP] for e in range(H)], axis=0)
        for k in range(2)
    ]
    locals_[1].wait()
    for copy in ps:
        copy.wait_recv()
    ranks = part[0]
    for m in range(1, MP):
        ranks = ranks + part[m]
    ranks = ranks.astype(bf).astype(f32)
    rank_q = ranks[:, :ADAPTER_RANK].astype(bf)
    rank_v = pltpu.roll(ranks, ADAPTER_RANK, 1)[:, :ADAPTER_RANK].astype(bf)
    qs = []
    for c in range(NCH):
        cols = slice(c * CW, (c + 1) * CW)
        delta = (_dot(rank_q, b_v[0, 0, :, cols]) * ADAPTER_SCALE).astype(bf).astype(f32)
        k, off = (c * CW) // W2, (c * CW) % W2
        raw = bq_half[k][:, off : off + CW] + delta
        for h in range(CW // D):
            queries[c][me, :, h * D : (h + 1) * D] = turn(
                raw[:, h * D : (h + 1) * D], cos_t[T : T + 1], sin_t[T : T + 1]
            ).astype(bf)
        view = queries[c].at[me]
        qs.append(
            [send(view, view, q_s.at[c, d], q_r.at[c, d], "hosts", d) for d in range(1, H)]
        )
    delta = _dot(rank_v, b_v[0, 1]) * ADAPTER_SCALE
    for e in range(H):
        snd_v[e] = folded(delta, e).astype(bf)
    vs = [
        send(snd_v.at[other("hosts", d)], rcv_v.at[me], v_s.at[d], v_r.at[d], "hosts", d)
        for d in range(1, H)
    ]
    rcv_v[me] = snd_v[me]

    sub128 = _iota((128, 128), 0)
    both = jnp.where(sub128 == 0, th[0:1].astype(f32), jnp.where(sub128 == 1, rank_f, 0.0))
    turned = both.T[:A].astype(jnp.int32)
    th_c, rank_c = turned[:, 0:1], turned[:, 1:2]
    lane_a = _iota((A, 128), 1)
    live_c = _iota((A, 1), 0) < n_live
    owner_c = jnp.full((A, 1), -1, jnp.int32)
    cos_a = jnp.zeros((A, 128), f32)
    sin_a = jnp.zeros((A, 128), f32)
    blocks_c = [jnp.full((A, 1), -1, jnp.int32) for _ in range(PB)]
    for t in range(T):
        here = th_c == t
        owner_c = jnp.where(here, apr[t], owner_c)
        cos_a = jnp.where(here, cos_t[t : t + 1], cos_a)
        sin_a = jnp.where(here, sin_t[t : t + 1], sin_a)
        for j in range(PB):
            blocks_c[j] = jnp.where(here, jnp.where(j < cnt[t], ppr[t, j], -1), blocks_c[j])
    owner_c = jnp.where(live_c, owner_c, -1)
    slot_ok = jnp.where(rank_c == (lane_a & (CAP - 1)), 1, 0)
    group = lane_a >> shift
    used = jnp.zeros((A, 128), jnp.int32)
    for j in range(PB):
        used = used + jnp.where(blocks_c[j] == group, 1, 0)
    used = jnp.where(live_c, used * slot_ok, 0) > 0
    fetch = jnp.where(owner_c * H + me == group, slot_ok, 0).astype(f32).astype(bf)
    unpack = jnp.where(
        owner_c * CAP + rank_c == _iota((A, S), 1), jnp.where(owner_c >= 0, 1.0, 0.0), 0.0
    ).astype(bf)
    keys = []
    locals_[5].wait()
    for h in range(HEADS):
        cols = slice(h * D, (h + 1) * D)
        key = turn(base_k[:, cols].astype(f32), cos_a, sin_a).astype(bf).astype(f32)
        keys.append(key)
        key_out[:, cols] = jnp.where(live_c, key, 0.0).astype(bf)

    whose = []
    for b in range(L):
        index = jnp.int32(0)
        for t in range(T):
            for j in range(PB):
                index = jnp.where(ppr[t, j] == me * L + b, apr[t], index)
        whose.append(index)
    scale = D ** (-0.5)
    locals_[2].wait()
    lane_block = (_iota((128, 128), 1) >> shift) & (L - 1)
    sub_h = _iota((HEADS, 128), 0)
    lse_t = jnp.zeros((HEADS, 128), f32)
    ms = []
    for c in range(NCH):
        for copy in qs[c]:
            copy.wait_recv()
        for h in range(c * CW // D, (c + 1) * CW // D):
            cols = slice(h * D, (h + 1) * D)
            within = slice(h * D - c * CW, (h + 1) * D - c * CW)
            asked = [queries[c][whose[b], :, within].astype(f32) for b in range(L)]
            asked = jnp.concatenate(
                [asked[b][e * CAP : (e + 1) * CAP] for e in range(H) for b in range(L)], axis=0
            ).astype(bf)
            scores = _dot_t(kv_v[0, 0, :, cols], asked)
            for b in range(1, L):
                scores = jnp.where(lane_block == b, _dot_t(kv_v[b, 0, :, cols], asked), scores)
            scores = scores * scale
            top = jnp.max(scores, axis=0, keepdims=True)
            weights = jnp.exp(scores - top)
            total = jnp.sum(weights, axis=0, keepdims=True)
            lse_t = jnp.where(sub_h == h, top + jnp.log(total), lse_t)
            weights = (weights * (1.0 / total)).T
            mixed = []
            for b in range(L):
                rows = jnp.concatenate(
                    [weights[(e * L + b) * CAP : (e * L + b + 1) * CAP] for e in range(H)], axis=0
                )
                mixed.append(_dot(rows.astype(bf), kv_v[b, 1, :, cols]))
            for e in range(H):
                snd_m[e, :, cols] = jnp.concatenate(
                    [mixed[b][e * CAP : (e + 1) * CAP] for b in range(L)], axis=0
                ).astype(bf)
        if c == NCH - 1:
            rcv_l[me] = lse_t
            for d in range(1, H):
                snd_l[d] = pltpu.roll(lse_t, (128 - L * CAP * d) % 128, 1)
            ls = [
                send(snd_l.at[d], rcv_l.at[me], l_s.at[d], l_r.at[d], "hosts", d)
                for d in range(1, H)
            ]
        span = pl.ds(c * CW, CW)
        ms.append(
            [
                send(
                    snd_m.at[other("hosts", d), :, span], rcv_m.at[me, :, span],
                    m_s.at[c, d], m_r.at[c, d], "hosts", d,
                )
                for d in range(1, H)
            ]
        )
    rcv_m[me] = snd_m[me]

    locals_[3].wait()
    N = gen_v.shape[0]
    lane_n, sub_n = _iota((A, N), 1), _iota((A, N), 0)
    mine = ((lane_n >> (SUF.bit_length())) == sub_n) & ((lane_n & (2 * SUF - 1)) < SUF)
    own_top, own_total, own_self = [], [], []
    for h in range(HEADS):
        cols = slice(h * D, (h + 1) * D)
        c, start = (h * D) // CW, (h * D) % CW
        query = _dot(fetch, queries[c][:, :, start : start + D].reshape(H * S, D))
        scores = _dot_t(query.astype(bf), gen_v[:, cols]) * scale
        scores = jnp.where(mine, scores, NEG_FILL)
        self_score = jnp.sum(query * keys[h], axis=1, keepdims=True) * scale
        top = jnp.maximum(jnp.max(scores, axis=1, keepdims=True), self_score)
        weights = jnp.where(mine, jnp.exp(scores - top), 0.0)
        self_weight = jnp.exp(self_score - top)
        own_top.append(top)
        own_total.append(jnp.sum(weights, axis=1, keepdims=True) + self_weight)
        own_mix[:, cols] = (
            _dot(pltpu.roll(weights, SUF, 1).astype(bf), gen_v[:, cols])
        )
        own_self.append(self_weight.astype(bf).astype(f32))

    locals_[6].wait()
    for copy in vs:
        copy.wait_recv()
    dv = rcv_v[...].astype(f32)
    dv_att = [
        _dot(
            unpack,
            jnp.concatenate([dv[p, k * CAP : (k + 1) * CAP] for p in range(H)], axis=0).astype(bf),
        )
        for k in range(2)
    ]
    for h in range(HEADS):
        cols = slice(h * D, (h + 1) * D)
        k, off = (h * D) // W2, (h * D) % W2
        value = (base_v[:, cols].astype(f32) + dv_att[k][:, off : off + D]).astype(bf).astype(f32)
        val_out[:, cols] = jnp.where(live_c, value, 0.0).astype(bf)
        own_mix[:, cols] += own_self[h] * value

    for copy in ls:
        copy.wait_recv()
    lse = jnp.zeros((HEADS, 128), f32)
    lane_h = _iota((HEADS, 128), 1)
    for g in range(H):
        lse = jnp.where((lane_h >= g * L * CAP) & (lane_h < (g + 1) * L * CAP), rcv_l[g], lse)
    for c in range(NCH):
        for copy in ms[c]:
            copy.wait_recv()
        for h in range(c * CW // D, (c + 1) * CW // D):
            cols = slice(h * D, (h + 1) * D)
            logs = jnp.where(used, lse[h : h + 1], NEG_FILL)
            top = jnp.maximum(jnp.max(logs, axis=1, keepdims=True), own_top[h])
            factor = jnp.where(used, jnp.exp(logs - top), 0.0)
            own_factor = jnp.exp(own_top[h] - top)
            inverse = 1.0 / (jnp.sum(factor, axis=1, keepdims=True) + own_total[h] * own_factor)
            result = _dot(
                (factor * inverse).astype(bf), rcv_m[:, :, cols].reshape(H * L * CAP, D)
            ) + own_mix[:, cols] * (own_factor * inverse)
            out[:, cols] = jnp.where(live_c, result, 0.0).astype(bf)
    for copies in [hs, bqs, ps, vs, ls] + qs + ms:
        for copy in copies:
            copy.wait_send()


def write_kernel(*refs):
    sems = refs[6]
    copies = [pltpu.make_async_copy(refs[i], refs[3 + i], sems.at[i]) for i in range(3)]
    for copy in copies:
        copy.start()
    for copy in copies:
        copy.wait()


def fused_body(
    hidden, base_q, base_k, base_v, a_in, b_out, cache, generated, thm, live, apr, ppr, cnt
):
    H, MP = lax.axis_size("hosts"), lax.axis_size("mp")
    A, W = hidden.shape
    CAP = A // H
    L, SUF = cache.shape[0], generated.shape[2]
    HEADS = W // HEAD_SIZE
    S = H * CAP
    NCH = 2
    bf, f32 = jnp.bfloat16, jnp.float32
    N = generated.shape[0] * 2 * SUF
    sizes = (H, MP, A, CAP, L, apr.shape[0], ppr.shape[1], HEADS, SUF, NCH)
    smem = pl.BlockSpec(memory_space=pltpu.SMEM)
    vmem = pl.BlockSpec(memory_space=pltpu.VMEM)
    hbm = pl.BlockSpec(memory_space=pl.ANY)
    fold = (H, 2 * CAP, W // 2)
    sem = lambda *shape: pltpu.SemaphoreType.DMA(shape)
    results = pl.pallas_call(
        functools.partial(fused_kernel, sizes),
        out_shape=[pltpu.VMEM((A, W), bf)] * 3,
        in_specs=[smem] * 4 + [vmem] * 2 + [hbm] * 7,
        out_specs=[vmem] * 3,
        scratch_shapes=[
            pltpu.SMEM(live.shape, jnp.int32),
            pltpu.VMEM((A, W), bf),
            pltpu.VMEM((A, W), bf),
            pltpu.VMEM(a_in.shape, bf),
            pltpu.VMEM(b_out.shape, bf),
            pltpu.VMEM(cache.shape, bf),
            pltpu.VMEM((N, W), bf),
            pltpu.VMEM(fold, bf),
            pltpu.VMEM(fold, bf),
            pltpu.VMEM(fold, bf),
            pltpu.VMEM(fold, bf),
            pltpu.VMEM((MP, S, 128), f32),
            pltpu.VMEM(fold, bf),
            pltpu.VMEM(fold, bf),
            pltpu.VMEM((H, L * CAP, W), bf),
            pltpu.VMEM((H, L * CAP, W), bf),
            pltpu.VMEM((H, HEADS, 128), f32),
            pltpu.VMEM((H, HEADS, 128), f32),
            pltpu.VMEM((A, W), f32),
            sem(7), sem(H), sem(H), sem(H), sem(H), sem(MP), sem(MP),
            sem(NCH, H), sem(NCH, H), sem(H), sem(H), sem(NCH, H), sem(NCH, H), sem(H), sem(H),
        ]
        + [pltpu.VMEM((H, S, W // NCH), bf)] * NCH,
        compiler_params=pltpu.CompilerParams(
            collective_id=0, has_side_effects=True, vmem_limit_bytes=60 * 1024 * 1024
        ),
        cost_estimate=pl.CostEstimate(
            flops=2 * 10**8, bytes_accessed=4 * 10**6, transcendentals=10**6
        ),
    )(
        thm, apr, ppr, cnt, hidden, base_q, live, base_k, base_v, a_in, b_out, cache,
        generated.reshape(N, W),
    )
    return pl.pallas_call(
        write_kernel,
        out_shape=[jax.ShapeDtypeStruct((A, W), bf)] * 3,
        in_specs=[vmem] * 3,
        out_specs=[hbm] * 3,
        scratch_shapes=[sem(3)],
        compiler_params=pltpu.CompilerParams(vmem_limit_bytes=2**20),
    )(*results)


def step(hidden, base_q, base_k, base_v, a_in, b_out, cache, generated, thm, live, apr, ppr, cnt):
    H = lax.axis_size("hosts")
    A, W = hidden.shape
    capacity = A // H
    fits = (
        capacity == 8
        and H <= 8
        and A <= 128
        and a_in.shape[0] == 1
        and A * cache.shape[0] == 128
        and cache.shape[0] == 4
        and cache.shape[2] == 128
        and H * A == 128
        and W == 8 * HEAD_SIZE
        and generated.shape[2] == 8
        and apr.shape[0] < 8
    )
    run = fused_body if fits else body
    return run(hidden, base_q, base_k, base_v, a_in, b_out, cache, generated, thm, live, apr, ppr, cnt)


def solution(mesh):
    placed = (
        P(("groups", "hosts"), "mp"),
        P(("groups", "hosts"), "mp"),
        P(("groups", "hosts"), "mp"),
        P(("groups", "hosts"), "mp"),
        P(("groups", "hosts"), "mp", None),
        P(("groups", "hosts"), None, None, "mp"),
        P(("groups", "hosts"), None, None, "mp"),
        P(("groups", "hosts"), None, None, "mp"),
        P(("groups", "hosts")),
        P(("groups", "hosts")),
        P("groups"),
        P("groups", None),
        P("groups"),
    )
    return jax.shard_map(
        step,
        mesh=mesh,
        in_specs=placed,
        out_specs=(
            P(("groups", "hosts"), "mp"),
            P(("groups", "hosts"), "mp"),
            P(("groups", "hosts"), "mp"),
        ),
        check_vma=False,
    )
```

```python
import functools
import math

import jax
import jax.numpy as jnp
from jax import lax
from jax.experimental import pallas as pl
from jax.experimental.pallas import tpu as pltpu
from jax.sharding import PartitionSpec as P

HEAD_SIZE = 128
ADAPTER_RANK = 64
BLK = 128
PBLK = 4


ADAPTER_SCALE = 0.5
ROPE_BASE = 10000.0
NEG_FILL = -1e30
MESH = pl.DeviceIdType.MESH


def rotate(values, position):
    shaped = values.reshape(values.shape[:-1] + (-1, HEAD_SIZE))
    halfway = HEAD_SIZE // 2
    frequency = ROPE_BASE ** (-(jnp.arange(halfway, dtype=jnp.float32) * (2.0 / HEAD_SIZE)))
    angles = position.astype(jnp.float32)[..., None] * frequency
    cosine = jnp.cos(angles)[..., None, :]
    sine_part = jnp.sin(angles)[..., None, :]
    first_half = shaped[..., :halfway]
    second = shaped[..., halfway:]
    turned = jnp.concatenate(
        [first_half * cosine - second * sine_part, second * cosine + first_half * sine_part],
        axis=-1,
    )
    return turned.reshape(values.shape)


def lookup_table(source_table, wanted):
    matches = wanted[:, None] == jnp.arange(source_table.shape[0], dtype=jnp.int32)[None, :]
    if source_table.ndim == 1:
        return jnp.sum(jnp.where(matches, source_table[None, :], 0), axis=1)
    return jnp.sum(jnp.where(matches[:, :, None], source_table[None, :, :], 0), axis=1)


def route_matrix(destination, validity, capacity, host_total):
    ordinal = jnp.arange(destination.shape[0], dtype=jnp.int32)
    earlier = (
        (destination[:, None] == destination[None, :])
        & validity[None, :]
        & (ordinal[None, :] < ordinal[:, None])
    )
    ranking = jnp.sum(earlier.astype(jnp.int32), axis=1)
    target = destination * capacity + ranking
    places = jnp.arange(host_total * capacity, dtype=jnp.int32)
    return ((places[:, None] == target[None, :]) & validity[None, :]).astype(jnp.bfloat16)


def pack_rows(router, payload):
    return jnp.dot(router, payload, preferred_element_type=jnp.float32).astype(jnp.bfloat16)


def attend_local(queries, chosen, statement_prefix_cache):
    head_count = queries.shape[-1] // HEAD_SIZE
    blocks = statement_prefix_cache.shape[0]
    block_keys = statement_prefix_cache[:, 0].reshape(
        blocks, statement_prefix_cache.shape[2], head_count, HEAD_SIZE
    )
    block_values = statement_prefix_cache[:, 1].reshape(
        blocks, statement_prefix_cache.shape[2], head_count, HEAD_SIZE
    )
    shaped = queries.reshape(queries.shape[:-1] + (head_count, HEAD_SIZE))
    scores = jnp.einsum(
        "nchd,bthd->ncbht", shaped, block_keys, preferred_element_type=jnp.float32
    ) * HEAD_SIZE ** (-0.5)
    chosen_mask = (chosen > 0)[:, :, :, None, None]
    masked = jnp.where(chosen_mask, scores, NEG_FILL)
    top_score = jnp.max(masked, axis=(2, 4))
    weights = jnp.where(chosen_mask, jnp.exp(masked - top_score[:, :, None, :, None]), 0.0)
    totals = jnp.sum(weights, axis=(2, 4))
    mixed_rows = jnp.einsum(
        "ncbht,bthd->nchd",
        weights.astype(jnp.bfloat16),
        block_values,
        preferred_element_type=jnp.float32,
    )
    return (mixed_rows.reshape(queries.shape), top_score, totals)


def body(
    hidden,
    base_query_projection,
    base_key_projection,
    base_value_projection,
    adapter_input_factors,
    adapter_output_factors,
    statement_prefix_cache,
    generated_token_cache,
    attempt_theorem_index,
    host_live_count,
    adapter_pool_row,
    prefix_pool_row,
    prefix_block_count,
):
    host_total = lax.axis_size("hosts")
    attempts = hidden.shape[0]
    capacity = max(1, attempts // host_total)
    owner_held_rows = adapter_input_factors.shape[0]
    local_blocks = statement_prefix_cache.shape[0]
    row_width = base_query_projection.shape[1]
    head_count = row_width // HEAD_SIZE
    ordinal = jnp.arange(attempts, dtype=jnp.int32)
    living = ordinal < host_live_count[0]
    adapter_rows = lookup_table(adapter_pool_row, attempt_theorem_index)
    block_rows = lookup_table(prefix_pool_row, attempt_theorem_index)
    block_counts = lookup_table(prefix_block_count, attempt_theorem_index)
    position = BLK * block_counts + generated_token_cache.shape[2]
    adapter_router = route_matrix(adapter_rows // owner_held_rows, living, capacity, host_total)
    adapter_pick = (
        adapter_rows[:, None] % owner_held_rows
        == jnp.arange(owner_held_rows, dtype=jnp.int32)[None, :]
    ).astype(jnp.bfloat16)
    sent_hidden = pack_rows(adapter_router, hidden).reshape(host_total, capacity, hidden.shape[1])
    sent_pick = pack_rows(adapter_router, adapter_pick).reshape(
        host_total, capacity, owner_held_rows
    )
    incoming_rows = lax.all_to_all(sent_hidden, "hosts", split_axis=0, concat_axis=0, tiled=True)
    pick_in = lax.all_to_all(sent_pick, "hosts", split_axis=0, concat_axis=0, tiled=True)
    projected_rows = jnp.einsum(
        "xjp,epk->xjek", incoming_rows, adapter_input_factors, preferred_element_type=jnp.float32
    )
    partial_rank = jnp.sum(projected_rows * pick_in.astype(jnp.float32)[..., None], axis=2)
    rank_rows = lax.psum(partial_rank, "mp").astype(jnp.bfloat16)
    spread_rows = rank_rows[:, :, None, :] * pick_in[..., None]
    query_correction = jnp.einsum(
        "exqw,qwf->exf",
        spread_rows[..., :ADAPTER_RANK],
        adapter_output_factors[:, 0],
        preferred_element_type=jnp.float32,
    )
    value_correction = jnp.einsum(
        "exqw,qwf->exf",
        spread_rows[..., ADAPTER_RANK:],
        adapter_output_factors[:, 1],
        preferred_element_type=jnp.float32,
    )
    adapter_corrections = (
        jnp.concatenate([query_correction, value_correction], axis=-1) * ADAPTER_SCALE
    ).astype(jnp.bfloat16)
    returned = lax.all_to_all(adapter_corrections, "hosts", split_axis=0, concat_axis=0, tiled=True)
    adapter_corrections = jnp.dot(
        adapter_router.T,
        returned.reshape(host_total * capacity, 2 * row_width),
        preferred_element_type=jnp.float32,
    )
    query_rows = rotate(
        base_query_projection.astype(jnp.float32) + adapter_corrections[:, :row_width], position
    ).astype(jnp.bfloat16)
    value_rows = (
        base_value_projection.astype(jnp.float32) + adapter_corrections[:, row_width:]
    ).astype(jnp.bfloat16)
    key_rows = rotate(base_key_projection.astype(jnp.float32), position).astype(jnp.bfloat16)
    requests = []
    for block_index in range(PBLK):
        wanted = living & (block_index < block_counts)
        holder = block_rows[:, block_index]
        router = route_matrix(holder // local_blocks, wanted, capacity, host_total)
        block_pick = (
            holder[:, None] % local_blocks == jnp.arange(local_blocks, dtype=jnp.int32)[None, :]
        ).astype(jnp.bfloat16)
        sent_queries = pack_rows(router, query_rows).reshape(host_total, capacity, row_width)
        sent_blocks = pack_rows(router, block_pick).reshape(host_total, capacity, local_blocks)
        requests.append((router, wanted, sent_queries, sent_blocks))
    partials = []
    for request in requests:
        answer_mixed_rows, answer_top_score, answer_totals = attend_local(
            lax.all_to_all(request[2], "hosts", split_axis=0, concat_axis=0, tiled=True),
            lax.all_to_all(request[3], "hosts", split_axis=0, concat_axis=0, tiled=True),
            statement_prefix_cache,
        )
        partials.append(
            (
                lax.all_to_all(answer_mixed_rows, "hosts", split_axis=0, concat_axis=0, tiled=True),
                lax.all_to_all(answer_top_score, "hosts", split_axis=0, concat_axis=0, tiled=True),
                lax.all_to_all(answer_totals, "hosts", split_axis=0, concat_axis=0, tiled=True),
            )
        )
    entries = []
    for block_index in range(PBLK):
        router, wanted = (requests[block_index][0], requests[block_index][1])
        mixed_rows, top_score, totals = partials[block_index]
        back_router = router.T.astype(jnp.float32)
        flat_mixed = jnp.dot(
            back_router,
            mixed_rows.reshape(host_total * capacity, row_width),
            precision=lax.Precision.HIGHEST,
        )
        flat_top = jnp.dot(
            back_router,
            top_score.reshape(host_total * capacity, head_count),
            precision=lax.Precision.HIGHEST,
        )
        flat_totals = jnp.dot(
            back_router,
            totals.reshape(host_total * capacity, head_count),
            precision=lax.Precision.HIGHEST,
        )
        flat_top = jnp.where(wanted[:, None], flat_top, NEG_FILL)
        entries.append((flat_mixed, flat_top, flat_totals))
    shaped_query = query_rows.reshape(attempts, head_count, HEAD_SIZE)
    own_keys = jnp.concatenate([generated_token_cache[:, 0], key_rows[:, None, :]], axis=1).reshape(
        attempts, -1, head_count, HEAD_SIZE
    )
    own_values = jnp.concatenate(
        [generated_token_cache[:, 1], value_rows[:, None, :]], axis=1
    ).reshape(attempts, -1, head_count, HEAD_SIZE)
    own_scores = jnp.einsum(
        "ahd,athd->aht", shaped_query, own_keys, preferred_element_type=jnp.float32
    ) * HEAD_SIZE ** (-0.5)
    own_top = jnp.max(own_scores, axis=2)
    own_weights = jnp.exp(own_scores - own_top[..., None])
    own_totals = jnp.sum(own_weights, axis=2)
    own_mixed = jnp.einsum(
        "aht,athd->ahd",
        own_weights.astype(jnp.bfloat16),
        own_values,
        preferred_element_type=jnp.float32,
    )
    overall = own_top
    for flat_mixed, flat_top, flat_totals in entries:
        overall = jnp.maximum(overall, flat_top)
    own_factor = jnp.exp(own_top - overall)
    numerator = own_mixed * own_factor[..., None]
    denominator = own_totals * own_factor
    for flat_mixed, flat_top, flat_totals in entries:
        factor = jnp.exp(flat_top - overall)
        numerator = (
            numerator + flat_mixed.reshape(attempts, head_count, HEAD_SIZE) * factor[..., None]
        )
        denominator = denominator + flat_totals * factor
    attended = (numerator / denominator[..., None]).reshape(attempts, row_width)
    live_rows = living[:, None]
    return (
        jnp.where(live_rows, attended, 0.0).astype(jnp.bfloat16),
        jnp.where(live_rows, key_rows, 0.0),
        jnp.where(live_rows, value_rows, 0.0),
    )


def _iota(shape, dim):
    return lax.broadcasted_iota(jnp.int32, shape, dim)


def _dot(a, b):
    return jnp.dot(a, b, preferred_element_type=jnp.float32)


def _dot_t(a, b):
    return lax.dot_general(a, b, (((1,), (1,)), ((), ())), preferred_element_type=jnp.float32)


def fused_kernel(
    sizes,
    thm, apr, ppr, cnt,
    hidden, base_q, live_hbm, k_hbm, val_hbm, a_hbm, b_hbm, kv_hbm, gen_hbm,
    out, key_out, val_out,
    live, base_k, base_v, a_v, b_v, kv_v, gen_v,
    snd_h, rcv_h, snd_q, rcv_q, part, snd_v, rcv_v, snd_m, rcv_m, snd_l, rcv_l, own_mix,
    local_sem, h_s, h_r, bq_s, bq_r, p_s, p_r, q_s, q_r, v_s, v_r, m_s, m_r, l_s, l_r,
    *queries,
):
    H, MP, A, CAP, L, T, PB, HEADS, SUF, NCH = sizes
    f32, bf = jnp.float32, jnp.bfloat16
    D = HEAD_SIZE
    W = HEADS * D
    W2 = W // 2
    S = H * CAP
    CW = W // NCH
    shift = CAP.bit_length() - 1
    me = lax.axis_index("hosts")
    mme = lax.axis_index("mp")

    def other(axis, d):
        return lax.rem((me if axis == "hosts" else mme) + d, H if axis == "hosts" else MP)

    locals_ = [
        pltpu.make_async_copy(src, dst, local_sem.at[i])
        for i, (src, dst) in enumerate(
            [
                (a_hbm, a_v), (b_hbm, b_v), (kv_hbm, kv_v), (gen_hbm, gen_v),
                (live_hbm, live), (k_hbm, base_k), (val_hbm, base_v),
            ]
        )
    ]
    for i in (4, 0, 1, 2, 5, 6, 3):
        locals_[i].start()

    barrier = pltpu.get_barrier_semaphore()
    for d in range(1, H):
        pl.semaphore_signal(barrier, inc=1, device_id={"hosts": other("hosts", d)}, device_id_type=MESH)
    for d in range(1, MP):
        pl.semaphore_signal(barrier, inc=1, device_id={"mp": other("mp", d)}, device_id_type=MESH)

    def send(src, dst, s, r, axis, d):
        copy = pltpu.make_async_remote_copy(
            src_ref=src, dst_ref=dst, send_sem=s, recv_sem=r,
            device_id={axis: other(axis, d)}, device_id_type=MESH,
        )
        copy.start()
        return copy

    lane8, sub8 = _iota((8, 128), 1), _iota((8, 128), 0)
    th = jnp.full((8, 128), -1, jnp.int32)
    for a in range(A):
        th = jnp.where(lane8 == a, thm[a], th)
    owner = jnp.full((8, 128), -1, jnp.int32)
    for t in range(T):
        owner = jnp.where(th == t, apr[t], owner)
    locals_[4].wait()
    n_live = live[0]
    owner = jnp.where(lane8 < n_live, owner, -1)
    member = jnp.where(owner == sub8, 1.0, 0.0).astype(f32)
    before = jnp.where(_iota((128, 128), 0) < _iota((128, 128), 1), 1.0, 0.0).astype(bf)
    rank_f = jnp.sum(member * _dot(member.astype(bf), before), axis=0, keepdims=True)
    rank_row = rank_f.astype(jnp.int32)
    target = jnp.where(owner[0:1] >= 0, owner[0:1] * CAP + rank_row, -1)
    router = jnp.where(_iota((S, A), 0) == target[:, :A], 1.0, 0.0).astype(bf)

    def folded(rows, e):
        piece = rows[e * CAP : (e + 1) * CAP]
        return jnp.concatenate([piece[:, :W2], piece[:, W2:]], axis=0)

    packed = _dot(router, hidden[...])
    for e in range(H):
        snd_h[e] = folded(packed, e).astype(bf)
    pl.semaphore_wait(barrier, H - 1 + MP - 1)
    hs = [
        send(snd_h.at[other("hosts", d)], rcv_h.at[me], h_s.at[d], h_r.at[d], "hosts", d)
        for d in range(1, H)
    ]
    packed = _dot(router, base_q[...])
    for e in range(H):
        snd_q[e] = folded(packed, e).astype(bf)
    bqs = [
        send(snd_q.at[other("hosts", d)], rcv_q.at[me], bq_s.at[d], bq_r.at[d], "hosts", d)
        for d in range(1, H)
    ]
    rcv_h[me] = snd_h[me]
    rcv_q[me] = snd_q[me]

    lane = _iota((8, 128), 1)
    half = jnp.where(lane < D // 2, lane, lane - D // 2).astype(f32)
    freq = jnp.exp(half * (-2.0 / D * math.log(ROPE_BASE)))
    counts = jnp.zeros((8, 128), jnp.int32)
    my_count = jnp.int32(0)
    for t in range(T):
        counts = jnp.where(sub8 == t, cnt[t], counts)
        my_count = jnp.where(apr[t] == me, cnt[t], my_count)
    counts = jnp.where(sub8 == T, my_count, counts)
    angle = (BLK * counts + SUF).astype(f32) * freq
    cos_t = jnp.cos(angle)
    sin_t = jnp.sin(angle)
    sin_t = jnp.where(lane < D // 2, -sin_t, sin_t)

    def turn(x, c, s):
        return x * c + pltpu.roll(x, D // 2, 1) * s

    locals_[0].wait()
    for copy in hs:
        copy.wait_recv()
    rows = rcv_h[...].reshape(H * 2 * CAP, W2)
    left = _dot(rows, a_v[0, :W2, :])
    right = _dot(rows, a_v[0, W2:, :])
    part[mme] = jnp.concatenate(
        [
            left[2 * CAP * e : 2 * CAP * e + CAP] + right[2 * CAP * e + CAP : 2 * CAP * (e + 1)]
            for e in range(H)
        ],
        axis=0,
    )
    ps = [
        send(part.at[mme], part.at[mme], p_s.at[d], p_r.at[d], "mp", d) for d in range(1, MP)
    ]
    for copy in bqs:
        copy.wait_recv()
    bq = rcv_q[...].astype(f32)
    bq_half = [
        jnp.concatenate([bq[e, k * CAP : (k + 1) * CAP] for e in range(H)], axis=0)
        for k in range(2)
    ]
    locals_[1].wait()
    for copy in ps:
        copy.wait_recv()
    ranks = part[0]
    for m in range(1, MP):
        ranks = ranks + part[m]
    ranks = ranks.astype(bf).astype(f32)
    rank_q = ranks[:, :ADAPTER_RANK].astype(bf)
    rank_v = pltpu.roll(ranks, ADAPTER_RANK, 1)[:, :ADAPTER_RANK].astype(bf)
    qs = []
    for c in range(NCH):
        cols = slice(c * CW, (c + 1) * CW)
        delta = (_dot(rank_q, b_v[0, 0, :, cols]) * ADAPTER_SCALE).astype(bf).astype(f32)
        k, off = (c * CW) // W2, (c * CW) % W2
        raw = bq_half[k][:, off : off + CW] + delta
        for h in range(CW // D):
            queries[c][me, :, h * D : (h + 1) * D] = turn(
                raw[:, h * D : (h + 1) * D], cos_t[T : T + 1], sin_t[T : T + 1]
            ).astype(bf)
        view = queries[c].at[me]
        qs.append(
            [send(view, view, q_s.at[c, d], q_r.at[c, d], "hosts", d) for d in range(1, H)]
        )
    delta = _dot(rank_v, b_v[0, 1]) * ADAPTER_SCALE
    for e in range(H):
        snd_v[e] = folded(delta, e).astype(bf)
    vs = [
        send(snd_v.at[other("hosts", d)], rcv_v.at[me], v_s.at[d], v_r.at[d], "hosts", d)
        for d in range(1, H)
    ]
    rcv_v[me] = snd_v[me]

    sub128 = _iota((128, 128), 0)
    both = jnp.where(sub128 == 0, th[0:1].astype(f32), jnp.where(sub128 == 1, rank_f, 0.0))
    turned = both.T[:A].astype(jnp.int32)
    th_c, rank_c = turned[:, 0:1], turned[:, 1:2]
    lane_a = _iota((A, 128), 1)
    live_c = _iota((A, 1), 0) < n_live
    owner_c = jnp.full((A, 1), -1, jnp.int32)
    cos_a = jnp.zeros((A, 128), f32)
    sin_a = jnp.zeros((A, 128), f32)
    blocks_c = [jnp.full((A, 1), -1, jnp.int32) for _ in range(PB)]
    for t in range(T):
        here = th_c == t
        owner_c = jnp.where(here, apr[t], owner_c)
        cos_a = jnp.where(here, cos_t[t : t + 1], cos_a)
        sin_a = jnp.where(here, sin_t[t : t + 1], sin_a)
        for j in range(PB):
            blocks_c[j] = jnp.where(here, jnp.where(j < cnt[t], ppr[t, j], -1), blocks_c[j])
    owner_c = jnp.where(live_c, owner_c, -1)
    slot_ok = jnp.where(rank_c == (lane_a & (CAP - 1)), 1, 0)
    group = lane_a >> shift
    used = jnp.zeros((A, 128), jnp.int32)
    for j in range(PB):
        used = used + jnp.where(blocks_c[j] == group, 1, 0)
    used = jnp.where(live_c, used * slot_ok, 0) > 0
    fetch = jnp.where(owner_c * H + me == group, slot_ok, 0).astype(f32).astype(bf)
    unpack = jnp.where(
        owner_c * CAP + rank_c == _iota((A, S), 1), jnp.where(owner_c >= 0, 1.0, 0.0), 0.0
    ).astype(bf)
    keys = []
    locals_[5].wait()
    for h in range(HEADS):
        cols = slice(h * D, (h + 1) * D)
        key = turn(base_k[:, cols].astype(f32), cos_a, sin_a).astype(bf).astype(f32)
        keys.append(key)
        key_out[:, cols] = jnp.where(live_c, key, 0.0).astype(bf)

    whose = []
    for b in range(L):
        index = jnp.int32(0)
        for t in range(T):
            for j in range(PB):
                index = jnp.where(ppr[t, j] == me * L + b, apr[t], index)
        whose.append(index)
    scale = D ** (-0.5)
    locals_[2].wait()
    lane_block = (_iota((128, 128), 1) >> shift) & (L - 1)
    sub_h = _iota((HEADS, 128), 0)
    lse_t = jnp.zeros((HEADS, 128), f32)
    ms = []
    for c in range(NCH):
        for copy in qs[c]:
            copy.wait_recv()
        for h in range(c * CW // D, (c + 1) * CW // D):
            cols = slice(h * D, (h + 1) * D)
            within = slice(h * D - c * CW, (h + 1) * D - c * CW)
            asked = [queries[c][whose[b], :, within].astype(f32) for b in range(L)]
            asked = jnp.concatenate(
                [asked[b][e * CAP : (e + 1) * CAP] for e in range(H) for b in range(L)], axis=0
            ).astype(bf)
            scores = _dot_t(kv_v[0, 0, :, cols], asked)
            for b in range(1, L):
                scores = jnp.where(lane_block == b, _dot_t(kv_v[b, 0, :, cols], asked), scores)
            scores = scores * scale
            top = jnp.max(scores, axis=0, keepdims=True)
            weights = jnp.exp(scores - top)
            total = jnp.sum(weights, axis=0, keepdims=True)
            lse_t = jnp.where(sub_h == h, top + jnp.log(total), lse_t)
            weights = (weights * (1.0 / total)).T
            mixed = []
            for b in range(L):
                rows = jnp.concatenate(
                    [weights[(e * L + b) * CAP : (e * L + b + 1) * CAP] for e in range(H)], axis=0
                )
                mixed.append(_dot(rows.astype(bf), kv_v[b, 1, :, cols]))
            for e in range(H):
                snd_m[e, :, cols] = jnp.concatenate(
                    [mixed[b][e * CAP : (e + 1) * CAP] for b in range(L)], axis=0
                ).astype(bf)
        if c == NCH - 1:
            rcv_l[me] = lse_t
            for d in range(1, H):
                snd_l[d] = pltpu.roll(lse_t, (128 - L * CAP * d) % 128, 1)
            ls = [
                send(snd_l.at[d], rcv_l.at[me], l_s.at[d], l_r.at[d], "hosts", d)
                for d in range(1, H)
            ]
        span = pl.ds(c * CW, CW)
        ms.append(
            [
                send(
                    snd_m.at[other("hosts", d), :, span], rcv_m.at[me, :, span],
                    m_s.at[c, d], m_r.at[c, d], "hosts", d,
                )
                for d in range(1, H)
            ]
        )
    rcv_m[me] = snd_m[me]

    locals_[3].wait()
    N = gen_v.shape[0]
    lane_n, sub_n = _iota((A, N), 1), _iota((A, N), 0)
    mine = ((lane_n >> (SUF.bit_length())) == sub_n) & ((lane_n & (2 * SUF - 1)) < SUF)
    own_top, own_total, own_self = [], [], []
    for h in range(HEADS):
        cols = slice(h * D, (h + 1) * D)
        c, start = (h * D) // CW, (h * D) % CW
        query = _dot(fetch, queries[c][:, :, start : start + D].reshape(H * S, D))
        scores = _dot_t(query.astype(bf), gen_v[:, cols]) * scale
        scores = jnp.where(mine, scores, NEG_FILL)
        self_score = jnp.sum(query * keys[h], axis=1, keepdims=True) * scale
        top = jnp.maximum(jnp.max(scores, axis=1, keepdims=True), self_score)
        weights = jnp.where(mine, jnp.exp(scores - top), 0.0)
        self_weight = jnp.exp(self_score - top)
        own_top.append(top)
        own_total.append(jnp.sum(weights, axis=1, keepdims=True) + self_weight)
        own_mix[:, cols] = (
            _dot(pltpu.roll(weights, SUF, 1).astype(bf), gen_v[:, cols])
        )
        own_self.append(self_weight.astype(bf).astype(f32))

    locals_[6].wait()
    for copy in vs:
        copy.wait_recv()
    dv = rcv_v[...].astype(f32)
    dv_att = [
        _dot(
            unpack,
            jnp.concatenate([dv[p, k * CAP : (k + 1) * CAP] for p in range(H)], axis=0).astype(bf),
        )
        for k in range(2)
    ]
    for h in range(HEADS):
        cols = slice(h * D, (h + 1) * D)
        k, off = (h * D) // W2, (h * D) % W2
        value = (base_v[:, cols].astype(f32) + dv_att[k][:, off : off + D]).astype(bf).astype(f32)
        val_out[:, cols] = jnp.where(live_c, value, 0.0).astype(bf)
        own_mix[:, cols] += own_self[h] * value

    for copy in ls:
        copy.wait_recv()
    lse = jnp.zeros((HEADS, 128), f32)
    lane_h = _iota((HEADS, 128), 1)
    for g in range(H):
        lse = jnp.where((lane_h >= g * L * CAP) & (lane_h < (g + 1) * L * CAP), rcv_l[g], lse)
    for c in range(NCH):
        for copy in ms[c]:
            copy.wait_recv()
        for h in range(c * CW // D, (c + 1) * CW // D):
            cols = slice(h * D, (h + 1) * D)
            logs = jnp.where(used, lse[h : h + 1], NEG_FILL)
            top = jnp.maximum(jnp.max(logs, axis=1, keepdims=True), own_top[h])
            factor = jnp.where(used, jnp.exp(logs - top), 0.0)
            own_factor = jnp.exp(own_top[h] - top)
            inverse = 1.0 / (jnp.sum(factor, axis=1, keepdims=True) + own_total[h] * own_factor)
            result = _dot(
                (factor * inverse).astype(bf), rcv_m[:, :, cols].reshape(H * L * CAP, D)
            ) + own_mix[:, cols] * (own_factor * inverse)
            out[:, cols] = jnp.where(live_c, result, 0.0).astype(bf)
    for copies in [hs, bqs, ps, vs, ls] + qs + ms:
        for copy in copies:
            copy.wait_send()


def write_kernel(*refs):
    sems = refs[6]
    copies = [pltpu.make_async_copy(refs[i], refs[3 + i], sems.at[i]) for i in range(3)]
    for copy in copies:
        copy.start()
    for copy in copies:
        copy.wait()


def fused_body(
    hidden, base_q, base_k, base_v, a_in, b_out, cache, generated, thm, live, apr, ppr, cnt
):
    H, MP = lax.axis_size("hosts"), lax.axis_size("mp")
    A, W = hidden.shape
    CAP = A // H
    L, SUF = cache.shape[0], generated.shape[2]
    HEADS = W // HEAD_SIZE
    S = H * CAP
    NCH = 4
    bf, f32 = jnp.bfloat16, jnp.float32
    N = generated.shape[0] * 2 * SUF
    sizes = (H, MP, A, CAP, L, apr.shape[0], ppr.shape[1], HEADS, SUF, NCH)
    smem = pl.BlockSpec(memory_space=pltpu.SMEM)
    vmem = pl.BlockSpec(memory_space=pltpu.VMEM)
    hbm = pl.BlockSpec(memory_space=pl.ANY)
    fold = (H, 2 * CAP, W // 2)
    sem = lambda *shape: pltpu.SemaphoreType.DMA(shape)
    results = pl.pallas_call(
        functools.partial(fused_kernel, sizes),
        out_shape=[pltpu.VMEM((A, W), bf)] * 3,
        in_specs=[smem] * 4 + [vmem] * 2 + [hbm] * 7,
        out_specs=[vmem] * 3,
        scratch_shapes=[
            pltpu.SMEM(live.shape, jnp.int32),
            pltpu.VMEM((A, W), bf),
            pltpu.VMEM((A, W), bf),
            pltpu.VMEM(a_in.shape, bf),
            pltpu.VMEM(b_out.shape, bf),
            pltpu.VMEM(cache.shape, bf),
            pltpu.VMEM((N, W), bf),
            pltpu.VMEM(fold, bf),
            pltpu.VMEM(fold, bf),
            pltpu.VMEM(fold, bf),
            pltpu.VMEM(fold, bf),
            pltpu.VMEM((MP, S, 128), f32),
            pltpu.VMEM(fold, bf),
            pltpu.VMEM(fold, bf),
            pltpu.VMEM((H, L * CAP, W), bf),
            pltpu.VMEM((H, L * CAP, W), bf),
            pltpu.VMEM((H, HEADS, 128), f32),
            pltpu.VMEM((H, HEADS, 128), f32),
            pltpu.VMEM((A, W), f32),
            sem(7), sem(H), sem(H), sem(H), sem(H), sem(MP), sem(MP),
            sem(NCH, H), sem(NCH, H), sem(H), sem(H), sem(NCH, H), sem(NCH, H), sem(H), sem(H),
        ]
        + [pltpu.VMEM((H, S, W // NCH), bf)] * NCH,
        compiler_params=pltpu.CompilerParams(
            collective_id=0, has_side_effects=True, vmem_limit_bytes=60 * 1024 * 1024
        ),
        cost_estimate=pl.CostEstimate(
            flops=2 * 10**8, bytes_accessed=4 * 10**6, transcendentals=10**6
        ),
    )(
        thm, apr, ppr, cnt, hidden, base_q, live, base_k, base_v, a_in, b_out, cache,
        generated.reshape(N, W),
    )
    return pl.pallas_call(
        write_kernel,
        out_shape=[jax.ShapeDtypeStruct((A, W), bf)] * 3,
        in_specs=[vmem] * 3,
        out_specs=[hbm] * 3,
        scratch_shapes=[sem(3)],
        compiler_params=pltpu.CompilerParams(vmem_limit_bytes=2**20),
    )(*results)


def step(hidden, base_q, base_k, base_v, a_in, b_out, cache, generated, thm, live, apr, ppr, cnt):
    H = lax.axis_size("hosts")
    A, W = hidden.shape
    capacity = A // H
    fits = (
        capacity == 8
        and H <= 8
        and A <= 128
        and a_in.shape[0] == 1
        and A * cache.shape[0] == 128
        and cache.shape[0] == 4
        and cache.shape[2] == 128
        and H * A == 128
        and W == 8 * HEAD_SIZE
        and generated.shape[2] == 8
        and apr.shape[0] < 8
    )
    run = fused_body if fits else body
    return run(hidden, base_q, base_k, base_v, a_in, b_out, cache, generated, thm, live, apr, ppr, cnt)


def solution(mesh):
    placed = (
        P(("groups", "hosts"), "mp"),
        P(("groups", "hosts"), "mp"),
        P(("groups", "hosts"), "mp"),
        P(("groups", "hosts"), "mp"),
        P(("groups", "hosts"), "mp", None),
        P(("groups", "hosts"), None, None, "mp"),
        P(("groups", "hosts"), None, None, "mp"),
        P(("groups", "hosts"), None, None, "mp"),
        P(("groups", "hosts")),
        P(("groups", "hosts")),
        P("groups"),
        P("groups", None),
        P("groups"),
    )
    return jax.shard_map(
        step,
        mesh=mesh,
        in_specs=placed,
        out_specs=(
            P(("groups", "hosts"), "mp"),
            P(("groups", "hosts"), "mp"),
            P(("groups", "hosts"), "mp"),
        ),
        check_vma=False,
    )
```

```python
import functools
import math

import jax
import jax.numpy as jnp
from jax import lax
from jax.experimental import pallas as pl
from jax.experimental.pallas import tpu as pltpu
from jax.sharding import PartitionSpec as P

HEAD_SIZE = 128
ADAPTER_RANK = 64
BLK = 128
PBLK = 4


ADAPTER_SCALE = 0.5
ROPE_BASE = 10000.0
NEG_FILL = -1e30
MESH = pl.DeviceIdType.MESH


def rotate(values, position):
    shaped = values.reshape(values.shape[:-1] + (-1, HEAD_SIZE))
    halfway = HEAD_SIZE // 2
    frequency = ROPE_BASE ** (-(jnp.arange(halfway, dtype=jnp.float32) * (2.0 / HEAD_SIZE)))
    angles = position.astype(jnp.float32)[..., None] * frequency
    cosine = jnp.cos(angles)[..., None, :]
    sine_part = jnp.sin(angles)[..., None, :]
    first_half = shaped[..., :halfway]
    second = shaped[..., halfway:]
    turned = jnp.concatenate(
        [first_half * cosine - second * sine_part, second * cosine + first_half * sine_part],
        axis=-1,
    )
    return turned.reshape(values.shape)


def lookup_table(source_table, wanted):
    matches = wanted[:, None] == jnp.arange(source_table.shape[0], dtype=jnp.int32)[None, :]
    if source_table.ndim == 1:
        return jnp.sum(jnp.where(matches, source_table[None, :], 0), axis=1)
    return jnp.sum(jnp.where(matches[:, :, None], source_table[None, :, :], 0), axis=1)


def route_matrix(destination, validity, capacity, host_total):
    ordinal = jnp.arange(destination.shape[0], dtype=jnp.int32)
    earlier = (
        (destination[:, None] == destination[None, :])
        & validity[None, :]
        & (ordinal[None, :] < ordinal[:, None])
    )
    ranking = jnp.sum(earlier.astype(jnp.int32), axis=1)
    target = destination * capacity + ranking
    places = jnp.arange(host_total * capacity, dtype=jnp.int32)
    return ((places[:, None] == target[None, :]) & validity[None, :]).astype(jnp.bfloat16)


def pack_rows(router, payload):
    return jnp.dot(router, payload, preferred_element_type=jnp.float32).astype(jnp.bfloat16)


def attend_local(queries, chosen, statement_prefix_cache):
    head_count = queries.shape[-1] // HEAD_SIZE
    blocks = statement_prefix_cache.shape[0]
    block_keys = statement_prefix_cache[:, 0].reshape(
        blocks, statement_prefix_cache.shape[2], head_count, HEAD_SIZE
    )
    block_values = statement_prefix_cache[:, 1].reshape(
        blocks, statement_prefix_cache.shape[2], head_count, HEAD_SIZE
    )
    shaped = queries.reshape(queries.shape[:-1] + (head_count, HEAD_SIZE))
    scores = jnp.einsum(
        "nchd,bthd->ncbht", shaped, block_keys, preferred_element_type=jnp.float32
    ) * HEAD_SIZE ** (-0.5)
    chosen_mask = (chosen > 0)[:, :, :, None, None]
    masked = jnp.where(chosen_mask, scores, NEG_FILL)
    top_score = jnp.max(masked, axis=(2, 4))
    weights = jnp.where(chosen_mask, jnp.exp(masked - top_score[:, :, None, :, None]), 0.0)
    totals = jnp.sum(weights, axis=(2, 4))
    mixed_rows = jnp.einsum(
        "ncbht,bthd->nchd",
        weights.astype(jnp.bfloat16),
        block_values,
        preferred_element_type=jnp.float32,
    )
    return (mixed_rows.reshape(queries.shape), top_score, totals)


def body(
    hidden,
    base_query_projection,
    base_key_projection,
    base_value_projection,
    adapter_input_factors,
    adapter_output_factors,
    statement_prefix_cache,
    generated_token_cache,
    attempt_theorem_index,
    host_live_count,
    adapter_pool_row,
    prefix_pool_row,
    prefix_block_count,
):
    host_total = lax.axis_size("hosts")
    attempts = hidden.shape[0]
    capacity = max(1, attempts // host_total)
    owner_held_rows = adapter_input_factors.shape[0]
    local_blocks = statement_prefix_cache.shape[0]
    row_width = base_query_projection.shape[1]
    head_count = row_width // HEAD_SIZE
    ordinal = jnp.arange(attempts, dtype=jnp.int32)
    living = ordinal < host_live_count[0]
    adapter_rows = lookup_table(adapter_pool_row, attempt_theorem_index)
    block_rows = lookup_table(prefix_pool_row, attempt_theorem_index)
    block_counts = lookup_table(prefix_block_count, attempt_theorem_index)
    position = BLK * block_counts + generated_token_cache.shape[2]
    adapter_router = route_matrix(adapter_rows // owner_held_rows, living, capacity, host_total)
    adapter_pick = (
        adapter_rows[:, None] % owner_held_rows
        == jnp.arange(owner_held_rows, dtype=jnp.int32)[None, :]
    ).astype(jnp.bfloat16)
    sent_hidden = pack_rows(adapter_router, hidden).reshape(host_total, capacity, hidden.shape[1])
    sent_pick = pack_rows(adapter_router, adapter_pick).reshape(
        host_total, capacity, owner_held_rows
    )
    incoming_rows = lax.all_to_all(sent_hidden, "hosts", split_axis=0, concat_axis=0, tiled=True)
    pick_in = lax.all_to_all(sent_pick, "hosts", split_axis=0, concat_axis=0, tiled=True)
    projected_rows = jnp.einsum(
        "xjp,epk->xjek", incoming_rows, adapter_input_factors, preferred_element_type=jnp.float32
    )
    partial_rank = jnp.sum(projected_rows * pick_in.astype(jnp.float32)[..., None], axis=2)
    rank_rows = lax.psum(partial_rank, "mp").astype(jnp.bfloat16)
    spread_rows = rank_rows[:, :, None, :] * pick_in[..., None]
    query_correction = jnp.einsum(
        "exqw,qwf->exf",
        spread_rows[..., :ADAPTER_RANK],
        adapter_output_factors[:, 0],
        preferred_element_type=jnp.float32,
    )
    value_correction = jnp.einsum(
        "exqw,qwf->exf",
        spread_rows[..., ADAPTER_RANK:],
        adapter_output_factors[:, 1],
        preferred_element_type=jnp.float32,
    )
    adapter_corrections = (
        jnp.concatenate([query_correction, value_correction], axis=-1) * ADAPTER_SCALE
    ).astype(jnp.bfloat16)
    returned = lax.all_to_all(adapter_corrections, "hosts", split_axis=0, concat_axis=0, tiled=True)
    adapter_corrections = jnp.dot(
        adapter_router.T,
        returned.reshape(host_total * capacity, 2 * row_width),
        preferred_element_type=jnp.float32,
    )
    query_rows = rotate(
        base_query_projection.astype(jnp.float32) + adapter_corrections[:, :row_width], position
    ).astype(jnp.bfloat16)
    value_rows = (
        base_value_projection.astype(jnp.float32) + adapter_corrections[:, row_width:]
    ).astype(jnp.bfloat16)
    key_rows = rotate(base_key_projection.astype(jnp.float32), position).astype(jnp.bfloat16)
    requests = []
    for block_index in range(PBLK):
        wanted = living & (block_index < block_counts)
        holder = block_rows[:, block_index]
        router = route_matrix(holder // local_blocks, wanted, capacity, host_total)
        block_pick = (
            holder[:, None] % local_blocks == jnp.arange(local_blocks, dtype=jnp.int32)[None, :]
        ).astype(jnp.bfloat16)
        sent_queries = pack_rows(router, query_rows).reshape(host_total, capacity, row_width)
        sent_blocks = pack_rows(router, block_pick).reshape(host_total, capacity, local_blocks)
        requests.append((router, wanted, sent_queries, sent_blocks))
    partials = []
    for request in requests:
        answer_mixed_rows, answer_top_score, answer_totals = attend_local(
            lax.all_to_all(request[2], "hosts", split_axis=0, concat_axis=0, tiled=True),
            lax.all_to_all(request[3], "hosts", split_axis=0, concat_axis=0, tiled=True),
            statement_prefix_cache,
        )
        partials.append(
            (
                lax.all_to_all(answer_mixed_rows, "hosts", split_axis=0, concat_axis=0, tiled=True),
                lax.all_to_all(answer_top_score, "hosts", split_axis=0, concat_axis=0, tiled=True),
                lax.all_to_all(answer_totals, "hosts", split_axis=0, concat_axis=0, tiled=True),
            )
        )
    entries = []
    for block_index in range(PBLK):
        router, wanted = (requests[block_index][0], requests[block_index][1])
        mixed_rows, top_score, totals = partials[block_index]
        back_router = router.T.astype(jnp.float32)
        flat_mixed = jnp.dot(
            back_router,
            mixed_rows.reshape(host_total * capacity, row_width),
            precision=lax.Precision.HIGHEST,
        )
        flat_top = jnp.dot(
            back_router,
            top_score.reshape(host_total * capacity, head_count),
            precision=lax.Precision.HIGHEST,
        )
        flat_totals = jnp.dot(
            back_router,
            totals.reshape(host_total * capacity, head_count),
            precision=lax.Precision.HIGHEST,
        )
        flat_top = jnp.where(wanted[:, None], flat_top, NEG_FILL)
        entries.append((flat_mixed, flat_top, flat_totals))
    shaped_query = query_rows.reshape(attempts, head_count, HEAD_SIZE)
    own_keys = jnp.concatenate([generated_token_cache[:, 0], key_rows[:, None, :]], axis=1).reshape(
        attempts, -1, head_count, HEAD_SIZE
    )
    own_values = jnp.concatenate(
        [generated_token_cache[:, 1], value_rows[:, None, :]], axis=1
    ).reshape(attempts, -1, head_count, HEAD_SIZE)
    own_scores = jnp.einsum(
        "ahd,athd->aht", shaped_query, own_keys, preferred_element_type=jnp.float32
    ) * HEAD_SIZE ** (-0.5)
    own_top = jnp.max(own_scores, axis=2)
    own_weights = jnp.exp(own_scores - own_top[..., None])
    own_totals = jnp.sum(own_weights, axis=2)
    own_mixed = jnp.einsum(
        "aht,athd->ahd",
        own_weights.astype(jnp.bfloat16),
        own_values,
        preferred_element_type=jnp.float32,
    )
    overall = own_top
    for flat_mixed, flat_top, flat_totals in entries:
        overall = jnp.maximum(overall, flat_top)
    own_factor = jnp.exp(own_top - overall)
    numerator = own_mixed * own_factor[..., None]
    denominator = own_totals * own_factor
    for flat_mixed, flat_top, flat_totals in entries:
        factor = jnp.exp(flat_top - overall)
        numerator = (
            numerator + flat_mixed.reshape(attempts, head_count, HEAD_SIZE) * factor[..., None]
        )
        denominator = denominator + flat_totals * factor
    attended = (numerator / denominator[..., None]).reshape(attempts, row_width)
    live_rows = living[:, None]
    return (
        jnp.where(live_rows, attended, 0.0).astype(jnp.bfloat16),
        jnp.where(live_rows, key_rows, 0.0),
        jnp.where(live_rows, value_rows, 0.0),
    )


def _iota(shape, dim):
    return lax.broadcasted_iota(jnp.int32, shape, dim)


def _dot(a, b):
    return jnp.dot(a, b, preferred_element_type=jnp.float32)


def _dot_t(a, b):
    return lax.dot_general(a, b, (((1,), (1,)), ((), ())), preferred_element_type=jnp.float32)


def fused_kernel(
    sizes,
    thm_hbm, apr_hbm, ppr_hbm, cnt_hbm,
    hid_hbm, bq_hbm, live_hbm, k_hbm, val_hbm, a_hbm, b_hbm, kv_hbm, gen_hbm,
    out, key_out, val_out,
    thm, apr, ppr, cnt, hidden, base_q, live, base_k, base_v, a_v, b_v, kv_v, gen_v,
    snd_h, rcv_h, snd_q, rcv_q, part, snd_v, rcv_v, snd_m, rcv_m, snd_l, rcv_l, own_mix,
    local_sem, h_s, h_r, bq_s, bq_r, p_s, p_r, q_s, q_r, v_s, v_r, m_s, m_r, l_s, l_r,
    *queries,
):
    H, MP, A, CAP, L, T, PB, HEADS, SUF, NCH = sizes
    f32, bf = jnp.float32, jnp.bfloat16
    D = HEAD_SIZE
    W = HEADS * D
    W2 = W // 2
    S = H * CAP
    CW = W // NCH
    shift = CAP.bit_length() - 1
    me = lax.axis_index("hosts")
    mme = lax.axis_index("mp")

    def other(axis, d):
        return lax.rem((me if axis == "hosts" else mme) + d, H if axis == "hosts" else MP)

    locals_ = [
        pltpu.make_async_copy(src, dst, local_sem.at[i])
        for i, (src, dst) in enumerate(
            [
                (a_hbm, a_v), (b_hbm, b_v), (kv_hbm, kv_v), (gen_hbm, gen_v),
                (live_hbm, live), (k_hbm, base_k), (val_hbm, base_v),
                (thm_hbm, thm), (apr_hbm, apr), (ppr_hbm, ppr), (cnt_hbm, cnt),
                (hid_hbm, hidden), (bq_hbm, base_q),
            ]
        )
    ]

    barrier = pltpu.get_barrier_semaphore()
    for d in range(1, H):
        pl.semaphore_signal(barrier, inc=1, device_id={"hosts": other("hosts", d)}, device_id_type=MESH)
    for d in range(1, MP):
        pl.semaphore_signal(barrier, inc=1, device_id={"mp": other("mp", d)}, device_id_type=MESH)

    for i in (7, 8, 4, 11, 12, 0, 9, 10, 1, 2, 5, 6, 3):
        locals_[i].start()

    def send(src, dst, s, r, axis, d):
        copy = pltpu.make_async_remote_copy(
            src_ref=src, dst_ref=dst, send_sem=s, recv_sem=r,
            device_id={axis: other(axis, d)}, device_id_type=MESH,
        )
        copy.start()
        return copy

    lane8, sub8 = _iota((8, 128), 1), _iota((8, 128), 0)
    th = jnp.full((8, 128), -1, jnp.int32)
    locals_[7].wait()
    locals_[8].wait()
    for a in range(A):
        th = jnp.where(lane8 == a, thm[a], th)
    owner = jnp.full((8, 128), -1, jnp.int32)
    for t in range(T):
        owner = jnp.where(th == t, apr[t], owner)
    locals_[4].wait()
    n_live = live[0]
    owner = jnp.where(lane8 < n_live, owner, -1)
    member = jnp.where(owner == sub8, 1.0, 0.0).astype(f32)
    before = jnp.where(_iota((128, 128), 0) < _iota((128, 128), 1), 1.0, 0.0).astype(bf)
    rank_f = jnp.sum(member * _dot(member.astype(bf), before), axis=0, keepdims=True)
    rank_row = rank_f.astype(jnp.int32)
    target = jnp.where(owner[0:1] >= 0, owner[0:1] * CAP + rank_row, -1)
    router = jnp.where(_iota((S, A), 0) == target[:, :A], 1.0, 0.0).astype(bf)

    def folded(rows, e):
        piece = rows[e * CAP : (e + 1) * CAP]
        return jnp.concatenate([piece[:, :W2], piece[:, W2:]], axis=0)

    locals_[11].wait()
    packed = _dot(router, hidden[...])
    for e in range(H):
        snd_h[e] = folded(packed, e).astype(bf)
    pl.semaphore_wait(barrier, H - 1 + MP - 1)
    hs = [
        send(snd_h.at[other("hosts", d)], rcv_h.at[me], h_s.at[d], h_r.at[d], "hosts", d)
        for d in range(1, H)
    ]
    locals_[12].wait()
    packed = _dot(router, base_q[...])
    for e in range(H):
        snd_q[e] = folded(packed, e).astype(bf)
    bqs = [
        send(snd_q.at[other("hosts", d)], rcv_q.at[me], bq_s.at[d], bq_r.at[d], "hosts", d)
        for d in range(1, H)
    ]
    rcv_h[me] = snd_h[me]
    rcv_q[me] = snd_q[me]

    locals_[9].wait()
    locals_[10].wait()
    lane = _iota((8, 128), 1)
    half = jnp.where(lane < D // 2, lane, lane - D // 2).astype(f32)
    freq = jnp.exp(half * (-2.0 / D * math.log(ROPE_BASE)))
    counts = jnp.zeros((8, 128), jnp.int32)
    my_count = jnp.int32(0)
    for t in range(T):
        counts = jnp.where(sub8 == t, cnt[t], counts)
        my_count = jnp.where(apr[t] == me, cnt[t], my_count)
    counts = jnp.where(sub8 == T, my_count, counts)
    angle = (BLK * counts + SUF).astype(f32) * freq
    cos_t = jnp.cos(angle)
    sin_t = jnp.sin(angle)
    sin_t = jnp.where(lane < D // 2, -sin_t, sin_t)

    def turn(x, c, s):
        return x * c + pltpu.roll(x, D // 2, 1) * s

    locals_[0].wait()
    for copy in hs:
        copy.wait_recv()
    rows = rcv_h[...].reshape(H * 2 * CAP, W2)
    left = _dot(rows, a_v[0, :W2, :])
    right = _dot(rows, a_v[0, W2:, :])
    part[mme] = jnp.concatenate(
        [
            left[2 * CAP * e : 2 * CAP * e + CAP] + right[2 * CAP * e + CAP : 2 * CAP * (e + 1)]
            for e in range(H)
        ],
        axis=0,
    )
    ps = [
        send(part.at[mme], part.at[mme], p_s.at[d], p_r.at[d], "mp", d) for d in range(1, MP)
    ]
    for copy in bqs:
        copy.wait_recv()
    bq = rcv_q[...].astype(f32)
    bq_half = [
        jnp.concatenate([bq[e, k * CAP : (k + 1) * CAP] for e in range(H)], axis=0)
        for k in range(2)
    ]
    locals_[1].wait()
    for copy in ps:
        copy.wait_recv()
    ranks = part[0]
    for m in range(1, MP):
        ranks = ranks + part[m]
    ranks = ranks.astype(bf).astype(f32)
    rank_q = ranks[:, :ADAPTER_RANK].astype(bf)
    rank_v = pltpu.roll(ranks, ADAPTER_RANK, 1)[:, :ADAPTER_RANK].astype(bf)
    qs = []
    for c in range(NCH):
        cols = slice(c * CW, (c + 1) * CW)
        delta = (_dot(rank_q, b_v[0, 0, :, cols]) * ADAPTER_SCALE).astype(bf).astype(f32)
        k, off = (c * CW) // W2, (c * CW) % W2
        raw = bq_half[k][:, off : off + CW] + delta
        for h in range(CW // D):
            queries[c][me, :, h * D : (h + 1) * D] = turn(
                raw[:, h * D : (h + 1) * D], cos_t[T : T + 1], sin_t[T : T + 1]
            ).astype(bf)
        view = queries[c].at[me]
        qs.append(
            [send(view, view, q_s.at[c, d], q_r.at[c, d], "hosts", d) for d in range(1, H)]
        )
    delta = _dot(rank_v, b_v[0, 1]) * ADAPTER_SCALE
    for e in range(H):
        snd_v[e] = folded(delta, e).astype(bf)
    vs = [
        send(snd_v.at[other("hosts", d)], rcv_v.at[me], v_s.at[d], v_r.at[d], "hosts", d)
        for d in range(1, H)
    ]
    rcv_v[me] = snd_v[me]

    sub128 = _iota((128, 128), 0)
    both = jnp.where(sub128 == 0, th[0:1].astype(f32), jnp.where(sub128 == 1, rank_f, 0.0))
    turned = both.T[:A].astype(jnp.int32)
    th_c, rank_c = turned[:, 0:1], turned[:, 1:2]
    lane_a = _iota((A, 128), 1)
    live_c = _iota((A, 1), 0) < n_live
    owner_c = jnp.full((A, 1), -1, jnp.int32)
    cos_a = jnp.zeros((A, 128), f32)
    sin_a = jnp.zeros((A, 128), f32)
    blocks_c = [jnp.full((A, 1), -1, jnp.int32) for _ in range(PB)]
    for t in range(T):
        here = th_c == t
        owner_c = jnp.where(here, apr[t], owner_c)
        cos_a = jnp.where(here, cos_t[t : t + 1], cos_a)
        sin_a = jnp.where(here, sin_t[t : t + 1], sin_a)
        for j in range(PB):
            blocks_c[j] = jnp.where(here, jnp.where(j < cnt[t], ppr[t, j], -1), blocks_c[j])
    owner_c = jnp.where(live_c, owner_c, -1)
    slot_ok = jnp.where(rank_c == (lane_a & (CAP - 1)), 1, 0)
    group = lane_a >> shift
    used = jnp.zeros((A, 128), jnp.int32)
    for j in range(PB):
        used = used + jnp.where(blocks_c[j] == group, 1, 0)
    used = jnp.where(live_c, used * slot_ok, 0) > 0
    fetch = jnp.where(owner_c * H + me == group, slot_ok, 0).astype(f32).astype(bf)
    unpack = jnp.where(
        owner_c * CAP + rank_c == _iota((A, S), 1), jnp.where(owner_c >= 0, 1.0, 0.0), 0.0
    ).astype(bf)
    keys = []
    locals_[5].wait()
    for h in range(HEADS):
        cols = slice(h * D, (h + 1) * D)
        key = turn(base_k[:, cols].astype(f32), cos_a, sin_a).astype(bf).astype(f32)
        keys.append(key)
        key_out[:, cols] = jnp.where(live_c, key, 0.0).astype(bf)

    whose = []
    for b in range(L):
        index = jnp.int32(0)
        for t in range(T):
            for j in range(PB):
                index = jnp.where(ppr[t, j] == me * L + b, apr[t], index)
        whose.append(index)
    scale = D ** (-0.5)
    locals_[2].wait()
    lane_block = (_iota((128, 128), 1) >> shift) & (L - 1)
    sub_h = _iota((HEADS, 128), 0)
    lse_t = jnp.zeros((HEADS, 128), f32)
    ms = []
    for c in range(NCH):
        for copy in qs[c]:
            copy.wait_recv()
        for h in range(c * CW // D, (c + 1) * CW // D):
            cols = slice(h * D, (h + 1) * D)
            within = slice(h * D - c * CW, (h + 1) * D - c * CW)
            asked = [queries[c][whose[b], :, within].astype(f32) for b in range(L)]
            asked = jnp.concatenate(
                [asked[b][e * CAP : (e + 1) * CAP] for e in range(H) for b in range(L)], axis=0
            ).astype(bf)
            scores = _dot_t(kv_v[0, 0, :, cols], asked)
            for b in range(1, L):
                scores = jnp.where(lane_block == b, _dot_t(kv_v[b, 0, :, cols], asked), scores)
            scores = scores * scale
            top = jnp.max(scores, axis=0, keepdims=True)
            weights = jnp.exp(scores - top)
            total = jnp.sum(weights, axis=0, keepdims=True)
            lse_t = jnp.where(sub_h == h, top + jnp.log(total), lse_t)
            weights = (weights * (1.0 / total)).T
            mixed = []
            for b in range(L):
                rows = jnp.concatenate(
                    [weights[(e * L + b) * CAP : (e * L + b + 1) * CAP] for e in range(H)], axis=0
                )
                mixed.append(_dot(rows.astype(bf), kv_v[b, 1, :, cols]))
            for e in range(H):
                snd_m[e, :, cols] = jnp.concatenate(
                    [mixed[b][e * CAP : (e + 1) * CAP] for b in range(L)], axis=0
                ).astype(bf)
        if c == NCH - 1:
            rcv_l[me] = lse_t
            for d in range(1, H):
                snd_l[d] = pltpu.roll(lse_t, (128 - L * CAP * d) % 128, 1)
            ls = [
                send(snd_l.at[d], rcv_l.at[me], l_s.at[d], l_r.at[d], "hosts", d)
                for d in range(1, H)
            ]
        span = pl.ds(c * CW, CW)
        ms.append(
            [
                send(
                    snd_m.at[other("hosts", d), :, span], rcv_m.at[me, :, span],
                    m_s.at[c, d], m_r.at[c, d], "hosts", d,
                )
                for d in range(1, H)
            ]
        )
    rcv_m[me] = snd_m[me]

    locals_[3].wait()
    N = gen_v.shape[0]
    lane_n, sub_n = _iota((A, N), 1), _iota((A, N), 0)
    mine = ((lane_n >> (SUF.bit_length())) == sub_n) & ((lane_n & (2 * SUF - 1)) < SUF)
    own_top, own_total, own_self = [], [], []
    for h in range(HEADS):
        cols = slice(h * D, (h + 1) * D)
        c, start = (h * D) // CW, (h * D) % CW
        query = _dot(fetch, queries[c][:, :, start : start + D].reshape(H * S, D))
        scores = _dot_t(query.astype(bf), gen_v[:, cols]) * scale
        scores = jnp.where(mine, scores, NEG_FILL)
        self_score = jnp.sum(query * keys[h], axis=1, keepdims=True) * scale
        top = jnp.maximum(jnp.max(scores, axis=1, keepdims=True), self_score)
        weights = jnp.where(mine, jnp.exp(scores - top), 0.0)
        self_weight = jnp.exp(self_score - top)
        own_top.append(top)
        own_total.append(jnp.sum(weights, axis=1, keepdims=True) + self_weight)
        own_mix[:, cols] = (
            _dot(pltpu.roll(weights, SUF, 1).astype(bf), gen_v[:, cols])
        )
        own_self.append(self_weight.astype(bf).astype(f32))

    locals_[6].wait()
    for copy in vs:
        copy.wait_recv()
    dv = rcv_v[...].astype(f32)
    dv_att = [
        _dot(
            unpack,
            jnp.concatenate([dv[p, k * CAP : (k + 1) * CAP] for p in range(H)], axis=0).astype(bf),
        )
        for k in range(2)
    ]
    for h in range(HEADS):
        cols = slice(h * D, (h + 1) * D)
        k, off = (h * D) // W2, (h * D) % W2
        value = (base_v[:, cols].astype(f32) + dv_att[k][:, off : off + D]).astype(bf).astype(f32)
        val_out[:, cols] = jnp.where(live_c, value, 0.0).astype(bf)
        own_mix[:, cols] += own_self[h] * value

    for copy in ls:
        copy.wait_recv()
    lse = jnp.zeros((HEADS, 128), f32)
    lane_h = _iota((HEADS, 128), 1)
    for g in range(H):
        lse = jnp.where((lane_h >= g * L * CAP) & (lane_h < (g + 1) * L * CAP), rcv_l[g], lse)
    for c in range(NCH):
        for copy in ms[c]:
            copy.wait_recv()
        for h in range(c * CW // D, (c + 1) * CW // D):
            cols = slice(h * D, (h + 1) * D)
            logs = jnp.where(used, lse[h : h + 1], NEG_FILL)
            top = jnp.maximum(jnp.max(logs, axis=1, keepdims=True), own_top[h])
            factor = jnp.where(used, jnp.exp(logs - top), 0.0)
            own_factor = jnp.exp(own_top[h] - top)
            inverse = 1.0 / (jnp.sum(factor, axis=1, keepdims=True) + own_total[h] * own_factor)
            result = _dot(
                (factor * inverse).astype(bf), rcv_m[:, :, cols].reshape(H * L * CAP, D)
            ) + own_mix[:, cols] * (own_factor * inverse)
            out[:, cols] = jnp.where(live_c, result, 0.0).astype(bf)
    for copies in [hs, bqs, ps, vs, ls] + qs + ms:
        for copy in copies:
            copy.wait_send()


def write_kernel(*refs):
    sems = refs[6]
    copies = [pltpu.make_async_copy(refs[i], refs[3 + i], sems.at[i]) for i in range(3)]
    for copy in copies:
        copy.start()
    for copy in copies:
        copy.wait()


def fused_body(
    hidden, base_q, base_k, base_v, a_in, b_out, cache, generated, thm, live, apr, ppr, cnt
):
    H, MP = lax.axis_size("hosts"), lax.axis_size("mp")
    A, W = hidden.shape
    CAP = A // H
    L, SUF = cache.shape[0], generated.shape[2]
    HEADS = W // HEAD_SIZE
    S = H * CAP
    NCH = 2
    bf, f32 = jnp.bfloat16, jnp.float32
    N = generated.shape[0] * 2 * SUF
    sizes = (H, MP, A, CAP, L, apr.shape[0], ppr.shape[1], HEADS, SUF, NCH)
    vmem = pl.BlockSpec(memory_space=pltpu.VMEM)
    hbm = pl.BlockSpec(memory_space=pl.ANY)
    fold = (H, 2 * CAP, W // 2)
    sem = lambda *shape: pltpu.SemaphoreType.DMA(shape)
    results = pl.pallas_call(
        functools.partial(fused_kernel, sizes),
        out_shape=[pltpu.VMEM((A, W), bf)] * 3,
        in_specs=[hbm] * 13,
        out_specs=[vmem] * 3,
        scratch_shapes=[
            pltpu.SMEM(thm.shape, jnp.int32),
            pltpu.SMEM(apr.shape, jnp.int32),
            pltpu.SMEM(ppr.shape, jnp.int32),
            pltpu.SMEM(cnt.shape, jnp.int32),
            pltpu.VMEM((A, W), bf),
            pltpu.VMEM((A, W), bf),
            pltpu.SMEM(live.shape, jnp.int32),
            pltpu.VMEM((A, W), bf),
            pltpu.VMEM((A, W), bf),
            pltpu.VMEM(a_in.shape, bf),
            pltpu.VMEM(b_out.shape, bf),
            pltpu.VMEM(cache.shape, bf),
            pltpu.VMEM((N, W), bf),
            pltpu.VMEM(fold, bf),
            pltpu.VMEM(fold, bf),
            pltpu.VMEM(fold, bf),
            pltpu.VMEM(fold, bf),
            pltpu.VMEM((MP, S, 128), f32),
            pltpu.VMEM(fold, bf),
            pltpu.VMEM(fold, bf),
            pltpu.VMEM((H, L * CAP, W), bf),
            pltpu.VMEM((H, L * CAP, W), bf),
            pltpu.VMEM((H, HEADS, 128), f32),
            pltpu.VMEM((H, HEADS, 128), f32),
            pltpu.VMEM((A, W), f32),
            sem(13), sem(H), sem(H), sem(H), sem(H), sem(MP), sem(MP),
            sem(NCH, H), sem(NCH, H), sem(H), sem(H), sem(NCH, H), sem(NCH, H), sem(H), sem(H),
        ]
        + [pltpu.VMEM((H, S, W // NCH), bf)] * NCH,
        compiler_params=pltpu.CompilerParams(
            collective_id=0, has_side_effects=True, vmem_limit_bytes=60 * 1024 * 1024
        ),
        cost_estimate=pl.CostEstimate(
            flops=2 * 10**8, bytes_accessed=4 * 10**6, transcendentals=10**6
        ),
    )(
        thm, apr, ppr, cnt, hidden, base_q, live, base_k, base_v, a_in, b_out, cache,
        generated.reshape(N, W),
    )
    return pl.pallas_call(
        write_kernel,
        out_shape=[jax.ShapeDtypeStruct((A, W), bf)] * 3,
        in_specs=[vmem] * 3,
        out_specs=[hbm] * 3,
        scratch_shapes=[sem(3)],
        compiler_params=pltpu.CompilerParams(vmem_limit_bytes=2**20),
    )(*results)


def step(hidden, base_q, base_k, base_v, a_in, b_out, cache, generated, thm, live, apr, ppr, cnt):
    H = lax.axis_size("hosts")
    A, W = hidden.shape
    capacity = A // H
    fits = (
        capacity == 8
        and H <= 8
        and A <= 128
        and a_in.shape[0] == 1
        and A * cache.shape[0] == 128
        and cache.shape[0] == 4
        and cache.shape[2] == 128
        and H * A == 128
        and W == 8 * HEAD_SIZE
        and generated.shape[2] == 8
        and apr.shape[0] < 8
    )
    run = fused_body if fits else body
    return run(hidden, base_q, base_k, base_v, a_in, b_out, cache, generated, thm, live, apr, ppr, cnt)


def solution(mesh):
    placed = (
        P(("groups", "hosts"), "mp"),
        P(("groups", "hosts"), "mp"),
        P(("groups", "hosts"), "mp"),
        P(("groups", "hosts"), "mp"),
        P(("groups", "hosts"), "mp", None),
        P(("groups", "hosts"), None, None, "mp"),
        P(("groups", "hosts"), None, None, "mp"),
        P(("groups", "hosts"), None, None, "mp"),
        P(("groups", "hosts")),
        P(("groups", "hosts")),
        P("groups"),
        P("groups", None),
        P("groups"),
    )
    return jax.shard_map(
        step,
        mesh=mesh,
        in_specs=placed,
        out_specs=(
            P(("groups", "hosts"), "mp"),
            P(("groups", "hosts"), "mp"),
            P(("groups", "hosts"), "mp"),
        ),
        check_vma=False,
    )
```

```python
import functools
import math

import jax
import jax.numpy as jnp
from jax import lax
from jax.experimental import pallas as pl
from jax.experimental.pallas import tpu as pltpu
from jax.sharding import PartitionSpec as P

HEAD_SIZE = 128
ADAPTER_RANK = 64
BLK = 128
PBLK = 4


ADAPTER_SCALE = 0.5
ROPE_BASE = 10000.0
NEG_FILL = -1e30
MESH = pl.DeviceIdType.MESH


def rotate(values, position):
    shaped = values.reshape(values.shape[:-1] + (-1, HEAD_SIZE))
    halfway = HEAD_SIZE // 2
    frequency = ROPE_BASE ** (-(jnp.arange(halfway, dtype=jnp.float32) * (2.0 / HEAD_SIZE)))
    angles = position.astype(jnp.float32)[..., None] * frequency
    cosine = jnp.cos(angles)[..., None, :]
    sine_part = jnp.sin(angles)[..., None, :]
    first_half = shaped[..., :halfway]
    second = shaped[..., halfway:]
    turned = jnp.concatenate(
        [first_half * cosine - second * sine_part, second * cosine + first_half * sine_part],
        axis=-1,
    )
    return turned.reshape(values.shape)


def lookup_table(source_table, wanted):
    matches = wanted[:, None] == jnp.arange(source_table.shape[0], dtype=jnp.int32)[None, :]
    if source_table.ndim == 1:
        return jnp.sum(jnp.where(matches, source_table[None, :], 0), axis=1)
    return jnp.sum(jnp.where(matches[:, :, None], source_table[None, :, :], 0), axis=1)


def route_matrix(destination, validity, capacity, host_total):
    ordinal = jnp.arange(destination.shape[0], dtype=jnp.int32)
    earlier = (
        (destination[:, None] == destination[None, :])
        & validity[None, :]
        & (ordinal[None, :] < ordinal[:, None])
    )
    ranking = jnp.sum(earlier.astype(jnp.int32), axis=1)
    target = destination * capacity + ranking
    places = jnp.arange(host_total * capacity, dtype=jnp.int32)
    return ((places[:, None] == target[None, :]) & validity[None, :]).astype(jnp.bfloat16)


def pack_rows(router, payload):
    return jnp.dot(router, payload, preferred_element_type=jnp.float32).astype(jnp.bfloat16)


def attend_local(queries, chosen, statement_prefix_cache):
    head_count = queries.shape[-1] // HEAD_SIZE
    blocks = statement_prefix_cache.shape[0]
    block_keys = statement_prefix_cache[:, 0].reshape(
        blocks, statement_prefix_cache.shape[2], head_count, HEAD_SIZE
    )
    block_values = statement_prefix_cache[:, 1].reshape(
        blocks, statement_prefix_cache.shape[2], head_count, HEAD_SIZE
    )
    shaped = queries.reshape(queries.shape[:-1] + (head_count, HEAD_SIZE))
    scores = jnp.einsum(
        "nchd,bthd->ncbht", shaped, block_keys, preferred_element_type=jnp.float32
    ) * HEAD_SIZE ** (-0.5)
    chosen_mask = (chosen > 0)[:, :, :, None, None]
    masked = jnp.where(chosen_mask, scores, NEG_FILL)
    top_score = jnp.max(masked, axis=(2, 4))
    weights = jnp.where(chosen_mask, jnp.exp(masked - top_score[:, :, None, :, None]), 0.0)
    totals = jnp.sum(weights, axis=(2, 4))
    mixed_rows = jnp.einsum(
        "ncbht,bthd->nchd",
        weights.astype(jnp.bfloat16),
        block_values,
        preferred_element_type=jnp.float32,
    )
    return (mixed_rows.reshape(queries.shape), top_score, totals)


def body(
    hidden,
    base_query_projection,
    base_key_projection,
    base_value_projection,
    adapter_input_factors,
    adapter_output_factors,
    statement_prefix_cache,
    generated_token_cache,
    attempt_theorem_index,
    host_live_count,
    adapter_pool_row,
    prefix_pool_row,
    prefix_block_count,
):
    host_total = lax.axis_size("hosts")
    attempts = hidden.shape[0]
    capacity = max(1, attempts // host_total)
    owner_held_rows = adapter_input_factors.shape[0]
    local_blocks = statement_prefix_cache.shape[0]
    row_width = base_query_projection.shape[1]
    head_count = row_width // HEAD_SIZE
    ordinal = jnp.arange(attempts, dtype=jnp.int32)
    living = ordinal < host_live_count[0]
    adapter_rows = lookup_table(adapter_pool_row, attempt_theorem_index)
    block_rows = lookup_table(prefix_pool_row, attempt_theorem_index)
    block_counts = lookup_table(prefix_block_count, attempt_theorem_index)
    position = BLK * block_counts + generated_token_cache.shape[2]
    adapter_router = route_matrix(adapter_rows // owner_held_rows, living, capacity, host_total)
    adapter_pick = (
        adapter_rows[:, None] % owner_held_rows
        == jnp.arange(owner_held_rows, dtype=jnp.int32)[None, :]
    ).astype(jnp.bfloat16)
    sent_hidden = pack_rows(adapter_router, hidden).reshape(host_total, capacity, hidden.shape[1])
    sent_pick = pack_rows(adapter_router, adapter_pick).reshape(
        host_total, capacity, owner_held_rows
    )
    incoming_rows = lax.all_to_all(sent_hidden, "hosts", split_axis=0, concat_axis=0, tiled=True)
    pick_in = lax.all_to_all(sent_pick, "hosts", split_axis=0, concat_axis=0, tiled=True)
    projected_rows = jnp.einsum(
        "xjp,epk->xjek", incoming_rows, adapter_input_factors, preferred_element_type=jnp.float32
    )
    partial_rank = jnp.sum(projected_rows * pick_in.astype(jnp.float32)[..., None], axis=2)
    rank_rows = lax.psum(partial_rank, "mp").astype(jnp.bfloat16)
    spread_rows = rank_rows[:, :, None, :] * pick_in[..., None]
    query_correction = jnp.einsum(
        "exqw,qwf->exf",
        spread_rows[..., :ADAPTER_RANK],
        adapter_output_factors[:, 0],
        preferred_element_type=jnp.float32,
    )
    value_correction = jnp.einsum(
        "exqw,qwf->exf",
        spread_rows[..., ADAPTER_RANK:],
        adapter_output_factors[:, 1],
        preferred_element_type=jnp.float32,
    )
    adapter_corrections = (
        jnp.concatenate([query_correction, value_correction], axis=-1) * ADAPTER_SCALE
    ).astype(jnp.bfloat16)
    returned = lax.all_to_all(adapter_corrections, "hosts", split_axis=0, concat_axis=0, tiled=True)
    adapter_corrections = jnp.dot(
        adapter_router.T,
        returned.reshape(host_total * capacity, 2 * row_width),
        preferred_element_type=jnp.float32,
    )
    query_rows = rotate(
        base_query_projection.astype(jnp.float32) + adapter_corrections[:, :row_width], position
    ).astype(jnp.bfloat16)
    value_rows = (
        base_value_projection.astype(jnp.float32) + adapter_corrections[:, row_width:]
    ).astype(jnp.bfloat16)
    key_rows = rotate(base_key_projection.astype(jnp.float32), position).astype(jnp.bfloat16)
    requests = []
    for block_index in range(PBLK):
        wanted = living & (block_index < block_counts)
        holder = block_rows[:, block_index]
        router = route_matrix(holder // local_blocks, wanted, capacity, host_total)
        block_pick = (
            holder[:, None] % local_blocks == jnp.arange(local_blocks, dtype=jnp.int32)[None, :]
        ).astype(jnp.bfloat16)
        sent_queries = pack_rows(router, query_rows).reshape(host_total, capacity, row_width)
        sent_blocks = pack_rows(router, block_pick).reshape(host_total, capacity, local_blocks)
        requests.append((router, wanted, sent_queries, sent_blocks))
    partials = []
    for request in requests:
        answer_mixed_rows, answer_top_score, answer_totals = attend_local(
            lax.all_to_all(request[2], "hosts", split_axis=0, concat_axis=0, tiled=True),
            lax.all_to_all(request[3], "hosts", split_axis=0, concat_axis=0, tiled=True),
            statement_prefix_cache,
        )
        partials.append(
            (
                lax.all_to_all(answer_mixed_rows, "hosts", split_axis=0, concat_axis=0, tiled=True),
                lax.all_to_all(answer_top_score, "hosts", split_axis=0, concat_axis=0, tiled=True),
                lax.all_to_all(answer_totals, "hosts", split_axis=0, concat_axis=0, tiled=True),
            )
        )
    entries = []
    for block_index in range(PBLK):
        router, wanted = (requests[block_index][0], requests[block_index][1])
        mixed_rows, top_score, totals = partials[block_index]
        back_router = router.T.astype(jnp.float32)
        flat_mixed = jnp.dot(
            back_router,
            mixed_rows.reshape(host_total * capacity, row_width),
            precision=lax.Precision.HIGHEST,
        )
        flat_top = jnp.dot(
            back_router,
            top_score.reshape(host_total * capacity, head_count),
            precision=lax.Precision.HIGHEST,
        )
        flat_totals = jnp.dot(
            back_router,
            totals.reshape(host_total * capacity, head_count),
            precision=lax.Precision.HIGHEST,
        )
        flat_top = jnp.where(wanted[:, None], flat_top, NEG_FILL)
        entries.append((flat_mixed, flat_top, flat_totals))
    shaped_query = query_rows.reshape(attempts, head_count, HEAD_SIZE)
    own_keys = jnp.concatenate([generated_token_cache[:, 0], key_rows[:, None, :]], axis=1).reshape(
        attempts, -1, head_count, HEAD_SIZE
    )
    own_values = jnp.concatenate(
        [generated_token_cache[:, 1], value_rows[:, None, :]], axis=1
    ).reshape(attempts, -1, head_count, HEAD_SIZE)
    own_scores = jnp.einsum(
        "ahd,athd->aht", shaped_query, own_keys, preferred_element_type=jnp.float32
    ) * HEAD_SIZE ** (-0.5)
    own_top = jnp.max(own_scores, axis=2)
    own_weights = jnp.exp(own_scores - own_top[..., None])
    own_totals = jnp.sum(own_weights, axis=2)
    own_mixed = jnp.einsum(
        "aht,athd->ahd",
        own_weights.astype(jnp.bfloat16),
        own_values,
        preferred_element_type=jnp.float32,
    )
    overall = own_top
    for flat_mixed, flat_top, flat_totals in entries:
        overall = jnp.maximum(overall, flat_top)
    own_factor = jnp.exp(own_top - overall)
    numerator = own_mixed * own_factor[..., None]
    denominator = own_totals * own_factor
    for flat_mixed, flat_top, flat_totals in entries:
        factor = jnp.exp(flat_top - overall)
        numerator = (
            numerator + flat_mixed.reshape(attempts, head_count, HEAD_SIZE) * factor[..., None]
        )
        denominator = denominator + flat_totals * factor
    attended = (numerator / denominator[..., None]).reshape(attempts, row_width)
    live_rows = living[:, None]
    return (
        jnp.where(live_rows, attended, 0.0).astype(jnp.bfloat16),
        jnp.where(live_rows, key_rows, 0.0),
        jnp.where(live_rows, value_rows, 0.0),
    )


def _iota(shape, dim):
    return lax.broadcasted_iota(jnp.int32, shape, dim)


def _dot(a, b):
    return jnp.dot(a, b, preferred_element_type=jnp.float32)


def _dot_t(a, b):
    return lax.dot_general(a, b, (((1,), (1,)), ((), ())), preferred_element_type=jnp.float32)


def fused_kernel(
    sizes,
    thm_hbm, apr_hbm, ppr_hbm, cnt_hbm,
    hid_hbm, bq_hbm, live_hbm, k_hbm, val_hbm, a_hbm, b_hbm, kv_hbm, gen_hbm,
    out, key_out, val_out,
    thm, apr, ppr, cnt, hidden, base_q, live, base_k, base_v, a_v, b_v, kv_v, gen_v,
    snd_h, rcv_h, snd_q, rcv_q, part, snd_v, rcv_v, snd_m, rcv_m, snd_l, rcv_l, own_mix,
    local_sem, h_s, h_r, bq_s, bq_r, p_s, p_r, q_s, q_r, v_s, v_r, m_s, m_r, l_s, l_r,
    *queries,
):
    H, MP, A, CAP, L, T, PB, HEADS, SUF, NCH = sizes
    f32, bf = jnp.float32, jnp.bfloat16
    D = HEAD_SIZE
    W = HEADS * D
    W2 = W // 2
    S = H * CAP
    CW = W // NCH
    shift = CAP.bit_length() - 1
    me = lax.axis_index("hosts")
    mme = lax.axis_index("mp")

    def other(axis, d):
        return lax.rem((me if axis == "hosts" else mme) + d, H if axis == "hosts" else MP)

    locals_ = [
        pltpu.make_async_copy(src, dst, local_sem.at[i])
        for i, (src, dst) in enumerate(
            [
                (a_hbm, a_v), (b_hbm, b_v), (kv_hbm, kv_v), (gen_hbm, gen_v),
                (live_hbm, live), (k_hbm, base_k), (val_hbm, base_v),
                (thm_hbm, thm), (apr_hbm, apr), (ppr_hbm, ppr), (cnt_hbm, cnt),
                (hid_hbm, hidden), (bq_hbm, base_q),
            ]
        )
    ]

    barrier = pltpu.get_barrier_semaphore()
    for d in range(1, H):
        pl.semaphore_signal(barrier, inc=1, device_id={"hosts": other("hosts", d)}, device_id_type=MESH)
    for d in range(1, MP):
        pl.semaphore_signal(barrier, inc=1, device_id={"mp": other("mp", d)}, device_id_type=MESH)

    for i in (7, 8, 4, 11, 12, 0, 9, 10, 1, 2, 5, 6, 3):
        locals_[i].start()

    def send(src, dst, s, r, axis, d):
        copy = pltpu.make_async_remote_copy(
            src_ref=src, dst_ref=dst, send_sem=s, recv_sem=r,
            device_id={axis: other(axis, d)}, device_id_type=MESH,
        )
        copy.start()
        return copy

    lane8, sub8 = _iota((8, 128), 1), _iota((8, 128), 0)
    th = jnp.full((8, 128), -1, jnp.int32)
    locals_[7].wait()
    locals_[8].wait()
    for a in range(A):
        th = jnp.where(lane8 == a, thm[a], th)
    owner = jnp.full((8, 128), -1, jnp.int32)
    for t in range(T):
        owner = jnp.where(th == t, apr[t], owner)
    locals_[4].wait()
    n_live = live[0]
    owner = jnp.where(lane8 < n_live, owner, -1)
    member = jnp.where(owner == sub8, 1.0, 0.0).astype(f32)
    before = jnp.where(_iota((128, 128), 0) < _iota((128, 128), 1), 1.0, 0.0).astype(bf)
    rank_f = jnp.sum(member * _dot(member.astype(bf), before), axis=0, keepdims=True)
    rank_row = rank_f.astype(jnp.int32)
    target = jnp.where(owner[0:1] >= 0, owner[0:1] * CAP + rank_row, -1)
    router = jnp.where(_iota((S, A), 0) == target[:, :A], 1.0, 0.0).astype(bf)

    def folded(rows, e):
        piece = rows[e * CAP : (e + 1) * CAP]
        return jnp.concatenate([piece[:, :W2], piece[:, W2:]], axis=0)

    locals_[11].wait()
    packed = _dot(router, hidden[...])
    for e in range(H):
        snd_h[e] = folded(packed, e).astype(bf)
    pl.semaphore_wait(barrier, H - 1 + MP - 1)
    hs = [
        send(snd_h.at[other("hosts", d)], rcv_h.at[me], h_s.at[d], h_r.at[d], "hosts", d)
        for d in range(1, H)
    ]
    locals_[12].wait()
    packed = _dot(router, base_q[...])
    for e in range(H):
        snd_q[e] = folded(packed, e).astype(bf)
    bqs = [
        send(snd_q.at[other("hosts", d)], rcv_q.at[me], bq_s.at[d], bq_r.at[d], "hosts", d)
        for d in range(1, H)
    ]
    rcv_h[me] = snd_h[me]
    rcv_q[me] = snd_q[me]

    locals_[9].wait()
    locals_[10].wait()
    lane = _iota((8, 128), 1)
    half = jnp.where(lane < D // 2, lane, lane - D // 2).astype(f32)
    freq = jnp.exp(half * (-2.0 / D * math.log(ROPE_BASE)))
    counts = jnp.zeros((8, 128), jnp.int32)
    my_count = jnp.int32(0)
    for t in range(T):
        counts = jnp.where(sub8 == t, cnt[t], counts)
        my_count = jnp.where(apr[t] == me, cnt[t], my_count)
    counts = jnp.where(sub8 == T, my_count, counts)
    angle = (BLK * counts + SUF).astype(f32) * freq
    cos_t = jnp.cos(angle)
    sin_t = jnp.sin(angle)
    sin_t = jnp.where(lane < D // 2, -sin_t, sin_t)

    def turn(x, c, s):
        return x * c + pltpu.roll(x, D // 2, 1) * s

    locals_[0].wait()
    for copy in hs:
        copy.wait_recv()
    rows = rcv_h[...].reshape(H * 2 * CAP, W2)
    left = _dot(rows, a_v[0, :W2, :])
    right = _dot(rows, a_v[0, W2:, :])
    part[mme] = jnp.concatenate(
        [
            left[2 * CAP * e : 2 * CAP * e + CAP] + right[2 * CAP * e + CAP : 2 * CAP * (e + 1)]
            for e in range(H)
        ],
        axis=0,
    )
    ps = [
        send(part.at[mme], part.at[mme], p_s.at[d], p_r.at[d], "mp", d) for d in range(1, MP)
    ]
    for copy in bqs:
        copy.wait_recv()
    bq = rcv_q[...].astype(f32)
    bq_half = [
        jnp.concatenate([bq[e, k * CAP : (k + 1) * CAP] for e in range(H)], axis=0)
        for k in range(2)
    ]
    locals_[1].wait()
    for copy in ps:
        copy.wait_recv()
    ranks = part[0]
    for m in range(1, MP):
        ranks = ranks + part[m]
    ranks = ranks.astype(bf).astype(f32)
    rank_q = ranks[:, :ADAPTER_RANK].astype(bf)
    rank_v = pltpu.roll(ranks, ADAPTER_RANK, 1)[:, :ADAPTER_RANK].astype(bf)
    qs = []
    for c in range(NCH):
        cols = slice(c * CW, (c + 1) * CW)
        delta = (_dot(rank_q, b_v[0, 0, :, cols]) * ADAPTER_SCALE).astype(bf).astype(f32)
        k, off = (c * CW) // W2, (c * CW) % W2
        raw = bq_half[k][:, off : off + CW] + delta
        for h in range(CW // D):
            queries[c][me, :, h * D : (h + 1) * D] = turn(
                raw[:, h * D : (h + 1) * D], cos_t[T : T + 1], sin_t[T : T + 1]
            ).astype(bf)
        view = queries[c].at[me]
        qs.append(
            [send(view, view, q_s.at[c, d], q_r.at[c, d], "hosts", d) for d in range(1, H)]
        )
    delta = _dot(rank_v, b_v[0, 1]) * ADAPTER_SCALE
    for e in range(H):
        snd_v[e] = folded(delta, e).astype(bf)
    vs = [
        send(snd_v.at[other("hosts", d)], rcv_v.at[me], v_s.at[d], v_r.at[d], "hosts", d)
        for d in range(1, H)
    ]
    rcv_v[me] = snd_v[me]

    sub128 = _iota((128, 128), 0)
    both = jnp.where(sub128 == 0, th[0:1].astype(f32), jnp.where(sub128 == 1, rank_f, 0.0))
    turned = both.T[:A].astype(jnp.int32)
    th_c, rank_c = turned[:, 0:1], turned[:, 1:2]
    lane_a = _iota((A, 128), 1)
    live_c = _iota((A, 1), 0) < n_live
    owner_c = jnp.full((A, 1), -1, jnp.int32)
    cos_a = jnp.zeros((A, 128), f32)
    sin_a = jnp.zeros((A, 128), f32)
    blocks_c = [jnp.full((A, 1), -1, jnp.int32) for _ in range(PB)]
    for t in range(T):
        here = th_c == t
        owner_c = jnp.where(here, apr[t], owner_c)
        cos_a = jnp.where(here, cos_t[t : t + 1], cos_a)
        sin_a = jnp.where(here, sin_t[t : t + 1], sin_a)
        for j in range(PB):
            blocks_c[j] = jnp.where(here, jnp.where(j < cnt[t], ppr[t, j], -1), blocks_c[j])
    owner_c = jnp.where(live_c, owner_c, -1)
    slot_ok = jnp.where(rank_c == (lane_a & (CAP - 1)), 1, 0)
    group = lane_a >> shift
    used = jnp.zeros((A, 128), jnp.int32)
    for j in range(PB):
        used = used + jnp.where(blocks_c[j] == group, 1, 0)
    used = jnp.where(live_c, used * slot_ok, 0) > 0
    fetch = jnp.where(owner_c * H + me == group, slot_ok, 0).astype(f32).astype(bf)
    unpack = jnp.where(
        owner_c * CAP + rank_c == _iota((A, S), 1), jnp.where(owner_c >= 0, 1.0, 0.0), 0.0
    ).astype(bf)
    keys = []
    locals_[5].wait()
    for h in range(HEADS):
        cols = slice(h * D, (h + 1) * D)
        key = turn(base_k[:, cols].astype(f32), cos_a, sin_a).astype(bf).astype(f32)
        keys.append(key)
        key_out[:, cols] = jnp.where(live_c, key, 0.0).astype(bf)

    whose = []
    for b in range(L):
        index = jnp.int32(0)
        for t in range(T):
            for j in range(PB):
                index = jnp.where(ppr[t, j] == me * L + b, apr[t], index)
        whose.append(index)
    scale = D ** (-0.5)
    locals_[2].wait()
    lane_block = (_iota((128, 128), 1) >> shift) & (L - 1)
    sub_h = _iota((HEADS, 128), 0)
    lse_t = jnp.zeros((HEADS, 128), f32)
    N = gen_v.shape[0]
    lane_n, sub_n = _iota((A, N), 1), _iota((A, N), 0)
    mine = ((lane_n >> (SUF.bit_length())) == sub_n) & ((lane_n & (2 * SUF - 1)) < SUF)
    own_top, own_total, own_self = [], [], []
    ms = []
    for c in range(NCH):
        for copy in qs[c]:
            copy.wait_recv()
        for h in range(c * CW // D, (c + 1) * CW // D):
            cols = slice(h * D, (h + 1) * D)
            within = slice(h * D - c * CW, (h + 1) * D - c * CW)
            asked = [queries[c][whose[b], :, within].astype(f32) for b in range(L)]
            asked = jnp.concatenate(
                [asked[b][e * CAP : (e + 1) * CAP] for e in range(H) for b in range(L)], axis=0
            ).astype(bf)
            scores = _dot_t(kv_v[0, 0, :, cols], asked)
            for b in range(1, L):
                scores = jnp.where(lane_block == b, _dot_t(kv_v[b, 0, :, cols], asked), scores)
            scores = scores * scale
            top = jnp.max(scores, axis=0, keepdims=True)
            weights = jnp.exp(scores - top)
            total = jnp.sum(weights, axis=0, keepdims=True)
            lse_t = jnp.where(sub_h == h, top + jnp.log(total), lse_t)
            weights = (weights * (1.0 / total)).T
            mixed = []
            for b in range(L):
                rows = jnp.concatenate(
                    [weights[(e * L + b) * CAP : (e * L + b + 1) * CAP] for e in range(H)], axis=0
                )
                mixed.append(_dot(rows.astype(bf), kv_v[b, 1, :, cols]))
            for e in range(H):
                snd_m[e, :, cols] = jnp.concatenate(
                    [mixed[b][e * CAP : (e + 1) * CAP] for b in range(L)], axis=0
                ).astype(bf)
        if c == NCH - 1:
            rcv_l[me] = lse_t
            for d in range(1, H):
                snd_l[d] = pltpu.roll(lse_t, (128 - L * CAP * d) % 128, 1)
            ls = [
                send(snd_l.at[d], rcv_l.at[me], l_s.at[d], l_r.at[d], "hosts", d)
                for d in range(1, H)
            ]
        span = pl.ds(c * CW, CW)
        ms.append(
            [
                send(
                    snd_m.at[other("hosts", d), :, span], rcv_m.at[me, :, span],
                    m_s.at[c, d], m_r.at[c, d], "hosts", d,
                )
                for d in range(1, H)
            ]
        )
        if c == 0:
            locals_[3].wait()
        for h in range(c * CW // D, (c + 1) * CW // D):
            cols = slice(h * D, (h + 1) * D)
            start = h * D - c * CW
            query = _dot(fetch, queries[c][:, :, start : start + D].reshape(H * S, D))
            scores = _dot_t(query.astype(bf), gen_v[:, cols]) * scale
            scores = jnp.where(mine, scores, NEG_FILL)
            self_score = jnp.sum(query * keys[h], axis=1, keepdims=True) * scale
            top = jnp.maximum(jnp.max(scores, axis=1, keepdims=True), self_score)
            weights = jnp.where(mine, jnp.exp(scores - top), 0.0)
            self_weight = jnp.exp(self_score - top)
            own_top.append(top)
            own_total.append(jnp.sum(weights, axis=1, keepdims=True) + self_weight)
            own_mix[:, cols] = (
                _dot(pltpu.roll(weights, SUF, 1).astype(bf), gen_v[:, cols])
            )
            own_self.append(self_weight.astype(bf).astype(f32))
    rcv_m[me] = snd_m[me]

    locals_[6].wait()
    for copy in vs:
        copy.wait_recv()
    dv = rcv_v[...].astype(f32)
    dv_att = [
        _dot(
            unpack,
            jnp.concatenate([dv[p, k * CAP : (k + 1) * CAP] for p in range(H)], axis=0).astype(bf),
        )
        for k in range(2)
    ]
    for h in range(HEADS):
        cols = slice(h * D, (h + 1) * D)
        k, off = (h * D) // W2, (h * D) % W2
        value = (base_v[:, cols].astype(f32) + dv_att[k][:, off : off + D]).astype(bf).astype(f32)
        val_out[:, cols] = jnp.where(live_c, value, 0.0).astype(bf)
        own_mix[:, cols] += own_self[h] * value

    for copy in ls:
        copy.wait_recv()
    lse = jnp.zeros((HEADS, 128), f32)
    lane_h = _iota((HEADS, 128), 1)
    for g in range(H):
        lse = jnp.where((lane_h >= g * L * CAP) & (lane_h < (g + 1) * L * CAP), rcv_l[g], lse)
    for c in range(NCH):
        for copy in ms[c]:
            copy.wait_recv()
        for h in range(c * CW // D, (c + 1) * CW // D):
            cols = slice(h * D, (h + 1) * D)
            logs = jnp.where(used, lse[h : h + 1], NEG_FILL)
            top = jnp.maximum(jnp.max(logs, axis=1, keepdims=True), own_top[h])
            factor = jnp.where(used, jnp.exp(logs - top), 0.0)
            own_factor = jnp.exp(own_top[h] - top)
            inverse = 1.0 / (jnp.sum(factor, axis=1, keepdims=True) + own_total[h] * own_factor)
            result = _dot(
                (factor * inverse).astype(bf), rcv_m[:, :, cols].reshape(H * L * CAP, D)
            ) + own_mix[:, cols] * (own_factor * inverse)
            out[:, cols] = jnp.where(live_c, result, 0.0).astype(bf)
    for copies in [hs, bqs, ps, vs, ls] + qs + ms:
        for copy in copies:
            copy.wait_send()


def write_kernel(*refs):
    sems = refs[6]
    copies = [pltpu.make_async_copy(refs[i], refs[3 + i], sems.at[i]) for i in range(3)]
    for copy in copies:
        copy.start()
    for copy in copies:
        copy.wait()


def fused_body(
    hidden, base_q, base_k, base_v, a_in, b_out, cache, generated, thm, live, apr, ppr, cnt
):
    H, MP = lax.axis_size("hosts"), lax.axis_size("mp")
    A, W = hidden.shape
    CAP = A // H
    L, SUF = cache.shape[0], generated.shape[2]
    HEADS = W // HEAD_SIZE
    S = H * CAP
    NCH = 2
    bf, f32 = jnp.bfloat16, jnp.float32
    N = generated.shape[0] * 2 * SUF
    sizes = (H, MP, A, CAP, L, apr.shape[0], ppr.shape[1], HEADS, SUF, NCH)
    vmem = pl.BlockSpec(memory_space=pltpu.VMEM)
    hbm = pl.BlockSpec(memory_space=pl.ANY)
    fold = (H, 2 * CAP, W // 2)
    sem = lambda *shape: pltpu.SemaphoreType.DMA(shape)
    results = pl.pallas_call(
        functools.partial(fused_kernel, sizes),
        out_shape=[pltpu.VMEM((A, W), bf)] * 3,
        in_specs=[hbm] * 13,
        out_specs=[vmem] * 3,
        scratch_shapes=[
            pltpu.SMEM(thm.shape, jnp.int32),
            pltpu.SMEM(apr.shape, jnp.int32),
            pltpu.SMEM(ppr.shape, jnp.int32),
            pltpu.SMEM(cnt.shape, jnp.int32),
            pltpu.VMEM((A, W), bf),
            pltpu.VMEM((A, W), bf),
            pltpu.SMEM(live.shape, jnp.int32),
            pltpu.VMEM((A, W), bf),
            pltpu.VMEM((A, W), bf),
            pltpu.VMEM(a_in.shape, bf),
            pltpu.VMEM(b_out.shape, bf),
            pltpu.VMEM(cache.shape, bf),
            pltpu.VMEM((N, W), bf),
            pltpu.VMEM(fold, bf),
            pltpu.VMEM(fold, bf),
            pltpu.VMEM(fold, bf),
            pltpu.VMEM(fold, bf),
            pltpu.VMEM((MP, S, 128), f32),
            pltpu.VMEM(fold, bf),
            pltpu.VMEM(fold, bf),
            pltpu.VMEM((H, L * CAP, W), bf),
            pltpu.VMEM((H, L * CAP, W), bf),
            pltpu.VMEM((H, HEADS, 128), f32),
            pltpu.VMEM((H, HEADS, 128), f32),
            pltpu.VMEM((A, W), f32),
            sem(13), sem(H), sem(H), sem(H), sem(H), sem(MP), sem(MP),
            sem(NCH, H), sem(NCH, H), sem(H), sem(H), sem(NCH, H), sem(NCH, H), sem(H), sem(H),
        ]
        + [pltpu.VMEM((H, S, W // NCH), bf)] * NCH,
        compiler_params=pltpu.CompilerParams(
            collective_id=0, has_side_effects=True, vmem_limit_bytes=60 * 1024 * 1024
        ),
        cost_estimate=pl.CostEstimate(
            flops=2 * 10**8, bytes_accessed=4 * 10**6, transcendentals=10**6
        ),
    )(
        thm, apr, ppr, cnt, hidden, base_q, live, base_k, base_v, a_in, b_out, cache,
        generated.reshape(N, W),
    )
    return pl.pallas_call(
        write_kernel,
        out_shape=[jax.ShapeDtypeStruct((A, W), bf)] * 3,
        in_specs=[vmem] * 3,
        out_specs=[hbm] * 3,
        scratch_shapes=[sem(3)],
        compiler_params=pltpu.CompilerParams(vmem_limit_bytes=2**20),
    )(*results)


def step(hidden, base_q, base_k, base_v, a_in, b_out, cache, generated, thm, live, apr, ppr, cnt):
    H = lax.axis_size("hosts")
    A, W = hidden.shape
    capacity = A // H
    fits = (
        capacity == 8
        and H <= 8
        and A <= 128
        and a_in.shape[0] == 1
        and A * cache.shape[0] == 128
        and cache.shape[0] == 4
        and cache.shape[2] == 128
        and H * A == 128
        and W == 8 * HEAD_SIZE
        and generated.shape[2] == 8
        and apr.shape[0] < 8
    )
    run = fused_body if fits else body
    return run(hidden, base_q, base_k, base_v, a_in, b_out, cache, generated, thm, live, apr, ppr, cnt)


def solution(mesh):
    placed = (
        P(("groups", "hosts"), "mp"),
        P(("groups", "hosts"), "mp"),
        P(("groups", "hosts"), "mp"),
        P(("groups", "hosts"), "mp"),
        P(("groups", "hosts"), "mp", None),
        P(("groups", "hosts"), None, None, "mp"),
        P(("groups", "hosts"), None, None, "mp"),
        P(("groups", "hosts"), None, None, "mp"),
        P(("groups", "hosts")),
        P(("groups", "hosts")),
        P("groups"),
        P("groups", None),
        P("groups"),
    )
    return jax.shard_map(
        step,
        mesh=mesh,
        in_specs=placed,
        out_specs=(
            P(("groups", "hosts"), "mp"),
            P(("groups", "hosts"), "mp"),
            P(("groups", "hosts"), "mp"),
        ),
        check_vma=False,
    )
```

```python
import functools
import math

import jax
import jax.numpy as jnp
from jax import lax
from jax.experimental import pallas as pl
from jax.experimental.pallas import tpu as pltpu
from jax.sharding import PartitionSpec as P

HEAD_SIZE = 128
ADAPTER_RANK = 64
BLK = 128
PBLK = 4


ADAPTER_SCALE = 0.5
ROPE_BASE = 10000.0
NEG_FILL = -1e30
MESH = pl.DeviceIdType.MESH


def rotate(values, position):
    shaped = values.reshape(values.shape[:-1] + (-1, HEAD_SIZE))
    halfway = HEAD_SIZE // 2
    frequency = ROPE_BASE ** (-(jnp.arange(halfway, dtype=jnp.float32) * (2.0 / HEAD_SIZE)))
    angles = position.astype(jnp.float32)[..., None] * frequency
    cosine = jnp.cos(angles)[..., None, :]
    sine_part = jnp.sin(angles)[..., None, :]
    first_half = shaped[..., :halfway]
    second = shaped[..., halfway:]
    turned = jnp.concatenate(
        [first_half * cosine - second * sine_part, second * cosine + first_half * sine_part],
        axis=-1,
    )
    return turned.reshape(values.shape)


def lookup_table(source_table, wanted):
    matches = wanted[:, None] == jnp.arange(source_table.shape[0], dtype=jnp.int32)[None, :]
    if source_table.ndim == 1:
        return jnp.sum(jnp.where(matches, source_table[None, :], 0), axis=1)
    return jnp.sum(jnp.where(matches[:, :, None], source_table[None, :, :], 0), axis=1)


def route_matrix(destination, validity, capacity, host_total):
    ordinal = jnp.arange(destination.shape[0], dtype=jnp.int32)
    earlier = (
        (destination[:, None] == destination[None, :])
        & validity[None, :]
        & (ordinal[None, :] < ordinal[:, None])
    )
    ranking = jnp.sum(earlier.astype(jnp.int32), axis=1)
    target = destination * capacity + ranking
    places = jnp.arange(host_total * capacity, dtype=jnp.int32)
    return ((places[:, None] == target[None, :]) & validity[None, :]).astype(jnp.bfloat16)


def pack_rows(router, payload):
    return jnp.dot(router, payload, preferred_element_type=jnp.float32).astype(jnp.bfloat16)


def attend_local(queries, chosen, statement_prefix_cache):
    head_count = queries.shape[-1] // HEAD_SIZE
    blocks = statement_prefix_cache.shape[0]
    block_keys = statement_prefix_cache[:, 0].reshape(
        blocks, statement_prefix_cache.shape[2], head_count, HEAD_SIZE
    )
    block_values = statement_prefix_cache[:, 1].reshape(
        blocks, statement_prefix_cache.shape[2], head_count, HEAD_SIZE
    )
    shaped = queries.reshape(queries.shape[:-1] + (head_count, HEAD_SIZE))
    scores = jnp.einsum(
        "nchd,bthd->ncbht", shaped, block_keys, preferred_element_type=jnp.float32
    ) * HEAD_SIZE ** (-0.5)
    chosen_mask = (chosen > 0)[:, :, :, None, None]
    masked = jnp.where(chosen_mask, scores, NEG_FILL)
    top_score = jnp.max(masked, axis=(2, 4))
    weights = jnp.where(chosen_mask, jnp.exp(masked - top_score[:, :, None, :, None]), 0.0)
    totals = jnp.sum(weights, axis=(2, 4))
    mixed_rows = jnp.einsum(
        "ncbht,bthd->nchd",
        weights.astype(jnp.bfloat16),
        block_values,
        preferred_element_type=jnp.float32,
    )
    return (mixed_rows.reshape(queries.shape), top_score, totals)


def body(
    hidden,
    base_query_projection,
    base_key_projection,
    base_value_projection,
    adapter_input_factors,
    adapter_output_factors,
    statement_prefix_cache,
    generated_token_cache,
    attempt_theorem_index,
    host_live_count,
    adapter_pool_row,
    prefix_pool_row,
    prefix_block_count,
):
    host_total = lax.axis_size("hosts")
    attempts = hidden.shape[0]
    capacity = max(1, attempts // host_total)
    owner_held_rows = adapter_input_factors.shape[0]
    local_blocks = statement_prefix_cache.shape[0]
    row_width = base_query_projection.shape[1]
    head_count = row_width // HEAD_SIZE
    ordinal = jnp.arange(attempts, dtype=jnp.int32)
    living = ordinal < host_live_count[0]
    adapter_rows = lookup_table(adapter_pool_row, attempt_theorem_index)
    block_rows = lookup_table(prefix_pool_row, attempt_theorem_index)
    block_counts = lookup_table(prefix_block_count, attempt_theorem_index)
    position = BLK * block_counts + generated_token_cache.shape[2]
    adapter_router = route_matrix(adapter_rows // owner_held_rows, living, capacity, host_total)
    adapter_pick = (
        adapter_rows[:, None] % owner_held_rows
        == jnp.arange(owner_held_rows, dtype=jnp.int32)[None, :]
    ).astype(jnp.bfloat16)
    sent_hidden = pack_rows(adapter_router, hidden).reshape(host_total, capacity, hidden.shape[1])
    sent_pick = pack_rows(adapter_router, adapter_pick).reshape(
        host_total, capacity, owner_held_rows
    )
    incoming_rows = lax.all_to_all(sent_hidden, "hosts", split_axis=0, concat_axis=0, tiled=True)
    pick_in = lax.all_to_all(sent_pick, "hosts", split_axis=0, concat_axis=0, tiled=True)
    projected_rows = jnp.einsum(
        "xjp,epk->xjek", incoming_rows, adapter_input_factors, preferred_element_type=jnp.float32
    )
    partial_rank = jnp.sum(projected_rows * pick_in.astype(jnp.float32)[..., None], axis=2)
    rank_rows = lax.psum(partial_rank, "mp").astype(jnp.bfloat16)
    spread_rows = rank_rows[:, :, None, :] * pick_in[..., None]
    query_correction = jnp.einsum(
        "exqw,qwf->exf",
        spread_rows[..., :ADAPTER_RANK],
        adapter_output_factors[:, 0],
        preferred_element_type=jnp.float32,
    )
    value_correction = jnp.einsum(
        "exqw,qwf->exf",
        spread_rows[..., ADAPTER_RANK:],
        adapter_output_factors[:, 1],
        preferred_element_type=jnp.float32,
    )
    adapter_corrections = (
        jnp.concatenate([query_correction, value_correction], axis=-1) * ADAPTER_SCALE
    ).astype(jnp.bfloat16)
    returned = lax.all_to_all(adapter_corrections, "hosts", split_axis=0, concat_axis=0, tiled=True)
    adapter_corrections = jnp.dot(
        adapter_router.T,
        returned.reshape(host_total * capacity, 2 * row_width),
        preferred_element_type=jnp.float32,
    )
    query_rows = rotate(
        base_query_projection.astype(jnp.float32) + adapter_corrections[:, :row_width], position
    ).astype(jnp.bfloat16)
    value_rows = (
        base_value_projection.astype(jnp.float32) + adapter_corrections[:, row_width:]
    ).astype(jnp.bfloat16)
    key_rows = rotate(base_key_projection.astype(jnp.float32), position).astype(jnp.bfloat16)
    requests = []
    for block_index in range(PBLK):
        wanted = living & (block_index < block_counts)
        holder = block_rows[:, block_index]
        router = route_matrix(holder // local_blocks, wanted, capacity, host_total)
        block_pick = (
            holder[:, None] % local_blocks == jnp.arange(local_blocks, dtype=jnp.int32)[None, :]
        ).astype(jnp.bfloat16)
        sent_queries = pack_rows(router, query_rows).reshape(host_total, capacity, row_width)
        sent_blocks = pack_rows(router, block_pick).reshape(host_total, capacity, local_blocks)
        requests.append((router, wanted, sent_queries, sent_blocks))
    partials = []
    for request in requests:
        answer_mixed_rows, answer_top_score, answer_totals = attend_local(
            lax.all_to_all(request[2], "hosts", split_axis=0, concat_axis=0, tiled=True),
            lax.all_to_all(request[3], "hosts", split_axis=0, concat_axis=0, tiled=True),
            statement_prefix_cache,
        )
        partials.append(
            (
                lax.all_to_all(answer_mixed_rows, "hosts", split_axis=0, concat_axis=0, tiled=True),
                lax.all_to_all(answer_top_score, "hosts", split_axis=0, concat_axis=0, tiled=True),
                lax.all_to_all(answer_totals, "hosts", split_axis=0, concat_axis=0, tiled=True),
            )
        )
    entries = []
    for block_index in range(PBLK):
        router, wanted = (requests[block_index][0], requests[block_index][1])
        mixed_rows, top_score, totals = partials[block_index]
        back_router = router.T.astype(jnp.float32)
        flat_mixed = jnp.dot(
            back_router,
            mixed_rows.reshape(host_total * capacity, row_width),
            precision=lax.Precision.HIGHEST,
        )
        flat_top = jnp.dot(
            back_router,
            top_score.reshape(host_total * capacity, head_count),
            precision=lax.Precision.HIGHEST,
        )
        flat_totals = jnp.dot(
            back_router,
            totals.reshape(host_total * capacity, head_count),
            precision=lax.Precision.HIGHEST,
        )
        flat_top = jnp.where(wanted[:, None], flat_top, NEG_FILL)
        entries.append((flat_mixed, flat_top, flat_totals))
    shaped_query = query_rows.reshape(attempts, head_count, HEAD_SIZE)
    own_keys = jnp.concatenate([generated_token_cache[:, 0], key_rows[:, None, :]], axis=1).reshape(
        attempts, -1, head_count, HEAD_SIZE
    )
    own_values = jnp.concatenate(
        [generated_token_cache[:, 1], value_rows[:, None, :]], axis=1
    ).reshape(attempts, -1, head_count, HEAD_SIZE)
    own_scores = jnp.einsum(
        "ahd,athd->aht", shaped_query, own_keys, preferred_element_type=jnp.float32
    ) * HEAD_SIZE ** (-0.5)
    own_top = jnp.max(own_scores, axis=2)
    own_weights = jnp.exp(own_scores - own_top[..., None])
    own_totals = jnp.sum(own_weights, axis=2)
    own_mixed = jnp.einsum(
        "aht,athd->ahd",
        own_weights.astype(jnp.bfloat16),
        own_values,
        preferred_element_type=jnp.float32,
    )
    overall = own_top
    for flat_mixed, flat_top, flat_totals in entries:
        overall = jnp.maximum(overall, flat_top)
    own_factor = jnp.exp(own_top - overall)
    numerator = own_mixed * own_factor[..., None]
    denominator = own_totals * own_factor
    for flat_mixed, flat_top, flat_totals in entries:
        factor = jnp.exp(flat_top - overall)
        numerator = (
            numerator + flat_mixed.reshape(attempts, head_count, HEAD_SIZE) * factor[..., None]
        )
        denominator = denominator + flat_totals * factor
    attended = (numerator / denominator[..., None]).reshape(attempts, row_width)
    live_rows = living[:, None]
    return (
        jnp.where(live_rows, attended, 0.0).astype(jnp.bfloat16),
        jnp.where(live_rows, key_rows, 0.0),
        jnp.where(live_rows, value_rows, 0.0),
    )


def _iota(shape, dim):
    return lax.broadcasted_iota(jnp.int32, shape, dim)


def _dot(a, b):
    return jnp.dot(a, b, preferred_element_type=jnp.float32)


def _dot_t(a, b):
    return lax.dot_general(a, b, (((1,), (1,)), ((), ())), preferred_element_type=jnp.float32)


def fused_kernel(
    sizes,
    thm_hbm, apr_hbm, ppr_hbm, cnt_hbm,
    hid_hbm, bq_hbm, live_hbm, k_hbm, val_hbm, a_hbm, b_hbm, kv_hbm, gen_hbm,
    out, key_out, val_out,
    thm, apr, ppr, cnt, hidden, base_q, live, base_k, base_v, a_v, b_v, kv_v, gen_v,
    snd_h, rcv_h, snd_q, rcv_q, part, snd_v, rcv_v, snd_m, rcv_m, snd_l, rcv_l, own_mix,
    local_sem, h_s, h_r, bq_s, bq_r, p_s, p_r, q_s, q_r, v_s, v_r, m_s, m_r, l_s, l_r,
    *queries,
):
    H, MP, A, CAP, L, T, PB, HEADS, SUF, NCH = sizes
    f32, bf = jnp.float32, jnp.bfloat16
    D = HEAD_SIZE
    W = HEADS * D
    W2 = W // 2
    S = H * CAP
    CW = W // NCH
    shift = CAP.bit_length() - 1
    me = lax.axis_index("hosts")
    mme = lax.axis_index("mp")

    def other(axis, d):
        return lax.rem((me if axis == "hosts" else mme) + d, H if axis == "hosts" else MP)

    locals_ = [
        pltpu.make_async_copy(src, dst, local_sem.at[i])
        for i, (src, dst) in enumerate(
            [
                (a_hbm, a_v), (b_hbm, b_v), (kv_hbm, kv_v), (gen_hbm, gen_v),
                (live_hbm, live), (k_hbm, base_k), (val_hbm, base_v),
                (thm_hbm, thm), (apr_hbm, apr), (ppr_hbm, ppr), (cnt_hbm, cnt),
                (hid_hbm, hidden), (bq_hbm, base_q),
            ]
        )
    ]

    barrier = pltpu.get_barrier_semaphore()
    for d in range(1, H):
        pl.semaphore_signal(barrier, inc=1, device_id={"hosts": other("hosts", d)}, device_id_type=MESH)
    for d in range(1, MP):
        pl.semaphore_signal(barrier, inc=1, device_id={"mp": other("mp", d)}, device_id_type=MESH)

    for i in (7, 8, 4, 11, 12, 0, 9, 10, 1, 2, 5, 6, 3):
        locals_[i].start()

    def send(src, dst, s, r, axis, d):
        copy = pltpu.make_async_remote_copy(
            src_ref=src, dst_ref=dst, send_sem=s, recv_sem=r,
            device_id={axis: other(axis, d)}, device_id_type=MESH,
        )
        copy.start()
        return copy

    lane8, sub8 = _iota((8, 128), 1), _iota((8, 128), 0)
    th = jnp.full((8, 128), -1, jnp.int32)
    locals_[7].wait()
    locals_[8].wait()
    for a in range(A):
        th = jnp.where(lane8 == a, thm[a], th)
    owner = jnp.full((8, 128), -1, jnp.int32)
    for t in range(T):
        owner = jnp.where(th == t, apr[t], owner)
    locals_[4].wait()
    n_live = live[0]
    owner = jnp.where(lane8 < n_live, owner, -1)
    member = jnp.where(owner == sub8, 1.0, 0.0).astype(f32)
    before = jnp.where(_iota((128, 128), 0) < _iota((128, 128), 1), 1.0, 0.0).astype(bf)
    rank_f = jnp.sum(member * _dot(member.astype(bf), before), axis=0, keepdims=True)
    rank_row = rank_f.astype(jnp.int32)
    target = jnp.where(owner[0:1] >= 0, owner[0:1] * CAP + rank_row, -1)
    router = jnp.where(_iota((S, A), 0) == target[:, :A], 1.0, 0.0).astype(bf)

    def folded(rows, e):
        piece = rows[e * CAP : (e + 1) * CAP]
        return jnp.concatenate([piece[:, :W2], piece[:, W2:]], axis=0)

    locals_[11].wait()
    packed = _dot(router, hidden[...])
    for e in range(H):
        snd_h[e] = folded(packed, e).astype(bf)
    pl.semaphore_wait(barrier, H - 1 + MP - 1)
    hs = [
        send(snd_h.at[other("hosts", d)], rcv_h.at[me], h_s.at[d], h_r.at[d], "hosts", d)
        for d in range(1, H)
    ]
    locals_[12].wait()
    packed = _dot(router, base_q[...])
    for e in range(H):
        snd_q[e] = folded(packed, e).astype(bf)
    bqs = [
        send(snd_q.at[other("hosts", d)], rcv_q.at[me], bq_s.at[d], bq_r.at[d], "hosts", d)
        for d in range(1, H)
    ]
    rcv_h[me] = snd_h[me]
    rcv_q[me] = snd_q[me]

    locals_[9].wait()
    locals_[10].wait()
    lane = _iota((8, 128), 1)
    half = jnp.where(lane < D // 2, lane, lane - D // 2).astype(f32)
    freq = jnp.exp(half * (-2.0 / D * math.log(ROPE_BASE)))
    counts = jnp.zeros((8, 128), jnp.int32)
    my_count = jnp.int32(0)
    for t in range(T):
        counts = jnp.where(sub8 == t, cnt[t], counts)
        my_count = jnp.where(apr[t] == me, cnt[t], my_count)
    counts = jnp.where(sub8 == T, my_count, counts)
    angle = (BLK * counts + SUF).astype(f32) * freq
    cos_t = jnp.cos(angle)
    sin_t = jnp.sin(angle)
    sin_t = jnp.where(lane < D // 2, -sin_t, sin_t)

    def turn(x, c, s):
        return x * c + pltpu.roll(x, D // 2, 1) * s

    locals_[0].wait()
    for copy in hs:
        copy.wait_recv()
    rows = rcv_h[...].reshape(H * 2 * CAP, W2)
    left = _dot(rows, a_v[0, :W2, :])
    right = _dot(rows, a_v[0, W2:, :])
    part[mme] = jnp.concatenate(
        [
            left[2 * CAP * e : 2 * CAP * e + CAP] + right[2 * CAP * e + CAP : 2 * CAP * (e + 1)]
            for e in range(H)
        ],
        axis=0,
    )
    ps = [
        send(part.at[mme], part.at[mme], p_s.at[d], p_r.at[d], "mp", d) for d in range(1, MP)
    ]
    for copy in bqs:
        copy.wait_recv()
    bq = rcv_q[...].astype(f32)
    bq_half = [
        jnp.concatenate([bq[e, k * CAP : (k + 1) * CAP] for e in range(H)], axis=0)
        for k in range(2)
    ]
    locals_[1].wait()
    for copy in ps:
        copy.wait_recv()
    ranks = part[0]
    for m in range(1, MP):
        ranks = ranks + part[m]
    ranks = ranks.astype(bf).astype(f32)
    rank_q = ranks[:, :ADAPTER_RANK].astype(bf)
    rank_v = pltpu.roll(ranks, ADAPTER_RANK, 1)[:, :ADAPTER_RANK].astype(bf)
    qs = []
    for c in range(NCH):
        cols = slice(c * CW, (c + 1) * CW)
        delta = (_dot(rank_q, b_v[0, 0, :, cols]) * ADAPTER_SCALE).astype(bf).astype(f32)
        k, off = (c * CW) // W2, (c * CW) % W2
        raw = bq_half[k][:, off : off + CW] + delta
        for h in range(CW // D):
            queries[c][me, :, h * D : (h + 1) * D] = turn(
                raw[:, h * D : (h + 1) * D], cos_t[T : T + 1], sin_t[T : T + 1]
            ).astype(bf)
        view = queries[c].at[me]
        qs.append(
            [send(view, view, q_s.at[c, d], q_r.at[c, d], "hosts", d) for d in range(1, H)]
        )
    delta = _dot(rank_v, b_v[0, 1]) * ADAPTER_SCALE
    for e in range(H):
        snd_v[e] = folded(delta, e).astype(bf)
    rcv_v[me] = snd_v[me]

    sub128 = _iota((128, 128), 0)
    both = jnp.where(sub128 == 0, th[0:1].astype(f32), jnp.where(sub128 == 1, rank_f, 0.0))
    turned = both.T[:A].astype(jnp.int32)
    th_c, rank_c = turned[:, 0:1], turned[:, 1:2]
    lane_a = _iota((A, 128), 1)
    live_c = _iota((A, 1), 0) < n_live
    owner_c = jnp.full((A, 1), -1, jnp.int32)
    cos_a = jnp.zeros((A, 128), f32)
    sin_a = jnp.zeros((A, 128), f32)
    blocks_c = [jnp.full((A, 1), -1, jnp.int32) for _ in range(PB)]
    for t in range(T):
        here = th_c == t
        owner_c = jnp.where(here, apr[t], owner_c)
        cos_a = jnp.where(here, cos_t[t : t + 1], cos_a)
        sin_a = jnp.where(here, sin_t[t : t + 1], sin_a)
        for j in range(PB):
            blocks_c[j] = jnp.where(here, jnp.where(j < cnt[t], ppr[t, j], -1), blocks_c[j])
    owner_c = jnp.where(live_c, owner_c, -1)
    slot_ok = jnp.where(rank_c == (lane_a & (CAP - 1)), 1, 0)
    group = lane_a >> shift
    used = jnp.zeros((A, 128), jnp.int32)
    for j in range(PB):
        used = used + jnp.where(blocks_c[j] == group, 1, 0)
    used = jnp.where(live_c, used * slot_ok, 0) > 0
    fetch = jnp.where(owner_c * H + me == group, slot_ok, 0).astype(f32).astype(bf)
    unpack = jnp.where(
        owner_c * CAP + rank_c == _iota((A, S), 1), jnp.where(owner_c >= 0, 1.0, 0.0), 0.0
    ).astype(bf)
    keys = []
    locals_[5].wait()
    for h in range(HEADS):
        cols = slice(h * D, (h + 1) * D)
        key = turn(base_k[:, cols].astype(f32), cos_a, sin_a).astype(bf).astype(f32)
        keys.append(key)
        key_out[:, cols] = jnp.where(live_c, key, 0.0).astype(bf)

    whose = []
    for b in range(L):
        index = jnp.int32(0)
        for t in range(T):
            for j in range(PB):
                index = jnp.where(ppr[t, j] == me * L + b, apr[t], index)
        whose.append(index)
    scale = D ** (-0.5)
    locals_[2].wait()
    lane_block = (_iota((128, 128), 1) >> shift) & (L - 1)
    sub_h = _iota((HEADS, 128), 0)
    lse_t = jnp.zeros((HEADS, 128), f32)
    N = gen_v.shape[0]
    lane_n, sub_n = _iota((A, N), 1), _iota((A, N), 0)
    mine = ((lane_n >> (SUF.bit_length())) == sub_n) & ((lane_n & (2 * SUF - 1)) < SUF)
    own_top, own_total, own_self = [], [], []
    ms = []
    for c in range(NCH):
        for copy in qs[c]:
            copy.wait_recv()
        for h in range(c * CW // D, (c + 1) * CW // D):
            cols = slice(h * D, (h + 1) * D)
            within = slice(h * D - c * CW, (h + 1) * D - c * CW)
            asked = [queries[c][whose[b], :, within].astype(f32) for b in range(L)]
            asked = jnp.concatenate(
                [asked[b][e * CAP : (e + 1) * CAP] for e in range(H) for b in range(L)], axis=0
            ).astype(bf)
            scores = _dot_t(kv_v[0, 0, :, cols], asked)
            for b in range(1, L):
                scores = jnp.where(lane_block == b, _dot_t(kv_v[b, 0, :, cols], asked), scores)
            scores = scores * scale
            top = jnp.max(scores, axis=0, keepdims=True)
            weights = jnp.exp(scores - top)
            total = jnp.sum(weights, axis=0, keepdims=True)
            lse_t = jnp.where(sub_h == h, top + jnp.log(total), lse_t)
            weights = (weights * (1.0 / total)).T
            mixed = []
            for b in range(L):
                rows = jnp.concatenate(
                    [weights[(e * L + b) * CAP : (e * L + b + 1) * CAP] for e in range(H)], axis=0
                )
                mixed.append(_dot(rows.astype(bf), kv_v[b, 1, :, cols]))
            for e in range(H):
                snd_m[e, :, cols] = jnp.concatenate(
                    [mixed[b][e * CAP : (e + 1) * CAP] for b in range(L)], axis=0
                ).astype(bf)
        if c == NCH - 1:
            rcv_l[me] = lse_t
            for d in range(1, H):
                snd_l[d] = pltpu.roll(lse_t, (128 - L * CAP * d) % 128, 1)
            ls = [
                send(snd_l.at[d], rcv_l.at[me], l_s.at[d], l_r.at[d], "hosts", d)
                for d in range(1, H)
            ]
        span = pl.ds(c * CW, CW)
        ms.append(
            [
                send(
                    snd_m.at[other("hosts", d), :, span], rcv_m.at[me, :, span],
                    m_s.at[c, d], m_r.at[c, d], "hosts", d,
                )
                for d in range(1, H)
            ]
        )
        if c == 0:
            vs = [
                send(snd_v.at[other("hosts", d)], rcv_v.at[me], v_s.at[d], v_r.at[d], "hosts", d)
                for d in range(1, H)
            ]
            locals_[3].wait()
        for h in range(c * CW // D, (c + 1) * CW // D):
            cols = slice(h * D, (h + 1) * D)
            start = h * D - c * CW
            query = _dot(fetch, queries[c][:, :, start : start + D].reshape(H * S, D))
            scores = _dot_t(query.astype(bf), gen_v[:, cols]) * scale
            scores = jnp.where(mine, scores, NEG_FILL)
            self_score = jnp.sum(query * keys[h], axis=1, keepdims=True) * scale
            top = jnp.maximum(jnp.max(scores, axis=1, keepdims=True), self_score)
            weights = jnp.where(mine, jnp.exp(scores - top), 0.0)
            self_weight = jnp.exp(self_score - top)
            own_top.append(top)
            own_total.append(jnp.sum(weights, axis=1, keepdims=True) + self_weight)
            own_mix[:, cols] = (
                _dot(pltpu.roll(weights, SUF, 1).astype(bf), gen_v[:, cols])
            )
            own_self.append(self_weight.astype(bf).astype(f32))
    rcv_m[me] = snd_m[me]

    locals_[6].wait()
    for copy in vs:
        copy.wait_recv()
    dv = rcv_v[...].astype(f32)
    dv_att = [
        _dot(
            unpack,
            jnp.concatenate([dv[p, k * CAP : (k + 1) * CAP] for p in range(H)], axis=0).astype(bf),
        )
        for k in range(2)
    ]
    for h in range(HEADS):
        cols = slice(h * D, (h + 1) * D)
        k, off = (h * D) // W2, (h * D) % W2
        value = (base_v[:, cols].astype(f32) + dv_att[k][:, off : off + D]).astype(bf).astype(f32)
        val_out[:, cols] = jnp.where(live_c, value, 0.0).astype(bf)
        own_mix[:, cols] += own_self[h] * value

    for copy in ls:
        copy.wait_recv()
    lse = jnp.zeros((HEADS, 128), f32)
    lane_h = _iota((HEADS, 128), 1)
    for g in range(H):
        lse = jnp.where((lane_h >= g * L * CAP) & (lane_h < (g + 1) * L * CAP), rcv_l[g], lse)
    for c in range(NCH):
        for copy in ms[c]:
            copy.wait_recv()
        for h in range(c * CW // D, (c + 1) * CW // D):
            cols = slice(h * D, (h + 1) * D)
            logs = jnp.where(used, lse[h : h + 1], NEG_FILL)
            top = jnp.maximum(jnp.max(logs, axis=1, keepdims=True), own_top[h])
            factor = jnp.where(used, jnp.exp(logs - top), 0.0)
            own_factor = jnp.exp(own_top[h] - top)
            inverse = 1.0 / (jnp.sum(factor, axis=1, keepdims=True) + own_total[h] * own_factor)
            result = _dot(
                (factor * inverse).astype(bf), rcv_m[:, :, cols].reshape(H * L * CAP, D)
            ) + own_mix[:, cols] * (own_factor * inverse)
            out[:, cols] = jnp.where(live_c, result, 0.0).astype(bf)
    for copies in [hs, bqs, ps, vs, ls] + qs + ms:
        for copy in copies:
            copy.wait_send()


def write_kernel(*refs):
    sems = refs[6]
    copies = [pltpu.make_async_copy(refs[i], refs[3 + i], sems.at[i]) for i in range(3)]
    for copy in copies:
        copy.start()
    for copy in copies:
        copy.wait()


def fused_body(
    hidden, base_q, base_k, base_v, a_in, b_out, cache, generated, thm, live, apr, ppr, cnt
):
    H, MP = lax.axis_size("hosts"), lax.axis_size("mp")
    A, W = hidden.shape
    CAP = A // H
    L, SUF = cache.shape[0], generated.shape[2]
    HEADS = W // HEAD_SIZE
    S = H * CAP
    NCH = 2
    bf, f32 = jnp.bfloat16, jnp.float32
    N = generated.shape[0] * 2 * SUF
    sizes = (H, MP, A, CAP, L, apr.shape[0], ppr.shape[1], HEADS, SUF, NCH)
    vmem = pl.BlockSpec(memory_space=pltpu.VMEM)
    hbm = pl.BlockSpec(memory_space=pl.ANY)
    fold = (H, 2 * CAP, W // 2)
    sem = lambda *shape: pltpu.SemaphoreType.DMA(shape)
    results = pl.pallas_call(
        functools.partial(fused_kernel, sizes),
        out_shape=[pltpu.VMEM((A, W), bf)] * 3,
        in_specs=[hbm] * 13,
        out_specs=[vmem] * 3,
        scratch_shapes=[
            pltpu.SMEM(thm.shape, jnp.int32),
            pltpu.SMEM(apr.shape, jnp.int32),
            pltpu.SMEM(ppr.shape, jnp.int32),
            pltpu.SMEM(cnt.shape, jnp.int32),
            pltpu.VMEM((A, W), bf),
            pltpu.VMEM((A, W), bf),
            pltpu.SMEM(live.shape, jnp.int32),
            pltpu.VMEM((A, W), bf),
            pltpu.VMEM((A, W), bf),
            pltpu.VMEM(a_in.shape, bf),
            pltpu.VMEM(b_out.shape, bf),
            pltpu.VMEM(cache.shape, bf),
            pltpu.VMEM((N, W), bf),
            pltpu.VMEM(fold, bf),
            pltpu.VMEM(fold, bf),
            pltpu.VMEM(fold, bf),
            pltpu.VMEM(fold, bf),
            pltpu.VMEM((MP, S, 128), f32),
            pltpu.VMEM(fold, bf),
            pltpu.VMEM(fold, bf),
            pltpu.VMEM((H, L * CAP, W), bf),
            pltpu.VMEM((H, L * CAP, W), bf),
            pltpu.VMEM((H, HEADS, 128), f32),
            pltpu.VMEM((H, HEADS, 128), f32),
            pltpu.VMEM((A, W), f32),
            sem(13), sem(H), sem(H), sem(H), sem(H), sem(MP), sem(MP),
            sem(NCH, H), sem(NCH, H), sem(H), sem(H), sem(NCH, H), sem(NCH, H), sem(H), sem(H),
        ]
        + [pltpu.VMEM((H, S, W // NCH), bf)] * NCH,
        compiler_params=pltpu.CompilerParams(
            collective_id=0, has_side_effects=True, vmem_limit_bytes=60 * 1024 * 1024
        ),
        cost_estimate=pl.CostEstimate(
            flops=2 * 10**8, bytes_accessed=4 * 10**6, transcendentals=10**6
        ),
    )(
        thm, apr, ppr, cnt, hidden, base_q, live, base_k, base_v, a_in, b_out, cache,
        generated.reshape(N, W),
    )
    return pl.pallas_call(
        write_kernel,
        out_shape=[jax.ShapeDtypeStruct((A, W), bf)] * 3,
        in_specs=[vmem] * 3,
        out_specs=[hbm] * 3,
        scratch_shapes=[sem(3)],
        compiler_params=pltpu.CompilerParams(vmem_limit_bytes=2**20),
    )(*results)


def step(hidden, base_q, base_k, base_v, a_in, b_out, cache, generated, thm, live, apr, ppr, cnt):
    H = lax.axis_size("hosts")
    A, W = hidden.shape
    capacity = A // H
    fits = (
        capacity == 8
        and H <= 8
        and A <= 128
        and a_in.shape[0] == 1
        and A * cache.shape[0] == 128
        and cache.shape[0] == 4
        and cache.shape[2] == 128
        and H * A == 128
        and W == 8 * HEAD_SIZE
        and generated.shape[2] == 8
        and apr.shape[0] < 8
    )
    run = fused_body if fits else body
    return run(hidden, base_q, base_k, base_v, a_in, b_out, cache, generated, thm, live, apr, ppr, cnt)


def solution(mesh):
    placed = (
        P(("groups", "hosts"), "mp"),
        P(("groups", "hosts"), "mp"),
        P(("groups", "hosts"), "mp"),
        P(("groups", "hosts"), "mp"),
        P(("groups", "hosts"), "mp", None),
        P(("groups", "hosts"), None, None, "mp"),
        P(("groups", "hosts"), None, None, "mp"),
        P(("groups", "hosts"), None, None, "mp"),
        P(("groups", "hosts")),
        P(("groups", "hosts")),
        P("groups"),
        P("groups", None),
        P("groups"),
    )
    return jax.shard_map(
        step,
        mesh=mesh,
        in_specs=placed,
        out_specs=(
            P(("groups", "hosts"), "mp"),
            P(("groups", "hosts"), "mp"),
            P(("groups", "hosts"), "mp"),
        ),
        check_vma=False,
    )
```
